512 devices in a mesh: cube: 4 (over z_lo), facet: 32 (over y, z_hi, core), dp: 4 (over x).
Axes of the slice: x: 4, y: 8, z: 8 (z_hi: 2, z_lo: 4; z = z_hi * 4 + z_lo), core: 2. Of those that a mesh axis runs over, the one named last changes fastest.
Arguments:
- image: float32 [4, 1536, 2560], P('cube', 'facet'), may hold values from 0 to 2
- dual: bfloat16 [4, 4, 1536, 2560], P(None, 'cube', 'facet'), may hold values from -5 to 5
- payload: bfloat16 [4, 8192, 16, 128], P('cube', ('facet', 'dp')), may hold values from -6 to 6
- vis_weight: bfloat16 [4, 8192, 16], P('cube', ('facet', 'dp')), may hold values from 0.25 to 2
- freq_start: int32 [4, 8192], P('cube', ('facet', 'dp')), may hold values from 0 to 2559
- tile_slot: int32 [4, 8192], P('cube', ('facet', 'dp')), may hold values from 0 to 5, as said below
- live: int32 [4, 128], P('cube', ('facet', 'dp')), may hold values from 1 to 64, as said below
Outputs:
- image_next: float32 [4, 1536, 2560], P('cube', 'facet')
- dual_next: bfloat16 [4, 4, 1536, 2560], P(None, 'cube', 'facet')
The draws below stay inside these ranges and needn't reach their ends.
Inputs may be any that keep to these rules, and one draw needn't show every extreme that they name: `tile_slot`: A block's tile lies in its own facet or the one above; blocks of the first facet use their own facet only. The live blocks of a worker are its first slots; in every draw some worker of each channel has all 64 slots live.
All inputs are finite; a program needn't handle non-finite values.
Results may differ from the reference program's by a relative error of at most 0.011.
Values may be sent and summed in bfloat16 or wider, within the bound.
No kernel may reach another device: no remote copies, remote signals or barrier semaphores. Data moves between devices by JAX's collectives and lax.ppermute only.
A program may use at most 64 MiB of HBM per device.

```python
import math
import jax
import jax.numpy as jnp
from jax import lax

W = 2560
NF = 64
TILE = 16
GROUP = 8
FR = 48
BLK = 64
CHANNELS = 4
H = 1536
WORKERS = 128
NB = 8192
N_DP = 4


def draw_tile_slot(key, part):
    key = jax.random.fold_in(key, 11)
    per_facet = FR // TILE
    slots = jnp.arange(NB, dtype=jnp.int32)
    facet_of = slots // (BLK * N_DP)
    raw_slot = jax.random.randint(key, (CHANNELS, NB), 0, 2 * per_facet)
    lowest = jnp.where(facet_of == 0, per_facet, 0)
    chosen = lowest + raw_slot % (2 * per_facet - lowest)
    chosen = jnp.where(slots == NB - 1, 2 * per_facet - 1, chosen)
    chosen = jnp.where(slots == BLK * N_DP, 0, chosen)
    return chosen.astype(jnp.int32)


def draw_live(key, part):
    key = jax.random.fold_in(key, 23)
    first_key, second_key, third_key = jax.random.split(key, 3)
    first_draw = jax.random.randint(first_key, (CHANNELS, WORKERS), 0, BLK + 1)
    second_draw = jax.random.randint(second_key, (CHANNELS, WORKERS), 0, BLK + 1)
    counts = jnp.maximum(first_draw * second_draw // BLK, 1)
    picked = jax.random.randint(third_key, (CHANNELS,), 0, WORKERS)
    filled = jnp.arange(WORKERS, dtype=jnp.int32)[None, :] == picked[:, None]
    return jnp.where(filled, BLK, counts).astype(jnp.int32)


def touch_ends(result, rng, least, largest):
    longest = result.shape.index(max(result.shape))
    spots = []
    for shift in (0, 1):
        where = [jax.random.randint(jax.random.fold_in(rng, axis), (), 0, length) for axis, length in enumerate(result.shape)]
        where[longest] = (where[longest] + shift) % result.shape[longest]
        spots.append(tuple(where))
    return result.at[spots[0]].set(least).at[spots[1]].set(largest)


def steps_of(stream_key, extent, shards, least, largest):
    gain, own = 1.0, jax.random.fold_in(stream_key, 6)
    for position, shards_of in shards:
        heights = jnp.exp(jax.random.uniform(jax.random.fold_in(own, position), (shards_of,), jnp.float32, least / len(shards), largest / len(shards)))
        gain = gain * jnp.repeat(heights, extent[position] // shards_of).reshape([-1 if axis == position else 1 for axis in range(len(extent))])
    return gain


def noise(stream_key, shape, spread, most, cuts=(), kind=jnp.bfloat16):
    level = steps_of(stream_key, shape, cuts, -0.22, 0.18) if cuts else 1.0
    entries = jax.random.normal(stream_key, shape, jnp.float32) * spread * level
    return jnp.minimum(jnp.maximum(entries, -most), most).astype(kind)


def setup_inputs(seed: int = 0) -> dict:
    splits = jax.random.split(jax.random.key(seed), 8)
    image = jnp.clip(2.0 * jax.random.uniform(splits[0], (CHANNELS, H, W), jnp.float32) ** steps_of(splits[0], (CHANNELS, H, W), ((0, 4), (1, 32)), -0.2, 0.2), 0.0, 2.0)
    dual = noise(splits[1], (4, CHANNELS, H, W), 1.0, 5.0, ((1, 4), (2, 32)))
    payload = noise(splits[2], (CHANNELS, NB, TILE, 2 * NF), 1.0, 6.0, ((0, 4), (1, 128)))
    vis_weight = jnp.clip(jnp.exp(math.log(2.0) - 2.0794415 * jax.random.uniform(splits[3], (CHANNELS, NB, TILE), jnp.float32) ** steps_of(splits[3], (CHANNELS, NB, TILE), ((0, 4), (1, 128)), -0.2, 0.2)), 0.25, 2.0).astype(jnp.bfloat16)
    freq_start = touch_ends(jax.random.randint(splits[4], (CHANNELS, NB), 0, W), jax.random.fold_in(splits[4], 1), 0, W - 1).astype(jnp.int32)
    tile_slot = draw_tile_slot(jax.random.fold_in(splits[7], 71), 0)
    live = draw_live(jax.random.fold_in(splits[7], 71), 0)
    return {"image": image, "dual": dual, "payload": payload, "vis_weight": vis_weight, "freq_start": freq_start, "tile_slot": tile_slot, "live": live}


LOWPASS = (0.2303778133088964, 0.7148465705529155, 0.6308807679298587, -0.027983769416859854, -0.18703481171909309, 0.030841381835560764, 0.0328830116668852, -0.010597401785069032)
HIGHPASS = (-0.010597401785069032, -0.0328830116668852, 0.030841381835560764, 0.18703481171909309, -0.027983769416859854, -0.6308807679298587, 0.7148465705529155, -0.2303778133088964)
TAU_STEP = 0.5
SIGMA_STEP = 0.5
RADIUS = 3.0

def forward_axis(padded, filter_taps, along, length):
    summed = filter_taps[0] * lax.slice_in_dim(padded, 7, 7 + length, axis=along)
    for k in range(1, 8):
        summed = summed + filter_taps[k] * lax.slice_in_dim(padded, 7 - k, 7 - k + length, axis=along)
    return summed

def backward_axis(padded, filter_taps, along, length):
    summed = filter_taps[0] * lax.slice_in_dim(padded, 0, length, axis=along)
    for k in range(1, 8):
        summed = summed + filter_taps[k] * lax.slice_in_dim(padded, k, k + length, axis=along)
    return summed

def analyze(padded, height, breadth):
    subbands = []
    for row_taps in (LOWPASS, HIGHPASS):
        filtered = forward_axis(padded, row_taps, 0, height)
        for col_taps in (LOWPASS, HIGHPASS):
            subbands.append(forward_axis(filtered, col_taps, 1, breadth))
    return jnp.stack(subbands)

def synthesize(coefficients, leading, height):
    breadth = coefficients.shape[-1]
    summed = jnp.zeros((height, breadth), jnp.float32)
    for a, row_taps in enumerate((LOWPASS, HIGHPASS)):
        for b, col_taps in enumerate((LOWPASS, HIGHPASS)):
            subband = coefficients[2 * a + b]
            across = backward_axis(jnp.pad(subband, ((0, 0), (0, 7))), col_taps, 1, breadth)
            summed = summed + backward_axis(jnp.pad(across, ((leading, 7), (0, 0))), row_taps, 0, height)
    return summed

def freq_table(breadth, count):
    columns = jnp.arange(breadth, dtype=jnp.int32)
    freqs = jnp.arange(count, dtype=jnp.int32)
    angles = (columns[:, None] * freqs[None, :] % breadth).astype(jnp.float32) * (2.0 * math.pi / breadth)
    return jnp.concatenate([jnp.cos(angles), -jnp.sin(angles)], 1).astype(jnp.bfloat16)

def block_terms(tile_block, payload, weights, starts, live_mask, spectrum_table, breadth):
    columns = jnp.arange(breadth, dtype=jnp.int32)
    phases = (starts[:, None] * columns[None, :] % breadth).astype(jnp.float32) * (2.0 * math.pi / breadth)
    cosine = jnp.cos(phases)[:, None, :]
    minus_sine = -jnp.sin(phases)[:, None, :]
    pixels = tile_block.astype(jnp.float32)
    stacked = jnp.concatenate([pixels * cosine, pixels * minus_sine], 1).astype(jnp.bfloat16)
    table_wide = spectrum_table.astype(jnp.float32)
    spectra = jnp.einsum('gtw,wk->gtk', stacked.astype(jnp.float32), table_wide)
    height = tile_block.shape[1]
    half_width = spectrum_table.shape[1] // 2
    upper_half = spectra[:, :height]
    lower_half = spectra[:, height:]
    norm_scale = 1.0 / math.sqrt(breadth)
    model_vis = jnp.concatenate([upper_half[..., :half_width] - lower_half[..., half_width:], upper_half[..., half_width:] + lower_half[..., :half_width]], -1) * norm_scale
    factor = live_mask.astype(jnp.float32)[:, None, None] * weights.astype(jnp.float32)[:, :, None]
    misfit = factor * (model_vis - payload.astype(jnp.float32))
    paired = jnp.concatenate([misfit, jnp.concatenate([misfit[..., half_width:], -misfit[..., :half_width]], -1)], 1).astype(jnp.bfloat16)
    adjoint_rows = jnp.einsum('gtk,wk->gtw', paired.astype(jnp.float32), table_wide)
    return (cosine * adjoint_rows[:, :height] + minus_sine * adjoint_rows[:, height:]) * norm_scale

def reference(image, dual, payload, vis_weight, freq_start, tile_slot, live):
    spectrum_table = freq_table(W, NF)
    per_facet = FR // TILE
    slots = jnp.arange(NB, dtype=jnp.int32)
    worker = slots // BLK
    facet_of = worker // N_DP
    updated_list = []
    shifted_list = []
    for channel in range(CHANNELS):
        pixels = image[channel].astype(jnp.bfloat16)
        live_mask = (slots % BLK < live[channel][worker]).astype(jnp.int32)
        row_start = (((facet_of - 1) * per_facet + tile_slot[channel]) * TILE).astype(jnp.int32)
        groups = NB // GROUP
        items = (payload[channel].reshape(groups, GROUP, TILE, 2 * NF), vis_weight[channel].reshape(groups, GROUP, TILE), freq_start[channel].reshape(groups, GROUP), live_mask.reshape(groups, GROUP), row_start.reshape(groups, GROUP))

        def advance(gradient, item):
            offsets = item[4]
            tile_block = jnp.stack([lax.dynamic_slice_in_dim(pixels, offsets[i], TILE, 0) for i in range(GROUP)])
            term_rows = block_terms(tile_block, item[0], item[1], item[2], item[3], spectrum_table, W)
            for i in range(GROUP):
                current = lax.dynamic_slice_in_dim(gradient, offsets[i], TILE, 0)
                gradient = lax.dynamic_update_slice_in_dim(gradient, current + term_rows[i], offsets[i], 0)
            return (gradient, None)
        gradient = lax.scan(advance, jnp.zeros((H, W), jnp.float32), items)[0]
        synthesized = synthesize(dual[:, channel].astype(jnp.float32), 0, H)
        updated = jnp.maximum(image[channel] - TAU_STEP * (gradient + synthesized), 0.0)
        updated_list.append(updated)
        extrapolated = 2.0 * updated - image[channel]
        stretched = jnp.pad(extrapolated, ((7, 0), (7, 0)))
        shifted_list.append(dual[:, channel].astype(jnp.float32) + SIGMA_STEP * analyze(stretched, H, W))
    shifted = jnp.stack(shifted_list, 1)
    norms = jnp.sqrt(lax.optimization_barrier(jnp.sum(shifted * shifted, axis=1, keepdims=True)))
    dual_next = (shifted * (RADIUS / jnp.maximum(norms, RADIUS))).astype(jnp.bfloat16)
    return (jnp.stack(updated_list), dual_next)
```

```python
import functools
import math

import jax
import jax.numpy as jnp
import numpy as np
from jax import lax
from jax.experimental import pallas as pl
from jax.experimental.pallas import tpu as pltpu
from jax.sharding import PartitionSpec as P

LOWPASS = (
    0.2303778133088964,
    0.7148465705529155,
    0.6308807679298587,
    -0.027983769416859854,
    -0.18703481171909309,
    0.030841381835560764,
    0.0328830116668852,
    -0.010597401785069032,
)
HIGHPASS = (
    -0.010597401785069032,
    -0.0328830116668852,
    0.030841381835560764,
    0.18703481171909309,
    -0.027983769416859854,
    -0.6308807679298587,
    0.7148465705529155,
    -0.2303778133088964,
)
TAU_STEP = 0.5
SIGMA_STEP = 0.5
RADIUS = 3.0

W = 2560
TILE = 16
FR = 48
BLK = 64
PER = FR // TILE
Q = 20
R = 128
DP = 4
PART = W // DP
HALO = 128
SPAN = PART + HALO
CHUNKS = W // 64
UNROLL = 4
NORM = 1.0 / math.sqrt(W)
C1, C2 = math.cos(2 * math.pi / 5), math.cos(4 * math.pi / 5)
S1, S2 = math.sin(2 * math.pi / 5), math.sin(4 * math.pi / 5)


def tables():
    x = np.arange(W).reshape(R, Q).T
    angles = (x[:, :, None] * np.arange(R)[None, None, :] % W) * (2.0 * math.pi / W)
    table = np.concatenate([np.cos(angles), -np.sin(angles)], -1).astype(jnp.bfloat16)
    y = np.arange(PART)
    order = np.zeros((PART, PART), np.float32)
    order[y, (y % Q) * 32 + y // Q] = 1.0
    return table, order.astype(jnp.bfloat16)


def times_i(value, sign):
    re, im = value
    return (-im, re) if sign > 0 else (im, -re)


def plus(u, v):
    return (u[0] + v[0], u[1] + v[1])


def minus(u, v):
    return (u[0] - v[0], u[1] - v[1])


def dft4(x, sign):
    a, b = plus(x[0], x[2]), minus(x[0], x[2])
    c, d = plus(x[1], x[3]), times_i(minus(x[1], x[3]), sign)
    return [plus(a, c), plus(b, d), minus(a, c), minus(b, d)]


def dft5(x, sign):
    t1, t2 = plus(x[1], x[4]), plus(x[2], x[3])
    t3, t4 = minus(x[1], x[4]), minus(x[2], x[3])
    m1 = tuple(z + C1 * u + C2 * v for z, u, v in zip(x[0], t1, t2))
    m2 = tuple(z + C2 * u + C1 * v for z, u, v in zip(x[0], t1, t2))
    n1 = times_i(tuple(S1 * u + S2 * v for u, v in zip(t3, t4)), sign)
    n2 = times_i(tuple(S2 * u - S1 * v for u, v in zip(t3, t4)), sign)
    return [plus(x[0], plus(t1, t2)), plus(m1, n1), plus(m2, n2), minus(m2, n2), minus(m1, n1)]


def dft20(x, sign):
    columns = [dft4([x[(5 * a + 4 * b) % 20] for a in range(4)], sign) for b in range(5)]
    out = [None] * 20
    for c in range(4):
        line = dft5([columns[b][c] for b in range(5)], sign)
        for e in range(5):
            out[(5 * c + 16 * e) % 20] = line[e]
    return out


def facet_pass(
    base,
    starts_ref,
    slots_ref,
    live_ref,
    pixels_ref,
    payload_ref,
    weight_ref,
    table_ref,
    order_ref,
    out_ref,
    re_ref,
    im_ref,
    spec_ref,
    grad_ref,
    list_ref,
):
    lane = lax.broadcasted_iota(jnp.int32, (1, 128), 1)
    low = lane < 64
    half = lane % 64
    quarter = lane // 32

    def collect(b, count):
        slot = slots_ref[b] - base
        list_ref[count] = b
        return count + jnp.where((slot >= 0) & (slot < PER), 1, 0)

    count = lax.fori_loop(0, live_ref[0], collect, 0)
    for u in range(UNROLL):
        list_ref[count + u] = list_ref[0]

    stacked = jnp.concatenate(
        [pixels_ref[:, PART * g : PART * (g + 1)] for g in range(4)], 0
    )
    sorted_rows = jnp.dot(stacked, order_ref[...], preferred_element_type=jnp.float32)
    for j in range(5):
        tiles = [sorted_rows[FR * g : FR * (g + 1), 128 * j : 128 * (j + 1)] for g in range(4)]
        for p in range(4):
            turned = [
                tiles[g] if g == p else pltpu.roll(tiles[g], (32 * (g - p)) % 128, 1)
                for g in range(4)
            ]
            rows = turned[3]
            for g in range(3):
                rows = jnp.where(quarter == g, turned[g], rows)
            q = 4 * j + p
            partial = jnp.dot(
                rows.astype(jnp.bfloat16), table_ref[q], preferred_element_type=jnp.float32
            )
            re_ref[q] = partial[:, :R]
            im_ref[q] = partial[:, R:]

    def forward(i, carry):
        rows = pl.ds(pl.multiple_of(i * 8, 8), 8)
        spectrum = dft20([(re_ref[q, rows, :], im_ref[q, rows, :]) for q in range(Q)], -1)
        for k, (re, im) in enumerate(spectrum):
            re, im = re * NORM, im * NORM
            spec_ref[2 * k, rows, :] = jnp.where(low, re, pltpu.roll(im, 64, 1))
            spec_ref[2 * k + 1, rows, :] = jnp.where(low, pltpu.roll(re, 64, 1), im)
        return carry

    lax.fori_loop(0, FR // 8, forward, 0)
    spec_ref[CHUNKS] = spec_ref[0]
    grad_ref[...] = jnp.zeros_like(grad_ref)

    def blocks(step, carry):
        found = []
        for u in range(UNROLL):
            place = step * UNROLL + u
            b = list_ref[place]
            start = starts_ref[b]
            slot = jnp.clip(slots_ref[b] - base, 0, PER - 1)
            chunk = start // 64
            offset = start % 64
            rows = pl.ds(pl.multiple_of(slot * TILE, TILE), TILE)
            first = pltpu.roll(spec_ref[chunk, rows, :], (128 - offset) % 128, 1)
            second = pltpu.roll(spec_ref[chunk + 1, rows, :], 64 - offset, 1)
            model = jnp.where(half < 64 - offset, first, second)
            factor = weight_ref[b].astype(jnp.float32) * jnp.where(place < count, 1.0, 0.0)
            misfit = factor * (model - payload_ref[b].astype(jnp.float32))
            lower = jnp.where(half >= offset, pltpu.roll(misfit, offset, 1), 0.0)
            upper = jnp.where(half < offset, pltpu.roll(misfit, 64 + offset, 1), 0.0)
            found.append((chunk, rows, lower, upper))
        for chunk, rows, lower, upper in found:
            grad_ref[chunk, rows, :] += lower
            grad_ref[chunk + 1, rows, :] += upper
        return carry

    lax.fori_loop(0, (count + UNROLL - 1) // UNROLL, blocks, 0)
    grad_ref[0] += grad_ref[CHUNKS]

    def backward(i, carry):
        rows = pl.ds(pl.multiple_of(i * 8, 8), 8)
        spectrum = []
        for k in range(Q):
            even, odd = grad_ref[2 * k, rows, :], grad_ref[2 * k + 1, rows, :]
            spectrum.append(
                (
                    jnp.where(low, even, pltpu.roll(odd, 64, 1)),
                    jnp.where(low, pltpu.roll(even, 64, 1), odd),
                )
            )
        for q, (re, im) in enumerate(dft20(spectrum, 1)):
            re_ref[q, rows, :] = re * NORM
            im_ref[q, rows, :] = im * NORM
        return carry

    lax.fori_loop(0, FR // 8, backward, 0)
    for j in range(5):
        places = [[] for _ in range(4)]
        for p in range(4):
            q = 4 * j + p
            pair = jnp.concatenate([re_ref[q], im_ref[q]], 1).astype(jnp.bfloat16)
            rows = lax.dot_general(
                pair, table_ref[q], (((1,), (1,)), ((), ())), preferred_element_type=jnp.float32
            )
            for g in range(4):
                places[g].append(rows if g == p else pltpu.roll(rows, (32 * (p - g)) % 128, 1))
        for g in range(4):
            tile = places[g][3]
            for p in range(3):
                tile = jnp.where(quarter == p, places[g][p], tile)
            spec_ref[5 * g + j] = tile
    mixed = jnp.concatenate(
        [jnp.concatenate([spec_ref[5 * g + j] for j in range(5)], 1) for g in range(4)], 0
    ).astype(jnp.bfloat16)
    natural = lax.dot_general(
        mixed, order_ref[...], (((1,), (1,)), ((), ())), preferred_element_type=jnp.float32
    ).astype(jnp.bfloat16)
    out_ref[0, :, :HALO] = jnp.zeros((FR, HALO), jnp.bfloat16)
    for g in range(4):
        rows = natural[FR * g : FR * (g + 1)]
        out_ref[g, :, HALO:] = rows
        if g < 3:
            out_ref[g + 1, :, :HALO] = rows[:, PART - HALO :]


def facet_terms(base, pixels, payload, weights, starts, slots, live, table, order):
    smem = pl.BlockSpec(memory_space=pltpu.SMEM)
    vmem = pl.BlockSpec(memory_space=pltpu.VMEM)
    return pl.pallas_call(
        functools.partial(facet_pass, base),
        out_shape=jax.ShapeDtypeStruct((DP, FR, SPAN), jnp.bfloat16),
        in_specs=[smem] * 3 + [vmem] * 5,
        out_specs=vmem,
        scratch_shapes=[
            pltpu.VMEM((Q, FR, R), jnp.float32),
            pltpu.VMEM((Q, FR, R), jnp.float32),
            pltpu.VMEM((CHUNKS + 1, FR, 128), jnp.float32),
            pltpu.VMEM((CHUNKS + 1, FR, 128), jnp.float32),
            pltpu.SMEM((BLK + UNROLL,), jnp.int32),
        ],
        compiler_params=pltpu.CompilerParams(vmem_limit_bytes=32 * 1024 * 1024),
        cost_estimate=pl.CostEstimate(
            flops=2 * 10**9, bytes_accessed=4 * 10**6, transcendentals=0
        ),
        name=f"facet_terms_{base}",
    )(starts, slots, live, pixels, payload, weights, table, order)


def hop(block, distance):
    devices = range(lax.axis_size("facet"))
    route = [(i - distance, i) for i in devices if i - distance in devices]
    return lax.ppermute(block, "facet", route)


def gathered_sum(parts):
    mixed = lax.all_to_all(parts, "dp", 0, 0)
    return jnp.sum(mixed.astype(jnp.float32), 0)


def synthesize(dual):
    summed = jnp.zeros((FR + 8, SPAN), jnp.float32)
    for a, row_taps in enumerate((LOWPASS, HIGHPASS)):
        across = jnp.zeros((FR, SPAN), jnp.float32)
        for b, col_taps in enumerate((LOWPASS, HIGHPASS)):
            for k in range(8):
                across = across + col_taps[k] * dual[2 * a + b][:, k : k + SPAN]
        padded = jnp.pad(across, ((8, 7), (0, 0)))
        for k in range(8):
            summed = summed + row_taps[k] * padded[k : k + FR + 8]
    return summed


def analyze(extra):
    subbands = []
    for row_taps in (LOWPASS, HIGHPASS):
        filtered = sum(row_taps[k] * extra[8 - k : 8 - k + FR] for k in range(8))
        for col_taps in (LOWPASS, HIGHPASS):
            subbands.append(
                sum(col_taps[k] * filtered[:, HALO - k : HALO - k + PART] for k in range(8))
            )
    return jnp.stack(subbands)


def on_device(image, dual, payload, vis_weight, freq_start, tile_slot, live):
    table, order = tables()
    table, order = jnp.asarray(table), jnp.asarray(order)
    position = lax.axis_index("dp")
    facet = lax.axis_index("facet")
    own_rows = image[0]
    pixels = own_rows.astype(jnp.bfloat16)
    rows_above = hop(pixels, 1)
    weights = jnp.broadcast_to(vis_weight[0][:, :, None], payload.shape[1:])
    blocks = (payload[0], weights, freq_start[0], tile_slot[0], live[0], table, order)

    left = position * PART
    own_dual = lax.dynamic_slice_in_dim(
        jnp.pad(dual[:, 0], ((0, 0), (0, 0), (HALO, 128))), left, SPAN + 128, 2
    ).astype(jnp.float32)
    own_image = lax.dynamic_slice_in_dim(
        jnp.pad(own_rows, ((0, 0), (HALO, 0))), left, SPAN, 1
    )
    synth = synthesize(own_dual)

    own_terms = facet_terms(PER, pixels, *blocks)
    own_sum = gathered_sum(own_terms) + synth[8:]
    last_rows = hop(own_sum[FR - 8 :].astype(jnp.bfloat16), 1)
    upper_terms = facet_terms(0, rows_above, *blocks)
    upper_sum = gathered_sum(upper_terms) + jnp.pad(synth[:8], ((FR - 8, 0), (0, 0)))
    from_below = hop(upper_sum.astype(jnp.bfloat16), -1)

    total = own_sum + from_below.astype(jnp.float32)
    above = last_rows.astype(jnp.float32) + upper_sum[FR - 8 :]
    image_above = lax.dynamic_slice_in_dim(
        jnp.pad(rows_above[FR - 8 :], ((0, 0), (HALO, 0))), left, SPAN, 1
    ).astype(jnp.float32)
    old = jnp.concatenate([image_above, own_image], 0)
    new = jnp.maximum(old - TAU_STEP * jnp.concatenate([above, total], 0), 0.0)
    column = lax.broadcasted_iota(jnp.int32, old.shape, 1) + left
    row = lax.broadcasted_iota(jnp.int32, old.shape, 0)
    inside = (column >= HALO) & ((row >= 8) | (facet > 0))
    extra = jnp.where(inside, 2.0 * new - old, 0.0)

    shifted = own_dual[:, :, HALO : HALO + PART] + SIGMA_STEP * analyze(extra)
    squares = lax.all_gather((shifted * shifted).astype(jnp.bfloat16), "cube")
    norms = jnp.sqrt(jnp.sum(squares.astype(jnp.float32), 0))
    dual_part = (shifted * (RADIUS / jnp.maximum(norms, RADIUS))).astype(jnp.bfloat16)
    dual_next = lax.all_gather(dual_part, "dp", axis=2, tiled=True)
    descent = lax.all_gather(total[:, HALO:].astype(jnp.bfloat16), "dp", axis=1, tiled=True)
    updated = jnp.maximum(own_rows - TAU_STEP * descent.astype(jnp.float32), 0.0)
    return (updated[None], dual_next[:, None])


def solution(mesh):
    return jax.shard_map(
        on_device,
        mesh=mesh,
        in_specs=(
            P("cube", "facet", None),
            P(None, "cube", "facet", None),
            P("cube", ("facet", "dp"), None, None),
            P("cube", ("facet", "dp"), None),
            P("cube", ("facet", "dp")),
            P("cube", ("facet", "dp")),
            P("cube", ("facet", "dp")),
        ),
        out_specs=(P("cube", "facet", None), P(None, "cube", "facet", None)),
        check_vma=False,
    )
```

```python
import functools
import math

import jax
import jax.numpy as jnp
import numpy as np
from jax import lax
from jax.experimental import pallas as pl
from jax.experimental.pallas import tpu as pltpu
from jax.sharding import PartitionSpec as P

LOWPASS = (
    0.2303778133088964,
    0.7148465705529155,
    0.6308807679298587,
    -0.027983769416859854,
    -0.18703481171909309,
    0.030841381835560764,
    0.0328830116668852,
    -0.010597401785069032,
)
HIGHPASS = (
    -0.010597401785069032,
    -0.0328830116668852,
    0.030841381835560764,
    0.18703481171909309,
    -0.027983769416859854,
    -0.6308807679298587,
    0.7148465705529155,
    -0.2303778133088964,
)
TAU_STEP = 0.5
SIGMA_STEP = 0.5
RADIUS = 3.0

W = 2560
TILE = 16
FR = 48
BLK = 64
PER = FR // TILE
Q = 20
R = 128
DP = 4
PART = W // DP
HALO = 128
SPAN = PART + HALO
CHUNKS = W // 64
UNROLL = 4
NORM = 1.0 / math.sqrt(W)
C1, C2 = math.cos(2 * math.pi / 5), math.cos(4 * math.pi / 5)
S1, S2 = math.sin(2 * math.pi / 5), math.sin(4 * math.pi / 5)


def tables():
    x = np.arange(W).reshape(R, Q).T
    angles = (x[:, :, None] * np.arange(R)[None, None, :] % W) * (2.0 * math.pi / W)
    table = np.concatenate([np.cos(angles), -np.sin(angles)], -1).astype(jnp.bfloat16)
    return table


def times_i(value, sign):
    re, im = value
    return (-im, re) if sign > 0 else (im, -re)


def plus(u, v):
    return (u[0] + v[0], u[1] + v[1])


def minus(u, v):
    return (u[0] - v[0], u[1] - v[1])


def dft4(x, sign):
    a, b = plus(x[0], x[2]), minus(x[0], x[2])
    c, d = plus(x[1], x[3]), times_i(minus(x[1], x[3]), sign)
    return [plus(a, c), plus(b, d), minus(a, c), minus(b, d)]


def dft5(x, sign):
    t1, t2 = plus(x[1], x[4]), plus(x[2], x[3])
    t3, t4 = minus(x[1], x[4]), minus(x[2], x[3])
    m1 = tuple(z + C1 * u + C2 * v for z, u, v in zip(x[0], t1, t2))
    m2 = tuple(z + C2 * u + C1 * v for z, u, v in zip(x[0], t1, t2))
    n1 = times_i(tuple(S1 * u + S2 * v for u, v in zip(t3, t4)), sign)
    n2 = times_i(tuple(S2 * u - S1 * v for u, v in zip(t3, t4)), sign)
    return [plus(x[0], plus(t1, t2)), plus(m1, n1), plus(m2, n2), minus(m2, n2), minus(m1, n1)]


def dft20(x, sign):
    columns = [dft4([x[(5 * a + 4 * b) % 20] for a in range(4)], sign) for b in range(5)]
    out = [None] * 20
    for c in range(4):
        line = dft5([columns[b][c] for b in range(5)], sign)
        for e in range(5):
            out[(5 * c + 16 * e) % 20] = line[e]
    return out


def residue_order():
    y = lax.broadcasted_iota(jnp.int32, (PART, 128), 0)
    group = ((y.astype(jnp.float32) + 0.5) * (1.0 / Q)).astype(jnp.int32)
    target = (y - Q * group) * 32 + group
    lane = lax.broadcasted_iota(jnp.int32, (PART, 128), 1)
    tiles = [jnp.where(target == lane + 128 * j, 1.0, 0.0) for j in range(PART // 128)]
    return jnp.concatenate(tiles, 1).astype(jnp.bfloat16)


def facet_pass(
    base,
    starts_hbm,
    slots_hbm,
    live_hbm,
    weight_hbm,
    payload_hbm,
    table_hbm,
    pixels_ref,
    out_ref,
    starts_ref,
    slots_ref,
    live_ref,
    list_ref,
    weight_ref,
    payload_ref,
    table_ref,
    order_ref,
    re_ref,
    im_ref,
    spec_ref,
    grad_ref,
    sems,
):
    pairs = [
        (table_hbm, table_ref),
        (starts_hbm, starts_ref),
        (slots_hbm, slots_ref),
        (live_hbm, live_ref),
        (weight_hbm, weight_ref),
        (payload_hbm, payload_ref),
    ]
    copies = [pltpu.make_async_copy(s, d, sems.at[i]) for i, (s, d) in enumerate(pairs)]
    for copy in copies:
        copy.start()

    lane = lax.broadcasted_iota(jnp.int32, (1, 128), 1)
    low = lane < 64
    half = lane & 63
    quarter = lane >> 5

    order_ref[...] = residue_order()
    stacked = jnp.concatenate(
        [pixels_ref[:, PART * g : PART * (g + 1)] for g in range(4)], 0
    )
    sorted_rows = jnp.dot(stacked, order_ref[...], preferred_element_type=jnp.float32)
    copies[0].wait()
    for j in range(5):
        tiles = [sorted_rows[FR * g : FR * (g + 1), 128 * j : 128 * (j + 1)] for g in range(4)]
        for p in range(4):
            turned = [
                tiles[g] if g == p else pltpu.roll(tiles[g], (32 * (g - p)) % 128, 1)
                for g in range(4)
            ]
            rows = turned[3]
            for g in range(3):
                rows = jnp.where(quarter == g, turned[g], rows)
            q = 4 * j + p
            partial = jnp.dot(
                rows.astype(jnp.bfloat16), table_ref[q], preferred_element_type=jnp.float32
            )
            re_ref[q] = partial[:, :R]
            im_ref[q] = partial[:, R:]

    def forward(i, carry):
        rows = pl.ds(pl.multiple_of(i * 8, 8), 8)
        spectrum = dft20([(re_ref[q, rows, :], im_ref[q, rows, :]) for q in range(Q)], -1)
        for k, (re, im) in enumerate(spectrum):
            re, im = re * NORM, im * NORM
            spec_ref[2 * k, rows, :] = jnp.where(low, re, pltpu.roll(im, 64, 1))
            spec_ref[2 * k + 1, rows, :] = jnp.where(low, pltpu.roll(re, 64, 1), im)
        return carry

    lax.fori_loop(0, FR // 8, forward, 0)
    spec_ref[CHUNKS] = spec_ref[0]
    grad_ref[...] = jnp.zeros_like(grad_ref)
    for copy in copies[1:]:
        copy.wait()

    def collect(b, count):
        slot = slots_ref[0, b] - base
        list_ref[count] = b
        return count + jnp.where((slot >= 0) & (slot < PER), 1, 0)

    count = lax.fori_loop(0, live_ref[0, 0], collect, 0)
    for u in range(UNROLL):
        list_ref[count + u] = list_ref[0]
    weights = weight_ref[...].astype(jnp.float32)
    slot_lane = lax.broadcasted_iota(jnp.int32, (1, BLK), 1)
    ones = jnp.ones((BLK, 128), jnp.bfloat16)

    def blocks(step, carry):
        places = [step * UNROLL + u for u in range(UNROLL)]
        numbers = [list_ref[place] for place in places]
        picked = [
            jnp.where(slot_lane == jnp.where(place < count, b, -1), weights, 0.0)
            for place, b in zip(places, numbers)
        ]
        factors = jnp.dot(
            jnp.concatenate(picked, 0).astype(jnp.bfloat16), ones, preferred_element_type=jnp.float32
        )
        found = []
        for u, b in enumerate(numbers):
            start = starts_ref[0, b]
            slot = jnp.clip(slots_ref[0, b] - base, 0, PER - 1)
            chunk = start >> 6
            offset = start & 63
            rows = pl.ds(pl.multiple_of(slot * TILE, TILE), TILE)
            first = pltpu.roll(spec_ref[chunk, rows, :], (128 - offset) & 127, 1)
            second = pltpu.roll(spec_ref[chunk + 1, rows, :], 64 - offset, 1)
            model = jnp.where(half < 64 - offset, first, second)
            misfit = factors[TILE * u : TILE * (u + 1)] * (
                model - payload_ref[b].astype(jnp.float32)
            )
            lower = jnp.where(half >= offset, pltpu.roll(misfit, offset, 1), 0.0)
            upper = jnp.where(half < offset, pltpu.roll(misfit, 64 + offset, 1), 0.0)
            found.append((chunk, rows, lower, upper))
        for chunk, rows, lower, upper in found:
            grad_ref[chunk, rows, :] += lower
            grad_ref[chunk + 1, rows, :] += upper
        return carry

    lax.fori_loop(0, (count + UNROLL - 1) // UNROLL, blocks, 0)
    grad_ref[0] += grad_ref[CHUNKS]

    def backward(i, carry):
        rows = pl.ds(pl.multiple_of(i * 8, 8), 8)
        spectrum = []
        for k in range(Q):
            even, odd = grad_ref[2 * k, rows, :], grad_ref[2 * k + 1, rows, :]
            spectrum.append(
                (
                    jnp.where(low, even, pltpu.roll(odd, 64, 1)),
                    jnp.where(low, pltpu.roll(even, 64, 1), odd),
                )
            )
        for q, (re, im) in enumerate(dft20(spectrum, 1)):
            re_ref[q, rows, :] = re * NORM
            im_ref[q, rows, :] = im * NORM
        return carry

    lax.fori_loop(0, FR // 8, backward, 0)
    for j in range(5):
        places = [[] for _ in range(4)]
        for p in range(4):
            q = 4 * j + p
            pair = jnp.concatenate([re_ref[q], im_ref[q]], 1).astype(jnp.bfloat16)
            rows = lax.dot_general(
                pair, table_ref[q], (((1,), (1,)), ((), ())), preferred_element_type=jnp.float32
            )
            for g in range(4):
                places[g].append(rows if g == p else pltpu.roll(rows, (32 * (p - g)) % 128, 1))
        for g in range(4):
            tile = places[g][3]
            for p in range(3):
                tile = jnp.where(quarter == p, places[g][p], tile)
            spec_ref[5 * g + j] = tile
    mixed = jnp.concatenate(
        [jnp.concatenate([spec_ref[5 * g + j] for j in range(5)], 1) for g in range(4)], 0
    ).astype(jnp.bfloat16)
    natural = lax.dot_general(
        mixed, order_ref[...], (((1,), (1,)), ((), ())), preferred_element_type=jnp.float32
    ).astype(jnp.bfloat16)
    out_ref[0, :, :HALO] = jnp.zeros((FR, HALO), jnp.bfloat16)
    for g in range(4):
        rows = natural[FR * g : FR * (g + 1)]
        out_ref[g, :, HALO:] = rows
        if g < 3:
            out_ref[g + 1, :, :HALO] = rows[:, PART - HALO :]


def facet_terms(base, pixels, starts, slots, live, weights, payload, table):
    hbm = pl.BlockSpec(memory_space=pltpu.HBM)
    vmem = pl.BlockSpec(memory_space=pltpu.VMEM)
    return pl.pallas_call(
        functools.partial(facet_pass, base),
        out_shape=jax.ShapeDtypeStruct((DP, FR, SPAN), jnp.bfloat16),
        in_specs=[hbm] * 6 + [vmem],
        out_specs=vmem,
        scratch_shapes=[
            pltpu.SMEM((1, BLK), jnp.int32),
            pltpu.SMEM((1, BLK), jnp.int32),
            pltpu.SMEM((1, 1), jnp.int32),
            pltpu.SMEM((BLK + UNROLL,), jnp.int32),
            pltpu.VMEM((TILE, BLK), jnp.bfloat16),
            pltpu.VMEM((BLK, TILE, 128), jnp.bfloat16),
            pltpu.VMEM((Q, R, 2 * R), jnp.bfloat16),
            pltpu.VMEM((PART, PART), jnp.bfloat16),
            pltpu.VMEM((Q, FR, R), jnp.float32),
            pltpu.VMEM((Q, FR, R), jnp.float32),
            pltpu.VMEM((CHUNKS + 1, FR, 128), jnp.float32),
            pltpu.VMEM((CHUNKS + 1, FR, 128), jnp.float32),
            pltpu.SemaphoreType.DMA((6,)),
        ],
        compiler_params=pltpu.CompilerParams(vmem_limit_bytes=32 * 1024 * 1024),
        cost_estimate=pl.CostEstimate(
            flops=2 * 10**9, bytes_accessed=4 * 10**6, transcendentals=0
        ),
        name=f"facet_terms_{base}",
    )(starts, slots, live, weights, payload, table, pixels)


def hop(block, distance):
    devices = range(lax.axis_size("facet"))
    route = [(i - distance, i) for i in devices if i - distance in devices]
    return lax.ppermute(block, "facet", route)


def gathered_sum(parts):
    mixed = lax.all_to_all(parts, "dp", 0, 0)
    return jnp.sum(mixed.astype(jnp.float32), 0)


def synthesize(dual):
    summed = jnp.zeros((FR + 8, SPAN), jnp.float32)
    for a, row_taps in enumerate((LOWPASS, HIGHPASS)):
        across = jnp.zeros((FR, SPAN), jnp.float32)
        for b, col_taps in enumerate((LOWPASS, HIGHPASS)):
            for k in range(8):
                across = across + col_taps[k] * dual[2 * a + b][:, k : k + SPAN]
        padded = jnp.pad(across, ((8, 7), (0, 0)))
        for k in range(8):
            summed = summed + row_taps[k] * padded[k : k + FR + 8]
    return summed


def analyze(extra):
    subbands = []
    for row_taps in (LOWPASS, HIGHPASS):
        filtered = sum(row_taps[k] * extra[8 - k : 8 - k + FR] for k in range(8))
        for col_taps in (LOWPASS, HIGHPASS):
            subbands.append(
                sum(col_taps[k] * filtered[:, HALO - k : HALO - k + PART] for k in range(8))
            )
    return jnp.stack(subbands)


def on_device(image, dual, payload, vis_weight, freq_start, tile_slot, live):
    table = jnp.asarray(tables())
    position = lax.axis_index("dp")
    facet = lax.axis_index("facet")
    own_rows = image[0]
    pixels = own_rows.astype(jnp.bfloat16)
    rows_above = hop(pixels, 1)
    blocks = (freq_start, tile_slot, live, vis_weight[0].T, payload[0], table)

    left = position * PART
    own_dual = lax.dynamic_slice_in_dim(
        jnp.pad(dual[:, 0], ((0, 0), (0, 0), (HALO, 128))), left, SPAN + 128, 2
    ).astype(jnp.float32)
    own_image = lax.dynamic_slice_in_dim(
        jnp.pad(own_rows, ((0, 0), (HALO, 0))), left, SPAN, 1
    )
    synth = synthesize(own_dual)

    own_terms = facet_terms(PER, pixels, *blocks)
    own_sum = gathered_sum(own_terms) + synth[8:]
    upper_terms = facet_terms(0, rows_above, *blocks)
    upper_sum = gathered_sum(upper_terms) + jnp.pad(synth[:8], ((FR - 8, 0), (0, 0)))
    sent_up, sent_down = lax.optimization_barrier(
        (upper_sum.astype(jnp.bfloat16), own_sum[FR - 8 :].astype(jnp.bfloat16))
    )
    from_below = hop(sent_up, -1)
    last_rows = hop(sent_down, 1)

    total = own_sum + from_below.astype(jnp.float32)
    above = last_rows.astype(jnp.float32) + upper_sum[FR - 8 :]
    image_above = lax.dynamic_slice_in_dim(
        jnp.pad(rows_above[FR - 8 :], ((0, 0), (HALO, 0))), left, SPAN, 1
    ).astype(jnp.float32)
    old = jnp.concatenate([image_above, own_image], 0)
    new = jnp.maximum(old - TAU_STEP * jnp.concatenate([above, total], 0), 0.0)
    column = lax.broadcasted_iota(jnp.int32, old.shape, 1) + left
    row = lax.broadcasted_iota(jnp.int32, old.shape, 0)
    inside = (column >= HALO) & ((row >= 8) | (facet > 0))
    extra = jnp.where(inside, 2.0 * new - old, 0.0)

    shifted = own_dual[:, :, HALO : HALO + PART] + SIGMA_STEP * analyze(extra)
    squares = lax.all_gather((shifted * shifted).astype(jnp.bfloat16), "cube")
    norms = jnp.sqrt(jnp.sum(squares.astype(jnp.float32), 0))
    dual_part = (shifted * (RADIUS / jnp.maximum(norms, RADIUS))).astype(jnp.bfloat16)
    own_part = jnp.concatenate([dual_part, total[None, :, HALO:].astype(jnp.bfloat16)], 0)
    parts = lax.all_to_all(jnp.broadcast_to(own_part, (DP,) + own_part.shape), "dp", 0, 0)
    whole = jnp.concatenate([parts[d] for d in range(DP)], -1)
    dual_next = whole[:4]
    updated = jnp.maximum(own_rows - TAU_STEP * whole[4].astype(jnp.float32), 0.0)
    return (updated[None], dual_next[:, None])


def solution(mesh):
    return jax.shard_map(
        on_device,
        mesh=mesh,
        in_specs=(
            P("cube", "facet", None),
            P(None, "cube", "facet", None),
            P("cube", ("facet", "dp"), None, None),
            P("cube", ("facet", "dp"), None),
            P("cube", ("facet", "dp")),
            P("cube", ("facet", "dp")),
            P("cube", ("facet", "dp")),
        ),
        out_specs=(P("cube", "facet", None), P(None, "cube", "facet", None)),
        check_vma=False,
    )
```

```python
import functools
import math

import jax
import jax.numpy as jnp
import numpy as np
from jax import lax
from jax.experimental import pallas as pl
from jax.experimental.pallas import tpu as pltpu
from jax.sharding import PartitionSpec as P

LOWPASS = (
    0.2303778133088964,
    0.7148465705529155,
    0.6308807679298587,
    -0.027983769416859854,
    -0.18703481171909309,
    0.030841381835560764,
    0.0328830116668852,
    -0.010597401785069032,
)
HIGHPASS = (
    -0.010597401785069032,
    -0.0328830116668852,
    0.030841381835560764,
    0.18703481171909309,
    -0.027983769416859854,
    -0.6308807679298587,
    0.7148465705529155,
    -0.2303778133088964,
)
TAU_STEP = 0.5
SIGMA_STEP = 0.5
RADIUS = 3.0

W = 2560
TILE = 16
FR = 48
BLK = 64
PER = FR // TILE
Q = 20
R = 128
DP = 4
PART = W // DP
HALO = 128
SPAN = PART + HALO
CHUNKS = W // 64
UNROLL = 4
VMEM_LIMIT = 62 * 1024 * 1024
NORM = 1.0 / math.sqrt(W)
C1, C2 = math.cos(2 * math.pi / 5), math.cos(4 * math.pi / 5)
S1, S2 = math.sin(2 * math.pi / 5), math.sin(4 * math.pi / 5)


def tables():
    x = np.arange(W).reshape(R, Q).T
    angles = (x[:, :, None] * np.arange(R)[None, None, :] % W) * (2.0 * math.pi / W)
    table = np.concatenate([np.cos(angles), -np.sin(angles)], -1).astype(jnp.bfloat16)
    return table


def times_i(value, sign):
    re, im = value
    return (-im, re) if sign > 0 else (im, -re)


def plus(u, v):
    return (u[0] + v[0], u[1] + v[1])


def minus(u, v):
    return (u[0] - v[0], u[1] - v[1])


def dft4(x, sign):
    a, b = plus(x[0], x[2]), minus(x[0], x[2])
    c, d = plus(x[1], x[3]), times_i(minus(x[1], x[3]), sign)
    return [plus(a, c), plus(b, d), minus(a, c), minus(b, d)]


def dft5(x, sign):
    t1, t2 = plus(x[1], x[4]), plus(x[2], x[3])
    t3, t4 = minus(x[1], x[4]), minus(x[2], x[3])
    m1 = tuple(z + C1 * u + C2 * v for z, u, v in zip(x[0], t1, t2))
    m2 = tuple(z + C2 * u + C1 * v for z, u, v in zip(x[0], t1, t2))
    n1 = times_i(tuple(S1 * u + S2 * v for u, v in zip(t3, t4)), sign)
    n2 = times_i(tuple(S2 * u - S1 * v for u, v in zip(t3, t4)), sign)
    return [plus(x[0], plus(t1, t2)), plus(m1, n1), plus(m2, n2), minus(m2, n2), minus(m1, n1)]


def dft20(x, sign):
    columns = [dft4([x[(5 * a + 4 * b) % 20] for a in range(4)], sign) for b in range(5)]
    out = [None] * 20
    for c in range(4):
        line = dft5([columns[b][c] for b in range(5)], sign)
        for e in range(5):
            out[(5 * c + 16 * e) % 20] = line[e]
    return out


def residue_order():
    y = lax.broadcasted_iota(jnp.int32, (PART, 128), 0)
    group = ((y.astype(jnp.float32) + 0.5) * (1.0 / Q)).astype(jnp.int32)
    target = (y - Q * group) * 32 + group
    lane = lax.broadcasted_iota(jnp.int32, (PART, 128), 1)
    tiles = [jnp.where(target == lane + 128 * j, 1.0, 0.0) for j in range(PART // 128)]
    return jnp.concatenate(tiles, 1).astype(jnp.bfloat16)


def facet_pass(
    base,
    starts_hbm,
    slots_hbm,
    live_hbm,
    weight_hbm,
    payload_hbm,
    table_hbm,
    pixels_ref,
    *refs,
):
    if base == 0:
        below_ref, refs = refs[0], refs[1:]
    (
        out_ref,
        starts_ref,
        slots_ref,
        live_ref,
        list_ref,
        weight_ref,
        payload_ref,
        table_ref,
        order_ref,
        re_ref,
        im_ref,
        spec_ref,
        grad_ref,
        sems,
    ) = refs
    pairs = [
        (table_hbm, table_ref),
        (starts_hbm, starts_ref),
        (slots_hbm, slots_ref),
        (live_hbm, live_ref),
        (weight_hbm, weight_ref),
        (payload_hbm, payload_ref),
    ]
    copies = [pltpu.make_async_copy(s, d, sems.at[i]) for i, (s, d) in enumerate(pairs)]
    for copy in copies:
        copy.start()

    lane = lax.broadcasted_iota(jnp.int32, (1, 128), 1)
    low = lane < 64
    half = lane & 63
    quarter = lane >> 5

    order_ref[...] = residue_order()
    stacked = jnp.concatenate(
        [pixels_ref[:, PART * g : PART * (g + 1)] for g in range(4)], 0
    )
    sorted_rows = jnp.dot(stacked, order_ref[...], preferred_element_type=jnp.float32)
    copies[0].wait()
    for j in range(5):
        tiles = [sorted_rows[FR * g : FR * (g + 1), 128 * j : 128 * (j + 1)] for g in range(4)]
        for p in range(4):
            turned = [
                tiles[g] if g == p else pltpu.roll(tiles[g], (32 * (g - p)) % 128, 1)
                for g in range(4)
            ]
            rows = turned[3]
            for g in range(3):
                rows = jnp.where(quarter == g, turned[g], rows)
            q = 4 * j + p
            partial = jnp.dot(
                rows.astype(jnp.bfloat16), table_ref[q], preferred_element_type=jnp.float32
            )
            re_ref[q] = partial[:, :R]
            im_ref[q] = partial[:, R:]

    def forward(i, carry):
        rows = pl.ds(pl.multiple_of(i * 8, 8), 8)
        spectrum = dft20([(re_ref[q, rows, :], im_ref[q, rows, :]) for q in range(Q)], -1)
        for k, (re, im) in enumerate(spectrum):
            re, im = re * NORM, im * NORM
            spec_ref[2 * k, rows, :] = jnp.where(low, re, pltpu.roll(im, 64, 1))
            spec_ref[2 * k + 1, rows, :] = jnp.where(low, pltpu.roll(re, 64, 1), im)
        return carry

    lax.fori_loop(0, FR // 8, forward, 0)
    spec_ref[CHUNKS] = spec_ref[0]
    grad_ref[...] = jnp.zeros_like(grad_ref)
    for copy in copies[1:]:
        copy.wait()

    def collect(b, count):
        slot = slots_ref[0, b] - base
        list_ref[count] = b
        return count + jnp.where((slot >= 0) & (slot < PER), 1, 0)

    count = lax.fori_loop(0, live_ref[0, 0], collect, 0)
    for u in range(UNROLL):
        list_ref[count + u] = list_ref[0]
    weights = weight_ref[...].astype(jnp.float32)
    slot_lane = lax.broadcasted_iota(jnp.int32, (1, BLK), 1)
    ones = jnp.ones((BLK, 128), jnp.bfloat16)

    def blocks(step, carry):
        places = [step * UNROLL + u for u in range(UNROLL)]
        numbers = [list_ref[place] for place in places]
        picked = [
            jnp.where(slot_lane == jnp.where(place < count, b, -1), weights, 0.0)
            for place, b in zip(places, numbers)
        ]
        factors = jnp.dot(
            jnp.concatenate(picked, 0).astype(jnp.bfloat16), ones, preferred_element_type=jnp.float32
        )
        found = []
        for u, b in enumerate(numbers):
            start = starts_ref[0, b]
            slot = jnp.clip(slots_ref[0, b] - base, 0, PER - 1)
            chunk = start >> 6
            offset = start & 63
            rows = pl.ds(pl.multiple_of(slot * TILE, TILE), TILE)
            first = pltpu.roll(spec_ref[chunk, rows, :], (128 - offset) & 127, 1)
            second = pltpu.roll(spec_ref[chunk + 1, rows, :], 64 - offset, 1)
            model = jnp.where(half < 64 - offset, first, second)
            misfit = factors[TILE * u : TILE * (u + 1)] * (
                model - payload_ref[b].astype(jnp.float32)
            )
            lower = jnp.where(half >= offset, pltpu.roll(misfit, offset, 1), 0.0)
            upper = jnp.where(half < offset, pltpu.roll(misfit, 64 + offset, 1), 0.0)
            found.append((chunk, rows, lower, upper))
        for chunk, rows, lower, upper in found:
            grad_ref[chunk, rows, :] += lower
            grad_ref[chunk + 1, rows, :] += upper
        return carry

    lax.fori_loop(0, (count + UNROLL - 1) // UNROLL, blocks, 0)
    grad_ref[0] += grad_ref[CHUNKS]

    def backward(i, carry):
        rows = pl.ds(pl.multiple_of(i * 8, 8), 8)
        spectrum = []
        for k in range(Q):
            even, odd = grad_ref[2 * k, rows, :], grad_ref[2 * k + 1, rows, :]
            spectrum.append(
                (
                    jnp.where(low, even, pltpu.roll(odd, 64, 1)),
                    jnp.where(low, pltpu.roll(even, 64, 1), odd),
                )
            )
        for q, (re, im) in enumerate(dft20(spectrum, 1)):
            re_ref[q, rows, :] = re * NORM
            im_ref[q, rows, :] = im * NORM
        return carry

    lax.fori_loop(0, FR // 8, backward, 0)
    for j in range(5):
        places = [[] for _ in range(4)]
        for p in range(4):
            q = 4 * j + p
            pair = jnp.concatenate([re_ref[q], im_ref[q]], 1).astype(jnp.bfloat16)
            rows = lax.dot_general(
                pair, table_ref[q], (((1,), (1,)), ((), ())), preferred_element_type=jnp.float32
            )
            for g in range(4):
                places[g].append(rows if g == p else pltpu.roll(rows, (32 * (p - g)) % 128, 1))
        for g in range(4):
            tile = places[g][3]
            for p in range(3):
                tile = jnp.where(quarter == p, places[g][p], tile)
            spec_ref[5 * g + j] = tile
    mixed = jnp.concatenate(
        [jnp.concatenate([spec_ref[5 * g + j] for j in range(5)], 1) for g in range(4)], 0
    ).astype(jnp.bfloat16)
    natural = lax.dot_general(
        mixed, order_ref[...], (((1,), (1,)), ((), ())), preferred_element_type=jnp.float32
    ).astype(jnp.bfloat16)
    out_ref[0, :FR, :HALO] = jnp.zeros((FR, HALO), jnp.bfloat16)
    for g in range(4):
        rows = natural[FR * g : FR * (g + 1)]
        out_ref[g, :FR, HALO:] = rows
        if g < 3:
            out_ref[g + 1, :FR, :HALO] = rows[:, PART - HALO :]
        if base == 0:
            out_ref[g, FR:, :] = below_ref[g]


def facet_terms(base, pixels, starts, slots, live, weights, payload, table, *below):
    hbm = pl.BlockSpec(memory_space=pltpu.HBM)
    vmem = pl.BlockSpec(memory_space=pltpu.VMEM)
    return pl.pallas_call(
        functools.partial(facet_pass, base),
        out_shape=jax.ShapeDtypeStruct((DP, FR * (1 + len(below)), SPAN), jnp.bfloat16),
        in_specs=[hbm] * 6 + [vmem] * (1 + len(below)),
        out_specs=vmem,
        scratch_shapes=[
            pltpu.SMEM((1, BLK), jnp.int32),
            pltpu.SMEM((1, BLK), jnp.int32),
            pltpu.SMEM((1, 1), jnp.int32),
            pltpu.SMEM((BLK + UNROLL,), jnp.int32),
            pltpu.VMEM((TILE, BLK), jnp.bfloat16),
            pltpu.VMEM((BLK, TILE, 128), jnp.bfloat16),
            pltpu.VMEM((Q, R, 2 * R), jnp.bfloat16),
            pltpu.VMEM((PART, PART), jnp.bfloat16),
            pltpu.VMEM((Q, FR, R), jnp.float32),
            pltpu.VMEM((Q, FR, R), jnp.float32),
            pltpu.VMEM((CHUNKS + 1, FR, 128), jnp.float32),
            pltpu.VMEM((CHUNKS + 1, FR, 128), jnp.float32),
            pltpu.SemaphoreType.DMA((6,)),
        ],
        compiler_params=pltpu.CompilerParams(vmem_limit_bytes=VMEM_LIMIT),
        cost_estimate=pl.CostEstimate(
            flops=2 * 10**9, bytes_accessed=4 * 10**6, transcendentals=0
        ),
        name=f"facet_terms_{base}",
    )(starts, slots, live, weights, payload, table, pixels, *below)


def hop(block, distance):
    devices = range(lax.axis_size("facet"))
    route = [(i - distance, i) for i in devices if i - distance in devices]
    return lax.ppermute(block, "facet", route)


def gathered_sum(parts):
    mixed = lax.all_to_all(parts, "dp", 0, 0)
    return jnp.sum(mixed.astype(jnp.float32), 0)


def synthesize(dual):
    summed = jnp.zeros((FR + 8, SPAN), jnp.float32)
    for a, row_taps in enumerate((LOWPASS, HIGHPASS)):
        across = jnp.zeros((FR, SPAN), jnp.float32)
        for b, col_taps in enumerate((LOWPASS, HIGHPASS)):
            for k in range(8):
                across = across + col_taps[k] * dual[2 * a + b][:, k : k + SPAN]
        padded = jnp.pad(across, ((8, 7), (0, 0)))
        for k in range(8):
            summed = summed + row_taps[k] * padded[k : k + FR + 8]
    return summed


def analyze(extra):
    subbands = []
    for row_taps in (LOWPASS, HIGHPASS):
        filtered = sum(row_taps[k] * extra[8 - k : 8 - k + FR] for k in range(8))
        for col_taps in (LOWPASS, HIGHPASS):
            subbands.append(
                sum(col_taps[k] * filtered[:, HALO - k : HALO - k + PART] for k in range(8))
            )
    return jnp.stack(subbands)


def on_device(image, dual, payload, vis_weight, freq_start, tile_slot, live):
    table = jnp.asarray(tables())
    position = lax.axis_index("dp")
    facet = lax.axis_index("facet")
    own_rows = image[0]
    pixels = own_rows.astype(jnp.bfloat16)
    rows_above = hop(pixels, 1)
    blocks = (freq_start, tile_slot, live, vis_weight[0].T, payload[0], table)

    left = position * PART
    own_dual = lax.dynamic_slice_in_dim(
        jnp.pad(dual[:, 0], ((0, 0), (0, 0), (HALO, 128))), left, SPAN + 128, 2
    ).astype(jnp.float32)
    own_image = lax.dynamic_slice_in_dim(
        jnp.pad(own_rows, ((0, 0), (HALO, 0))), left, SPAN, 1
    )
    synth = synthesize(own_dual)

    own_terms = facet_terms(PER, pixels, *blocks)
    terms = facet_terms(0, rows_above, *blocks, own_terms)
    sums = gathered_sum(terms)
    upper_sum = sums[:FR] + jnp.pad(synth[:8], ((FR - 8, 0), (0, 0)))
    own_sum = sums[FR:] + synth[8:]
    sent_up, sent_down = lax.optimization_barrier(
        (upper_sum.astype(jnp.bfloat16), own_sum[FR - 8 :].astype(jnp.bfloat16))
    )
    from_below = hop(sent_up, -1)
    last_rows = hop(sent_down, 1)

    total = own_sum + from_below.astype(jnp.float32)
    above = last_rows.astype(jnp.float32) + upper_sum[FR - 8 :]
    image_above = lax.dynamic_slice_in_dim(
        jnp.pad(rows_above[FR - 8 :], ((0, 0), (HALO, 0))), left, SPAN, 1
    ).astype(jnp.float32)
    old = jnp.concatenate([image_above, own_image], 0)
    new = jnp.maximum(old - TAU_STEP * jnp.concatenate([above, total], 0), 0.0)
    column = lax.broadcasted_iota(jnp.int32, old.shape, 1) + left
    row = lax.broadcasted_iota(jnp.int32, old.shape, 0)
    inside = (column >= HALO) & ((row >= 8) | (facet > 0))
    extra = jnp.where(inside, 2.0 * new - old, 0.0)

    shifted = own_dual[:, :, HALO : HALO + PART] + SIGMA_STEP * analyze(extra)
    squares = lax.all_gather((shifted * shifted).astype(jnp.bfloat16), "cube")
    norms = jnp.sqrt(jnp.sum(squares.astype(jnp.float32), 0))
    dual_part = (shifted * (RADIUS / jnp.maximum(norms, RADIUS))).astype(jnp.bfloat16)
    own_part = jnp.concatenate([dual_part, total[None, :, HALO:].astype(jnp.bfloat16)], 0)
    parts = lax.all_to_all(jnp.broadcast_to(own_part, (DP,) + own_part.shape), "dp", 0, 0)
    whole = jnp.concatenate([parts[d] for d in range(DP)], -1)
    dual_next = whole[:4]
    updated = jnp.maximum(own_rows - TAU_STEP * whole[4].astype(jnp.float32), 0.0)
    return (updated[None], dual_next[:, None])


def solution(mesh):
    return jax.shard_map(
        on_device,
        mesh=mesh,
        in_specs=(
            P("cube", "facet", None),
            P(None, "cube", "facet", None),
            P("cube", ("facet", "dp"), None, None),
            P("cube", ("facet", "dp"), None),
            P("cube", ("facet", "dp")),
            P("cube", ("facet", "dp")),
            P("cube", ("facet", "dp")),
        ),
        out_specs=(P("cube", "facet", None), P(None, "cube", "facet", None)),
        check_vma=False,
    )
```

```python
import functools
import math

import jax
import jax.numpy as jnp
import numpy as np
from jax import lax
from jax.experimental import pallas as pl
from jax.experimental.pallas import tpu as pltpu
from jax.sharding import PartitionSpec as P

LOWPASS = (
    0.2303778133088964,
    0.7148465705529155,
    0.6308807679298587,
    -0.027983769416859854,
    -0.18703481171909309,
    0.030841381835560764,
    0.0328830116668852,
    -0.010597401785069032,
)
HIGHPASS = (
    -0.010597401785069032,
    -0.0328830116668852,
    0.030841381835560764,
    0.18703481171909309,
    -0.027983769416859854,
    -0.6308807679298587,
    0.7148465705529155,
    -0.2303778133088964,
)
TAU_STEP = 0.5
SIGMA_STEP = 0.5
RADIUS = 3.0

W = 2560
TILE = 16
FR = 48
BLK = 64
PER = FR // TILE
Q = 20
R = 128
DP = 4
PART = W // DP
HALO = 128
SPAN = PART + HALO
CHUNKS = W // 64
UNROLL = 4
VMEM_LIMIT = 24 * 1024 * 1024
NORM = 1.0 / math.sqrt(W)
C1, C2 = math.cos(2 * math.pi / 5), math.cos(4 * math.pi / 5)
S1, S2 = math.sin(2 * math.pi / 5), math.sin(4 * math.pi / 5)


def tables():
    x = np.arange(W).reshape(R, Q).T
    angles = (x[:, :, None] * np.arange(R)[None, None, :] % W) * (2.0 * math.pi / W)
    table = np.concatenate([np.cos(angles), -np.sin(angles)], -1).astype(jnp.bfloat16)
    return table


def times_i(value, sign):
    re, im = value
    return (-im, re) if sign > 0 else (im, -re)


def plus(u, v):
    return (u[0] + v[0], u[1] + v[1])


def minus(u, v):
    return (u[0] - v[0], u[1] - v[1])


def dft4(x, sign):
    a, b = plus(x[0], x[2]), minus(x[0], x[2])
    c, d = plus(x[1], x[3]), times_i(minus(x[1], x[3]), sign)
    return [plus(a, c), plus(b, d), minus(a, c), minus(b, d)]


def dft5(x, sign):
    t1, t2 = plus(x[1], x[4]), plus(x[2], x[3])
    t3, t4 = minus(x[1], x[4]), minus(x[2], x[3])
    m1 = tuple(z + C1 * u + C2 * v for z, u, v in zip(x[0], t1, t2))
    m2 = tuple(z + C2 * u + C1 * v for z, u, v in zip(x[0], t1, t2))
    n1 = times_i(tuple(S1 * u + S2 * v for u, v in zip(t3, t4)), sign)
    n2 = times_i(tuple(S2 * u - S1 * v for u, v in zip(t3, t4)), sign)
    return [plus(x[0], plus(t1, t2)), plus(m1, n1), plus(m2, n2), minus(m2, n2), minus(m1, n1)]


def dft20(x, sign):
    columns = [dft4([x[(5 * a + 4 * b) % 20] for a in range(4)], sign) for b in range(5)]
    out = [None] * 20
    for c in range(4):
        line = dft5([columns[b][c] for b in range(5)], sign)
        for e in range(5):
            out[(5 * c + 16 * e) % 20] = line[e]
    return out


def residue_order():
    y = lax.broadcasted_iota(jnp.int32, (PART, 128), 0)
    group = ((y.astype(jnp.float32) + 0.5) * (1.0 / Q)).astype(jnp.int32)
    target = (y - Q * group) * 32 + group
    lane = lax.broadcasted_iota(jnp.int32, (PART, 128), 1)
    tiles = [jnp.where(target == lane + 128 * j, 1.0, 0.0) for j in range(PART // 128)]
    return jnp.concatenate(tiles, 1).astype(jnp.bfloat16)


def add_blocks(base, numbers_ref, weight_ref, payload_ref, spec_ref, grad_ref, list_ref):
    lane = lax.broadcasted_iota(jnp.int32, (1, 128), 1)
    half = lane & 63

    def collect(b, count):
        slot = numbers_ref[1, b] - base
        list_ref[count] = b
        return count + jnp.where((slot >= 0) & (slot < PER), 1, 0)

    count = lax.fori_loop(0, numbers_ref[2, 0], collect, 0)
    for u in range(UNROLL):
        list_ref[count + u] = list_ref[0]
    weights = weight_ref[...]
    slot_lane = lax.broadcasted_iota(jnp.int32, (1, BLK), 1)
    ones = jnp.ones((BLK, 128), jnp.bfloat16)

    def blocks(step, carry):
        places = [step * UNROLL + u for u in range(UNROLL)]
        numbers = [list_ref[place] for place in places]
        picked = [
            jnp.where(slot_lane == jnp.where(place < count, b, -1), weights, 0.0)
            for place, b in zip(places, numbers)
        ]
        factors = jnp.dot(
            jnp.concatenate(picked, 0).astype(jnp.bfloat16), ones, preferred_element_type=jnp.float32
        )
        found = []
        for u, b in enumerate(numbers):
            start = numbers_ref[0, b]
            slot = jnp.clip(numbers_ref[1, b] - base, 0, PER - 1)
            chunk = start >> 6
            offset = start & 63
            rows = pl.ds(pl.multiple_of(slot * TILE, TILE), TILE)
            first = pltpu.roll(spec_ref[chunk, rows, :], (128 - offset) & 127, 1)
            second = pltpu.roll(spec_ref[chunk + 1, rows, :], 64 - offset, 1)
            model = jnp.where(half < 64 - offset, first, second)
            misfit = factors[TILE * u : TILE * (u + 1)] * (
                model - payload_ref[b].astype(jnp.float32)
            )
            lower = jnp.where(half >= offset, pltpu.roll(misfit, offset, 1), 0.0)
            upper = jnp.where(half < offset, pltpu.roll(misfit, 64 + offset, 1), 0.0)
            found.append((chunk, rows, lower, upper))
        for chunk, rows, lower, upper in found:
            grad_ref[chunk, rows, :] += lower
            grad_ref[chunk + 1, rows, :] += upper
        return carry

    lax.fori_loop(0, (count + UNROLL - 1) // UNROLL, blocks, 0)


def own_pass(
    numbers_ref,
    weight_ref,
    payload_ref,
    table_ref,
    pixels_ref,
    spec_ref,
    grad_ref,
    order_ref,
    list_ref,
    re_ref,
    im_ref,
):
    lane = lax.broadcasted_iota(jnp.int32, (1, 128), 1)
    low = lane < 64
    quarter = lane >> 5

    order_ref[...] = residue_order()
    stacked = jnp.concatenate(
        [pixels_ref[:, PART * g : PART * (g + 1)] for g in range(4)], 0
    )
    sorted_rows = jnp.dot(stacked, order_ref[...], preferred_element_type=jnp.float32)
    for j in range(5):
        tiles = [sorted_rows[FR * g : FR * (g + 1), 128 * j : 128 * (j + 1)] for g in range(4)]
        for p in range(4):
            turned = [
                tiles[g] if g == p else pltpu.roll(tiles[g], (32 * (g - p)) % 128, 1)
                for g in range(4)
            ]
            rows = turned[3]
            for g in range(3):
                rows = jnp.where(quarter == g, turned[g], rows)
            q = 4 * j + p
            partial = jnp.dot(
                rows.astype(jnp.bfloat16), table_ref[q], preferred_element_type=jnp.float32
            )
            re_ref[q] = partial[:, :R]
            im_ref[q] = partial[:, R:]

    def forward(i, carry):
        rows = pl.ds(pl.multiple_of(i * 8, 8), 8)
        spectrum = dft20([(re_ref[q, rows, :], im_ref[q, rows, :]) for q in range(Q)], -1)
        for k, (re, im) in enumerate(spectrum):
            re, im = re * NORM, im * NORM
            spec_ref[2 * k, rows, :] = jnp.where(low, re, pltpu.roll(im, 64, 1))
            spec_ref[2 * k + 1, rows, :] = jnp.where(low, pltpu.roll(re, 64, 1), im)
        return carry

    lax.fori_loop(0, FR // 8, forward, 0)
    spec_ref[CHUNKS] = spec_ref[0]
    grad_ref[...] = jnp.zeros_like(grad_ref)
    add_blocks(PER, numbers_ref, weight_ref, payload_ref, spec_ref, grad_ref, list_ref)


def below_pass(
    numbers_ref,
    weight_ref,
    payload_ref,
    spec_ref,
    own_ref,
    table_ref,
    order_ref,
    out_ref,
    list_ref,
    re_ref,
    im_ref,
    grad_ref,
    tile_ref,
):
    lane = lax.broadcasted_iota(jnp.int32, (1, 128), 1)
    low = lane < 64
    quarter = lane >> 5
    grad_ref[...] = own_ref[...]
    add_blocks(0, numbers_ref, weight_ref, payload_ref, spec_ref, grad_ref, list_ref)
    grad_ref[0] += grad_ref[CHUNKS]

    def backward(i, carry):
        rows = pl.ds(pl.multiple_of(i * 8, 8), 8)
        spectrum = []
        for k in range(Q):
            even, odd = grad_ref[2 * k, rows, :], grad_ref[2 * k + 1, rows, :]
            spectrum.append(
                (
                    jnp.where(low, even, pltpu.roll(odd, 64, 1)),
                    jnp.where(low, pltpu.roll(even, 64, 1), odd),
                )
            )
        for q, (re, im) in enumerate(dft20(spectrum, 1)):
            re_ref[q, rows, :] = re * NORM
            im_ref[q, rows, :] = im * NORM
        return carry

    lax.fori_loop(0, FR // 8, backward, 0)
    for j in range(5):
        places = [[] for _ in range(4)]
        for p in range(4):
            q = 4 * j + p
            pair = jnp.concatenate([re_ref[q], im_ref[q]], 1).astype(jnp.bfloat16)
            rows = lax.dot_general(
                pair, table_ref[q], (((1,), (1,)), ((), ())), preferred_element_type=jnp.float32
            )
            for g in range(4):
                places[g].append(rows if g == p else pltpu.roll(rows, (32 * (p - g)) % 128, 1))
        for g in range(4):
            tile = places[g][3]
            for p in range(3):
                tile = jnp.where(quarter == p, places[g][p], tile)
            tile_ref[5 * g + j] = tile
    mixed = jnp.concatenate(
        [jnp.concatenate([tile_ref[5 * g + j] for j in range(5)], 1) for g in range(4)], 0
    ).astype(jnp.bfloat16)
    natural = lax.dot_general(
        mixed, order_ref[...], (((1,), (1,)), ((), ())), preferred_element_type=jnp.float32
    ).astype(jnp.bfloat16)
    out_ref[0, :, :HALO] = jnp.zeros((FR, HALO), jnp.bfloat16)
    for g in range(4):
        rows = natural[FR * g : FR * (g + 1)]
        out_ref[g, :, HALO:] = rows
        if g < 3:
            out_ref[g + 1, :, :HALO] = rows[:, PART - HALO :]


SMEM_SPEC = pl.BlockSpec(memory_space=pltpu.SMEM)
VMEM_SPEC = pl.BlockSpec(memory_space=pltpu.VMEM)
SPECTRA = jax.ShapeDtypeStruct((CHUNKS + 1, FR, 128), jnp.float32)


def own_spectra(numbers, weights, payload, table, pixels):
    return pl.pallas_call(
        own_pass,
        out_shape=(SPECTRA, SPECTRA, jax.ShapeDtypeStruct((PART, PART), jnp.bfloat16)),
        in_specs=[SMEM_SPEC] + [VMEM_SPEC] * 4,
        out_specs=(VMEM_SPEC,) * 3,
        scratch_shapes=[
            pltpu.SMEM((BLK + UNROLL,), jnp.int32),
            pltpu.VMEM((Q, FR, R), jnp.float32),
            pltpu.VMEM((Q, FR, R), jnp.float32),
        ],
        compiler_params=pltpu.CompilerParams(vmem_limit_bytes=VMEM_LIMIT),
        cost_estimate=pl.CostEstimate(
            flops=2 * 10**9, bytes_accessed=4 * 10**6, transcendentals=0
        ),
        name="own_spectra",
    )(numbers, weights, payload, table, pixels)


def gradient_parts(numbers, weights, payload, spectra, own, table, order):
    return pl.pallas_call(
        below_pass,
        out_shape=jax.ShapeDtypeStruct((DP, FR, SPAN), jnp.bfloat16),
        in_specs=[SMEM_SPEC] + [VMEM_SPEC] * 6,
        out_specs=VMEM_SPEC,
        scratch_shapes=[
            pltpu.SMEM((BLK + UNROLL,), jnp.int32),
            pltpu.VMEM((Q, FR, R), jnp.float32),
            pltpu.VMEM((Q, FR, R), jnp.float32),
            pltpu.VMEM((CHUNKS + 1, FR, 128), jnp.float32),
            pltpu.VMEM((Q, FR, R), jnp.float32),
        ],
        compiler_params=pltpu.CompilerParams(vmem_limit_bytes=VMEM_LIMIT),
        cost_estimate=pl.CostEstimate(
            flops=2 * 10**9, bytes_accessed=4 * 10**6, transcendentals=0
        ),
        name="gradient_parts",
    )(numbers, weights, payload, spectra, own, table, order)


def hop(block, distance):
    devices = range(lax.axis_size("facet"))
    route = [(i - distance, i) for i in devices if i - distance in devices]
    return lax.ppermute(block, "facet", route)


def gathered_sum(parts):
    mixed = lax.all_to_all(parts, "dp", 0, 0)
    return jnp.sum(mixed.astype(jnp.float32), 0)


def synthesize(dual):
    summed = jnp.zeros((FR + 8, SPAN), jnp.float32)
    for a, row_taps in enumerate((LOWPASS, HIGHPASS)):
        across = jnp.zeros((FR, SPAN), jnp.float32)
        for b, col_taps in enumerate((LOWPASS, HIGHPASS)):
            for k in range(8):
                across = across + col_taps[k] * dual[2 * a + b][:, k : k + SPAN]
        padded = jnp.pad(across, ((8, 7), (0, 0)))
        for k in range(8):
            summed = summed + row_taps[k] * padded[k : k + FR + 8]
    return summed


def analyze(extra):
    subbands = []
    for row_taps in (LOWPASS, HIGHPASS):
        filtered = sum(row_taps[k] * extra[8 - k : 8 - k + FR] for k in range(8))
        for col_taps in (LOWPASS, HIGHPASS):
            subbands.append(
                sum(col_taps[k] * filtered[:, HALO - k : HALO - k + PART] for k in range(8))
            )
    return jnp.stack(subbands)


def on_device(image, dual, payload, vis_weight, freq_start, tile_slot, live):
    table = jnp.asarray(tables())
    position = lax.axis_index("dp")
    own_rows = image[0]
    payload_below = hop(payload[0], -1)
    meta = jnp.concatenate(
        [
            vis_weight[0].T.astype(jnp.float32),
            freq_start.astype(jnp.float32),
            tile_slot.astype(jnp.float32),
            jnp.broadcast_to(live, (1, BLK)).astype(jnp.float32),
        ],
        0,
    )
    meta_below = hop(meta, -1)
    numbers = jnp.concatenate([freq_start, tile_slot, jnp.broadcast_to(live, (1, BLK))], 0)

    left = position * PART
    own_dual = lax.dynamic_slice_in_dim(
        jnp.pad(dual[:, 0], ((0, 0), (0, 0), (HALO, 128))), left, SPAN + 128, 2
    ).astype(jnp.float32)
    old = lax.dynamic_slice_in_dim(
        jnp.pad(own_rows, ((0, 0), (HALO, 0))), left, SPAN, 1
    )
    synth = synthesize(own_dual)
    synth_below = hop(synth[:8], -1)

    spectra, own, order = own_spectra(
        numbers, meta[:TILE], payload[0], table, own_rows.astype(jnp.bfloat16)
    )
    terms = gradient_parts(
        meta_below[TILE:].astype(jnp.int32),
        meta_below[:TILE],
        payload_below,
        spectra,
        own,
        table,
        order,
    )
    synth = synth[8:] + jnp.pad(synth_below, ((FR - 8, 0), (0, 0)))
    total = gathered_sum(terms) + synth
    new = jnp.maximum(old - TAU_STEP * total, 0.0)
    column = lax.broadcasted_iota(jnp.int32, old.shape, 1) + left
    extra = jnp.where(column >= HALO, 2.0 * new - old, 0.0)
    extra_above = hop(extra[FR - 8 :].astype(jnp.bfloat16), 1).astype(jnp.float32)
    extra = jnp.concatenate([extra_above, extra], 0)

    shifted = own_dual[:, :, HALO : HALO + PART] + SIGMA_STEP * analyze(extra)
    squares = lax.all_gather((shifted * shifted).astype(jnp.bfloat16), "cube")
    norms = jnp.sqrt(jnp.sum(squares.astype(jnp.float32), 0))
    dual_part = (shifted * (RADIUS / jnp.maximum(norms, RADIUS))).astype(jnp.bfloat16)
    own_part = jnp.concatenate([dual_part, total[None, :, HALO:].astype(jnp.bfloat16)], 0)
    parts = lax.all_to_all(jnp.broadcast_to(own_part, (DP,) + own_part.shape), "dp", 0, 0)
    whole = jnp.concatenate([parts[d] for d in range(DP)], -1)
    dual_next = whole[:4]
    updated = jnp.maximum(own_rows - TAU_STEP * whole[4].astype(jnp.float32), 0.0)
    return (updated[None], dual_next[:, None])


def solution(mesh):
    return jax.shard_map(
        on_device,
        mesh=mesh,
        in_specs=(
            P("cube", "facet", None),
            P(None, "cube", "facet", None),
            P("cube", ("facet", "dp"), None, None),
            P("cube", ("facet", "dp"), None),
            P("cube", ("facet", "dp")),
            P("cube", ("facet", "dp")),
            P("cube", ("facet", "dp")),
        ),
        out_specs=(P("cube", "facet", None), P(None, "cube", "facet", None)),
        check_vma=False,
    )
```

```python
import functools
import math

import jax
import jax.numpy as jnp
import numpy as np
from jax import lax
from jax.experimental import pallas as pl
from jax.experimental.pallas import tpu as pltpu
from jax.sharding import PartitionSpec as P

LOWPASS = (
    0.2303778133088964,
    0.7148465705529155,
    0.6308807679298587,
    -0.027983769416859854,
    -0.18703481171909309,
    0.030841381835560764,
    0.0328830116668852,
    -0.010597401785069032,
)
HIGHPASS = (
    -0.010597401785069032,
    -0.0328830116668852,
    0.030841381835560764,
    0.18703481171909309,
    -0.027983769416859854,
    -0.6308807679298587,
    0.7148465705529155,
    -0.2303778133088964,
)
TAU_STEP = 0.5
SIGMA_STEP = 0.5
RADIUS = 3.0

W = 2560
TILE = 16
FR = 48
BLK = 64
PER = FR // TILE
Q = 20
R = 128
DP = 4
PART = W // DP
HALO = 128
SPAN = PART + HALO
CHUNKS = W // 64
UNROLL = 4
VMEM_LIMIT = 24 * 1024 * 1024
NORM = 1.0 / math.sqrt(W)
C1, C2 = math.cos(2 * math.pi / 5), math.cos(4 * math.pi / 5)
S1, S2 = math.sin(2 * math.pi / 5), math.sin(4 * math.pi / 5)


def tables():
    x = np.arange(W).reshape(R, Q).T
    angles = (x[:, :, None] * np.arange(R)[None, None, :] % W) * (2.0 * math.pi / W)
    table = np.concatenate([np.cos(angles), -np.sin(angles)], -1).astype(jnp.bfloat16)
    return table


def column_filters():
    band = np.zeros((2 * HALO, 2 * HALO), np.float32)
    for b, taps in enumerate((LOWPASS, HIGHPASS)):
        for k in range(8):
            j = np.arange(HALO)
            band[HALO + j - k, HALO * b + j] = taps[k]
    leading = band.astype(jnp.bfloat16)
    rest = (band - leading.astype(np.float32)).astype(jnp.bfloat16)
    return np.stack([leading, rest])


def times_i(value, sign):
    re, im = value
    return (-im, re) if sign > 0 else (im, -re)


def plus(u, v):
    return (u[0] + v[0], u[1] + v[1])


def minus(u, v):
    return (u[0] - v[0], u[1] - v[1])


def dft4(x, sign):
    a, b = plus(x[0], x[2]), minus(x[0], x[2])
    c, d = plus(x[1], x[3]), times_i(minus(x[1], x[3]), sign)
    return [plus(a, c), plus(b, d), minus(a, c), minus(b, d)]


def dft5(x, sign):
    t1, t2 = plus(x[1], x[4]), plus(x[2], x[3])
    t3, t4 = minus(x[1], x[4]), minus(x[2], x[3])
    m1 = tuple(z + C1 * u + C2 * v for z, u, v in zip(x[0], t1, t2))
    m2 = tuple(z + C2 * u + C1 * v for z, u, v in zip(x[0], t1, t2))
    n1 = times_i(tuple(S1 * u + S2 * v for u, v in zip(t3, t4)), sign)
    n2 = times_i(tuple(S2 * u - S1 * v for u, v in zip(t3, t4)), sign)
    return [plus(x[0], plus(t1, t2)), plus(m1, n1), plus(m2, n2), minus(m2, n2), minus(m1, n1)]


def dft20(x, sign):
    columns = [dft4([x[(5 * a + 4 * b) % 20] for a in range(4)], sign) for b in range(5)]
    out = [None] * 20
    for c in range(4):
        line = dft5([columns[b][c] for b in range(5)], sign)
        for e in range(5):
            out[(5 * c + 16 * e) % 20] = line[e]
    return out


def residue_order():
    y = lax.broadcasted_iota(jnp.int32, (PART, 128), 0)
    group = ((y.astype(jnp.float32) + 0.5) * (1.0 / Q)).astype(jnp.int32)
    target = (y - Q * group) * 32 + group
    lane = lax.broadcasted_iota(jnp.int32, (PART, 128), 1)
    tiles = [jnp.where(target == lane + 128 * j, 1.0, 0.0) for j in range(PART // 128)]
    return jnp.concatenate(tiles, 1).astype(jnp.bfloat16)


def add_blocks(base, numbers_ref, weight_ref, payload_ref, spec_ref, grad_ref, list_ref):
    lane = lax.broadcasted_iota(jnp.int32, (1, 128), 1)
    half = lane & 63

    def collect(b, count):
        slot = numbers_ref[1, b] - base
        list_ref[count] = b
        return count + jnp.where((slot >= 0) & (slot < PER), 1, 0)

    count = lax.fori_loop(0, numbers_ref[2, 0], collect, 0)
    for u in range(UNROLL):
        list_ref[count + u] = list_ref[0]
    weights = weight_ref[...]
    slot_lane = lax.broadcasted_iota(jnp.int32, (1, BLK), 1)
    ones = jnp.ones((BLK, 128), jnp.bfloat16)

    def blocks(step, carry):
        places = [step * UNROLL + u for u in range(UNROLL)]
        numbers = [list_ref[place] for place in places]
        picked = [
            jnp.where(slot_lane == jnp.where(place < count, b, -1), weights, 0.0)
            for place, b in zip(places, numbers)
        ]
        factors = jnp.dot(
            jnp.concatenate(picked, 0).astype(jnp.bfloat16), ones, preferred_element_type=jnp.float32
        )
        found = []
        for u, b in enumerate(numbers):
            start = numbers_ref[0, b]
            slot = jnp.clip(numbers_ref[1, b] - base, 0, PER - 1)
            chunk = start >> 6
            offset = start & 63
            rows = pl.ds(pl.multiple_of(slot * TILE, TILE), TILE)
            first = pltpu.roll(spec_ref[chunk, rows, :], (128 - offset) & 127, 1)
            second = pltpu.roll(spec_ref[chunk + 1, rows, :], 64 - offset, 1)
            model = jnp.where(half < 64 - offset, first, second)
            misfit = factors[TILE * u : TILE * (u + 1)] * (
                model - payload_ref[b].astype(jnp.float32)
            )
            lower = jnp.where(half >= offset, pltpu.roll(misfit, offset, 1), 0.0)
            upper = jnp.where(half < offset, pltpu.roll(misfit, 64 + offset, 1), 0.0)
            found.append((chunk, rows, lower, upper))
        for chunk, rows, lower, upper in found:
            grad_ref[chunk, rows, :] += lower
            grad_ref[chunk + 1, rows, :] += upper
        return carry

    lax.fori_loop(0, (count + UNROLL - 1) // UNROLL, blocks, 0)


def own_pass(
    numbers_ref,
    weight_ref,
    payload_ref,
    table_ref,
    pixels_ref,
    spec_ref,
    grad_ref,
    order_ref,
    list_ref,
    re_ref,
    im_ref,
):
    lane = lax.broadcasted_iota(jnp.int32, (1, 128), 1)
    low = lane < 64
    quarter = lane >> 5

    order_ref[...] = residue_order()
    stacked = jnp.concatenate(
        [pixels_ref[:, PART * g : PART * (g + 1)].astype(jnp.bfloat16) for g in range(4)], 0
    )
    sorted_rows = jnp.dot(stacked, order_ref[...], preferred_element_type=jnp.float32)
    for j in range(5):
        tiles = [sorted_rows[FR * g : FR * (g + 1), 128 * j : 128 * (j + 1)] for g in range(4)]
        for p in range(4):
            turned = [
                tiles[g] if g == p else pltpu.roll(tiles[g], (32 * (g - p)) % 128, 1)
                for g in range(4)
            ]
            rows = turned[3]
            for g in range(3):
                rows = jnp.where(quarter == g, turned[g], rows)
            q = 4 * j + p
            partial = jnp.dot(
                rows.astype(jnp.bfloat16), table_ref[q], preferred_element_type=jnp.float32
            )
            re_ref[q] = partial[:, :R]
            im_ref[q] = partial[:, R:]

    def forward(i, carry):
        rows = pl.ds(pl.multiple_of(i * 8, 8), 8)
        spectrum = dft20([(re_ref[q, rows, :], im_ref[q, rows, :]) for q in range(Q)], -1)
        for k, (re, im) in enumerate(spectrum):
            re, im = re * NORM, im * NORM
            spec_ref[2 * k, rows, :] = jnp.where(low, re, pltpu.roll(im, 64, 1))
            spec_ref[2 * k + 1, rows, :] = jnp.where(low, pltpu.roll(re, 64, 1), im)
        return carry

    lax.fori_loop(0, FR // 8, forward, 0)
    spec_ref[CHUNKS] = spec_ref[0]
    grad_ref[...] = jnp.zeros_like(grad_ref)
    add_blocks(PER, numbers_ref, weight_ref, payload_ref, spec_ref, grad_ref, list_ref)


def below_pass(
    numbers_ref,
    weight_ref,
    payload_ref,
    spec_ref,
    own_ref,
    table_ref,
    order_ref,
    out_ref,
    list_ref,
    re_ref,
    im_ref,
    grad_ref,
    tile_ref,
):
    lane = lax.broadcasted_iota(jnp.int32, (1, 128), 1)
    low = lane < 64
    quarter = lane >> 5
    grad_ref[...] = own_ref[...]
    add_blocks(0, numbers_ref, weight_ref, payload_ref, spec_ref, grad_ref, list_ref)
    grad_ref[0] += grad_ref[CHUNKS]

    def backward(i, carry):
        rows = pl.ds(pl.multiple_of(i * 8, 8), 8)
        spectrum = []
        for k in range(Q):
            even, odd = grad_ref[2 * k, rows, :], grad_ref[2 * k + 1, rows, :]
            spectrum.append(
                (
                    jnp.where(low, even, pltpu.roll(odd, 64, 1)),
                    jnp.where(low, pltpu.roll(even, 64, 1), odd),
                )
            )
        for q, (re, im) in enumerate(dft20(spectrum, 1)):
            re_ref[q, rows, :] = re * NORM
            im_ref[q, rows, :] = im * NORM
        return carry

    lax.fori_loop(0, FR // 8, backward, 0)
    for j in range(5):
        places = [[] for _ in range(4)]
        for p in range(4):
            q = 4 * j + p
            pair = jnp.concatenate([re_ref[q], im_ref[q]], 1).astype(jnp.bfloat16)
            rows = lax.dot_general(
                pair, table_ref[q], (((1,), (1,)), ((), ())), preferred_element_type=jnp.float32
            )
            for g in range(4):
                places[g].append(rows if g == p else pltpu.roll(rows, (32 * (p - g)) % 128, 1))
        for g in range(4):
            tile = places[g][3]
            for p in range(3):
                tile = jnp.where(quarter == p, places[g][p], tile)
            tile_ref[5 * g + j] = tile
    mixed = jnp.concatenate(
        [jnp.concatenate([tile_ref[5 * g + j] for j in range(5)], 1) for g in range(4)], 0
    ).astype(jnp.bfloat16)
    natural = lax.dot_general(
        mixed, order_ref[...], (((1,), (1,)), ((), ())), preferred_element_type=jnp.float32
    ).astype(jnp.bfloat16)
    out_ref[0, :, :HALO] = jnp.zeros((FR, HALO), jnp.bfloat16)
    for g in range(4):
        rows = natural[FR * g : FR * (g + 1)]
        out_ref[g, :, HALO:] = rows
        if g < 3:
            out_ref[g + 1, :, :HALO] = rows[:, PART - HALO :]


SMEM_SPEC = pl.BlockSpec(memory_space=pltpu.SMEM)
VMEM_SPEC = pl.BlockSpec(memory_space=pltpu.VMEM)
SPECTRA = jax.ShapeDtypeStruct((CHUNKS + 1, FR, 128), jnp.float32)


def own_spectra(numbers, weights, payload, table, pixels):
    return pl.pallas_call(
        own_pass,
        out_shape=(SPECTRA, SPECTRA, jax.ShapeDtypeStruct((PART, PART), jnp.bfloat16)),
        in_specs=[SMEM_SPEC] + [VMEM_SPEC] * 4,
        out_specs=(VMEM_SPEC,) * 3,
        scratch_shapes=[
            pltpu.SMEM((BLK + UNROLL,), jnp.int32),
            pltpu.VMEM((Q, FR, R), jnp.float32),
            pltpu.VMEM((Q, FR, R), jnp.float32),
        ],
        compiler_params=pltpu.CompilerParams(vmem_limit_bytes=VMEM_LIMIT),
        cost_estimate=pl.CostEstimate(
            flops=2 * 10**9, bytes_accessed=4 * 10**6, transcendentals=0
        ),
        name="own_spectra",
    )(numbers, weights, payload, table, pixels)


def gradient_parts(numbers, weights, payload, spectra, own, table, order):
    return pl.pallas_call(
        below_pass,
        out_shape=jax.ShapeDtypeStruct((DP, FR, SPAN), jnp.bfloat16),
        in_specs=[SMEM_SPEC] + [VMEM_SPEC] * 6,
        out_specs=VMEM_SPEC,
        scratch_shapes=[
            pltpu.SMEM((BLK + UNROLL,), jnp.int32),
            pltpu.VMEM((Q, FR, R), jnp.float32),
            pltpu.VMEM((Q, FR, R), jnp.float32),
            pltpu.VMEM((CHUNKS + 1, FR, 128), jnp.float32),
            pltpu.VMEM((Q, FR, R), jnp.float32),
        ],
        compiler_params=pltpu.CompilerParams(vmem_limit_bytes=VMEM_LIMIT),
        cost_estimate=pl.CostEstimate(
            flops=2 * 10**9, bytes_accessed=4 * 10**6, transcendentals=0
        ),
        name="gradient_parts",
    )(numbers, weights, payload, spectra, own, table, order)


def update(left_ref, parts_ref, synth_ref, old_ref, copies_ref, last_ref, total_ref):
    total = synth_ref[...]
    for d in range(DP):
        total = total + parts_ref[d].astype(jnp.float32)
    old = old_ref[...]
    new = jnp.maximum(old - TAU_STEP * total, 0.0)
    column = lax.broadcasted_iota(jnp.int32, old.shape, 1) + left_ref[0]
    extra = jnp.where(column >= HALO, 2.0 * new - old, 0.0).astype(jnp.bfloat16)
    for c in range(4):
        copies_ref[c] = extra
    last_ref[...] = extra[FR - TILE :]
    total_ref[...] = total[:, HALO:].astype(jnp.bfloat16)


def updated_columns(left, parts, synth, old):
    return pl.pallas_call(
        update,
        out_shape=(
            jax.ShapeDtypeStruct((4, FR, SPAN), jnp.bfloat16),
            jax.ShapeDtypeStruct((TILE, SPAN), jnp.bfloat16),
            jax.ShapeDtypeStruct((FR, PART), jnp.bfloat16),
        ),
        in_specs=[SMEM_SPEC] + [VMEM_SPEC] * 3,
        out_specs=(VMEM_SPEC,) * 3,
        compiler_params=pltpu.CompilerParams(vmem_limit_bytes=VMEM_LIMIT),
        name="updated_columns",
    )(left, parts, synth, old)


def shrink(
    channel_ref,
    extra_ref,
    above0_ref,
    above1_ref,
    above2_ref,
    above3_ref,
    dual_ref,
    total_ref,
    filters_ref,
    out_ref,
    rows_ref,
    own_ref,
    norm_ref,
):
    above = (above0_ref, above1_ref, above2_ref, above3_ref)
    for k in range(4):
        channel = (channel_ref[0] + 4 - k) & 3
        for j in range(PART // HALO):
            window = pl.ds(HALO * j, 2 * HALO)
            block = jnp.concatenate([above[k][:, window], extra_ref[channel, :, window]], 0)
            rows_ref[...] = jnp.dot(
                block, filters_ref[0], preferred_element_type=jnp.float32
            ) + jnp.dot(block, filters_ref[1], preferred_element_type=jnp.float32)
            tile = pl.ds(HALO * j, HALO)
            for b in range(2):
                across = [rows_ref[TILE - i : TILE - i + FR, HALO * b : HALO * (b + 1)] for i in range(8)]
                for a, taps in enumerate((LOWPASS, HIGHPASS)):
                    value = taps[0] * across[0]
                    for i in range(1, 8):
                        value = value + taps[i] * across[i]
                    s = 2 * a + b
                    moved = (
                        dual_ref[channel, s, :, tile].astype(jnp.float32) + SIGMA_STEP * value
                    )
                    if k == 0:
                        own_ref[s, :, tile] = moved
                        norm_ref[s, :, tile] = moved * moved
                    elif k < 3:
                        norm_ref[s, :, tile] += moved * moved
                    else:
                        norm = norm_ref[s, :, tile] + moved * moved
                        scale = jnp.minimum(RADIUS * lax.rsqrt(norm), 1.0)
                        result = (own_ref[s, :, tile] * scale).astype(jnp.bfloat16)
                        for d in range(DP):
                            out_ref[d, s, :, tile] = result
    for d in range(DP):
        out_ref[d, 4] = total_ref[...]


def dual_columns(channel, extra, above, dual, total, filters):
    return pl.pallas_call(
        shrink,
        out_shape=jax.ShapeDtypeStruct((DP, 5, FR, PART), jnp.bfloat16),
        in_specs=[SMEM_SPEC] + [VMEM_SPEC] * 8,
        out_specs=VMEM_SPEC,
        scratch_shapes=[
            pltpu.VMEM((FR + TILE, 2 * HALO), jnp.float32),
            pltpu.VMEM((4, FR, PART), jnp.float32),
            pltpu.VMEM((4, FR, PART), jnp.float32),
        ],
        compiler_params=pltpu.CompilerParams(vmem_limit_bytes=VMEM_LIMIT),
        name="dual_columns",
    )(channel, extra, *above, dual, total, filters)


def copies(block, axis):
    return lax.all_to_all(block, axis, 0, 0)


def hop(block, distance, turn=0):
    channels, facets = lax.axis_size("cube"), lax.axis_size("facet")
    route = [
        (c * facets + f - distance, (c + turn) % channels * facets + f)
        for c in range(channels)
        for f in range(facets)
        if 0 <= f - distance < facets
    ]
    return lax.ppermute(block, ("cube", "facet"), route)


def synthesize(dual):
    summed = jnp.zeros((FR + 8, SPAN), jnp.float32)
    for a, row_taps in enumerate((LOWPASS, HIGHPASS)):
        across = jnp.zeros((FR, SPAN), jnp.float32)
        for b, col_taps in enumerate((LOWPASS, HIGHPASS)):
            for k in range(8):
                across = across + col_taps[k] * dual[2 * a + b][:, k : k + SPAN]
        padded = jnp.pad(across, ((8, 7), (0, 0)))
        for k in range(8):
            summed = summed + row_taps[k] * padded[k : k + FR + 8]
    return summed


def on_device(image, dual, payload, vis_weight, freq_start, tile_slot, live):
    table = jnp.asarray(tables())
    filters = jnp.asarray(column_filters())
    position = lax.axis_index("dp")
    own_rows = image[0]
    payload_below = hop(payload[0], -1)
    left = position * PART
    dual_slice = lax.dynamic_slice_in_dim(
        jnp.pad(dual[:, 0], ((0, 0), (0, 0), (0, 128))), left, SPAN, 2
    )
    duals = lax.all_gather(dual_slice, "cube")

    numbers = jnp.concatenate([freq_start, tile_slot, jnp.broadcast_to(live, (1, BLK))], 0)
    meta = jnp.concatenate([vis_weight[0].T.astype(jnp.float32), numbers.astype(jnp.float32)], 0)
    meta_below = hop(meta, -1)

    own_dual = lax.dynamic_slice_in_dim(
        jnp.pad(dual[:, 0], ((0, 0), (0, 0), (HALO, 128))), left, SPAN + 128, 2
    ).astype(jnp.float32)
    old = lax.dynamic_slice_in_dim(jnp.pad(own_rows, ((0, 0), (HALO, 0))), left, SPAN, 1)
    synth = synthesize(own_dual)
    synth_below = hop(synth[:8], -1)

    spectra, own, order = own_spectra(numbers, meta[:TILE], payload[0], table, own_rows)
    terms = gradient_parts(
        meta_below[TILE:].astype(jnp.int32),
        meta_below[:TILE],
        payload_below,
        spectra,
        own,
        table,
        order,
    )
    synth = synth[8:] + jnp.pad(synth_below, ((FR - 8, 0), (0, 0)))
    parts = copies(terms, "dp")
    extra_copies, last_rows, total = updated_columns(left[None], parts, synth, old)
    extra = copies(extra_copies, "cube")
    above = [hop(last_rows, 1, k) for k in range(4)]
    channel = lax.axis_index("cube")
    result = dual_columns(channel[None], extra, above, duals, total, filters)
    whole = jnp.concatenate([part for part in copies(result, "dp")], -1)
    dual_next = whole[:4]
    updated = jnp.maximum(own_rows - TAU_STEP * whole[4].astype(jnp.float32), 0.0)
    return (updated[None], dual_next[:, None])


def solution(mesh):
    return jax.shard_map(
        on_device,
        mesh=mesh,
        in_specs=(
            P("cube", "facet", None),
            P(None, "cube", "facet", None),
            P("cube", ("facet", "dp"), None, None),
            P("cube", ("facet", "dp"), None),
            P("cube", ("facet", "dp")),
            P("cube", ("facet", "dp")),
            P("cube", ("facet", "dp")),
        ),
        out_specs=(P("cube", "facet", None), P(None, "cube", "facet", None)),
        check_vma=False,
    )
```

```python
import functools
import math

import jax
import jax.numpy as jnp
import numpy as np
from jax import lax
from jax.experimental import pallas as pl
from jax.experimental.pallas import tpu as pltpu
from jax.sharding import PartitionSpec as P

LOWPASS = (
    0.2303778133088964,
    0.7148465705529155,
    0.6308807679298587,
    -0.027983769416859854,
    -0.18703481171909309,
    0.030841381835560764,
    0.0328830116668852,
    -0.010597401785069032,
)
HIGHPASS = (
    -0.010597401785069032,
    -0.0328830116668852,
    0.030841381835560764,
    0.18703481171909309,
    -0.027983769416859854,
    -0.6308807679298587,
    0.7148465705529155,
    -0.2303778133088964,
)
TAU_STEP = 0.5
SIGMA_STEP = 0.5
RADIUS = 3.0

W = 2560
TILE = 16
FR = 48
BLK = 64
PER = FR // TILE
Q = 20
R = 128
DP = 4
PART = W // DP
HALO = 128
SPAN = PART + HALO
CHUNKS = W // 64
UNROLL = 4
VMEM_LIMIT = 24 * 1024 * 1024
NORM = 1.0 / math.sqrt(W)
C1, C2 = math.cos(2 * math.pi / 5), math.cos(4 * math.pi / 5)
S1, S2 = math.sin(2 * math.pi / 5), math.sin(4 * math.pi / 5)


def tables():
    x = np.arange(W).reshape(R, Q).T
    angles = (x[:, :, None] * np.arange(R)[None, None, :] % W) * (2.0 * math.pi / W)
    table = np.concatenate([np.cos(angles), -np.sin(angles)], -1).astype(jnp.bfloat16)
    return table


def column_filters():
    band = np.zeros((2 * HALO, 2 * HALO), np.float32)
    for b, taps in enumerate((LOWPASS, HIGHPASS)):
        for k in range(8):
            j = np.arange(HALO)
            band[HALO + j - k, HALO * b + j] = taps[k]
    leading = band.astype(jnp.bfloat16)
    rest = (band - leading.astype(np.float32)).astype(jnp.bfloat16)
    return np.stack([leading, rest])


def times_i(value, sign):
    re, im = value
    return (-im, re) if sign > 0 else (im, -re)


def plus(u, v):
    return (u[0] + v[0], u[1] + v[1])


def minus(u, v):
    return (u[0] - v[0], u[1] - v[1])


def dft4(x, sign):
    a, b = plus(x[0], x[2]), minus(x[0], x[2])
    c, d = plus(x[1], x[3]), times_i(minus(x[1], x[3]), sign)
    return [plus(a, c), plus(b, d), minus(a, c), minus(b, d)]


def dft5(x, sign):
    t1, t2 = plus(x[1], x[4]), plus(x[2], x[3])
    t3, t4 = minus(x[1], x[4]), minus(x[2], x[3])
    m1 = tuple(z + C1 * u + C2 * v for z, u, v in zip(x[0], t1, t2))
    m2 = tuple(z + C2 * u + C1 * v for z, u, v in zip(x[0], t1, t2))
    n1 = times_i(tuple(S1 * u + S2 * v for u, v in zip(t3, t4)), sign)
    n2 = times_i(tuple(S2 * u - S1 * v for u, v in zip(t3, t4)), sign)
    return [plus(x[0], plus(t1, t2)), plus(m1, n1), plus(m2, n2), minus(m2, n2), minus(m1, n1)]


def dft20(x, sign):
    columns = [dft4([x[(5 * a + 4 * b) % 20] for a in range(4)], sign) for b in range(5)]
    out = [None] * 20
    for c in range(4):
        line = dft5([columns[b][c] for b in range(5)], sign)
        for e in range(5):
            out[(5 * c + 16 * e) % 20] = line[e]
    return out


def residue_order():
    y = lax.broadcasted_iota(jnp.int32, (PART, 128), 0)
    group = ((y.astype(jnp.float32) + 0.5) * (1.0 / Q)).astype(jnp.int32)
    target = (y - Q * group) * 32 + group
    lane = lax.broadcasted_iota(jnp.int32, (PART, 128), 1)
    tiles = [jnp.where(target == lane + 128 * j, 1.0, 0.0) for j in range(PART // 128)]
    return jnp.concatenate(tiles, 1).astype(jnp.bfloat16)


def add_blocks(base, numbers_ref, weight_ref, payload_ref, spec_ref, grad_ref, list_ref):
    lane = lax.broadcasted_iota(jnp.int32, (1, 128), 1)
    half = lane & 63

    def collect(b, count):
        slot = numbers_ref[1, b] - base
        list_ref[count] = b
        return count + jnp.where((slot >= 0) & (slot < PER), 1, 0)

    count = lax.fori_loop(0, numbers_ref[2, 0], collect, 0)
    for u in range(UNROLL):
        list_ref[count + u] = list_ref[0]
    weights = weight_ref[...]
    slot_lane = lax.broadcasted_iota(jnp.int32, (1, BLK), 1)
    ones = jnp.ones((BLK, 128), jnp.bfloat16)

    def blocks(step, carry):
        places = [step * UNROLL + u for u in range(UNROLL)]
        numbers = [list_ref[place] for place in places]
        picked = [
            jnp.where(slot_lane == jnp.where(place < count, b, -1), weights, 0.0)
            for place, b in zip(places, numbers)
        ]
        factors = jnp.dot(
            jnp.concatenate(picked, 0).astype(jnp.bfloat16), ones, preferred_element_type=jnp.float32
        )
        found = []
        for u, b in enumerate(numbers):
            start = numbers_ref[0, b]
            slot = jnp.clip(numbers_ref[1, b] - base, 0, PER - 1)
            chunk = start >> 6
            offset = start & 63
            rows = pl.ds(pl.multiple_of(slot * TILE, TILE), TILE)
            first = pltpu.roll(spec_ref[chunk, rows, :], (128 - offset) & 127, 1)
            second = pltpu.roll(spec_ref[chunk + 1, rows, :], 64 - offset, 1)
            model = jnp.where(half < 64 - offset, first, second)
            misfit = factors[TILE * u : TILE * (u + 1)] * (
                model - payload_ref[b].astype(jnp.float32)
            )
            lower = jnp.where(half >= offset, pltpu.roll(misfit, offset, 1), 0.0)
            upper = jnp.where(half < offset, pltpu.roll(misfit, 64 + offset, 1), 0.0)
            found.append((chunk, rows, lower, upper))
        for chunk, rows, lower, upper in found:
            grad_ref[chunk, rows, :] += lower
            grad_ref[chunk + 1, rows, :] += upper
        return carry

    lax.fori_loop(0, (count + UNROLL - 1) // UNROLL, blocks, 0)


def own_pass(
    numbers_ref,
    weight_ref,
    payload_ref,
    table_ref,
    pixels_ref,
    spec_ref,
    grad_ref,
    order_ref,
    list_ref,
    re_ref,
    im_ref,
):
    lane = lax.broadcasted_iota(jnp.int32, (1, 128), 1)
    low = lane < 64
    quarter = lane >> 5

    order_ref[...] = residue_order()
    stacked = jnp.concatenate(
        [pixels_ref[:, PART * g : PART * (g + 1)].astype(jnp.bfloat16) for g in range(4)], 0
    )
    sorted_rows = jnp.dot(stacked, order_ref[...], preferred_element_type=jnp.float32)
    for j in range(5):
        tiles = [sorted_rows[FR * g : FR * (g + 1), 128 * j : 128 * (j + 1)] for g in range(4)]
        for p in range(4):
            turned = [
                tiles[g] if g == p else pltpu.roll(tiles[g], (32 * (g - p)) % 128, 1)
                for g in range(4)
            ]
            rows = turned[3]
            for g in range(3):
                rows = jnp.where(quarter == g, turned[g], rows)
            q = 4 * j + p
            partial = jnp.dot(
                rows.astype(jnp.bfloat16), table_ref[q], preferred_element_type=jnp.float32
            )
            re_ref[q] = partial[:, :R]
            im_ref[q] = partial[:, R:]

    def forward(i, carry):
        rows = pl.ds(pl.multiple_of(i * 8, 8), 8)
        spectrum = dft20([(re_ref[q, rows, :], im_ref[q, rows, :]) for q in range(Q)], -1)
        for k, (re, im) in enumerate(spectrum):
            re, im = re * NORM, im * NORM
            spec_ref[2 * k, rows, :] = jnp.where(low, re, pltpu.roll(im, 64, 1))
            spec_ref[2 * k + 1, rows, :] = jnp.where(low, pltpu.roll(re, 64, 1), im)
        return carry

    lax.fori_loop(0, FR // 8, forward, 0)
    spec_ref[CHUNKS] = spec_ref[0]
    grad_ref[...] = jnp.zeros_like(grad_ref)
    add_blocks(PER, numbers_ref, weight_ref, payload_ref, spec_ref, grad_ref, list_ref)


def below_pass(
    numbers_ref,
    weight_ref,
    payload_ref,
    spec_ref,
    own_ref,
    table_ref,
    order_ref,
    out_ref,
    list_ref,
    re_ref,
    im_ref,
    grad_ref,
    tile_ref,
):
    lane = lax.broadcasted_iota(jnp.int32, (1, 128), 1)
    low = lane < 64
    quarter = lane >> 5
    grad_ref[...] = own_ref[...]
    add_blocks(0, numbers_ref, weight_ref, payload_ref, spec_ref, grad_ref, list_ref)
    grad_ref[0] += grad_ref[CHUNKS]

    def backward(i, carry):
        rows = pl.ds(pl.multiple_of(i * 8, 8), 8)
        spectrum = []
        for k in range(Q):
            even, odd = grad_ref[2 * k, rows, :], grad_ref[2 * k + 1, rows, :]
            spectrum.append(
                (
                    jnp.where(low, even, pltpu.roll(odd, 64, 1)),
                    jnp.where(low, pltpu.roll(even, 64, 1), odd),
                )
            )
        for q, (re, im) in enumerate(dft20(spectrum, 1)):
            re_ref[q, rows, :] = re * NORM
            im_ref[q, rows, :] = im * NORM
        return carry

    lax.fori_loop(0, FR // 8, backward, 0)
    for j in range(5):
        places = [[] for _ in range(4)]
        for p in range(4):
            q = 4 * j + p
            pair = jnp.concatenate([re_ref[q], im_ref[q]], 1).astype(jnp.bfloat16)
            rows = lax.dot_general(
                pair, table_ref[q], (((1,), (1,)), ((), ())), preferred_element_type=jnp.float32
            )
            for g in range(4):
                places[g].append(rows if g == p else pltpu.roll(rows, (32 * (p - g)) % 128, 1))
        for g in range(4):
            tile = places[g][3]
            for p in range(3):
                tile = jnp.where(quarter == p, places[g][p], tile)
            tile_ref[5 * g + j] = tile
    mixed = jnp.concatenate(
        [jnp.concatenate([tile_ref[5 * g + j] for j in range(5)], 1) for g in range(4)], 0
    ).astype(jnp.bfloat16)
    natural = lax.dot_general(
        mixed, order_ref[...], (((1,), (1,)), ((), ())), preferred_element_type=jnp.float32
    ).astype(jnp.bfloat16)
    out_ref[0, :, :HALO] = jnp.zeros((FR, HALO), jnp.bfloat16)
    for g in range(4):
        rows = natural[FR * g : FR * (g + 1)]
        out_ref[g, :, HALO:] = rows
        if g < 3:
            out_ref[g + 1, :, :HALO] = rows[:, PART - HALO :]


SMEM_SPEC = pl.BlockSpec(memory_space=pltpu.SMEM)
VMEM_SPEC = pl.BlockSpec(memory_space=pltpu.VMEM)
SPECTRA = jax.ShapeDtypeStruct((CHUNKS + 1, FR, 128), jnp.float32)


def own_spectra(numbers, weights, payload, table, pixels):
    return pl.pallas_call(
        own_pass,
        out_shape=(SPECTRA, SPECTRA, jax.ShapeDtypeStruct((PART, PART), jnp.bfloat16)),
        in_specs=[SMEM_SPEC] + [VMEM_SPEC] * 4,
        out_specs=(VMEM_SPEC,) * 3,
        scratch_shapes=[
            pltpu.SMEM((BLK + UNROLL,), jnp.int32),
            pltpu.VMEM((Q, FR, R), jnp.float32),
            pltpu.VMEM((Q, FR, R), jnp.float32),
        ],
        compiler_params=pltpu.CompilerParams(vmem_limit_bytes=VMEM_LIMIT),
        cost_estimate=pl.CostEstimate(
            flops=2 * 10**9, bytes_accessed=4 * 10**6, transcendentals=0
        ),
        name="own_spectra",
    )(numbers, weights, payload, table, pixels)


def gradient_parts(numbers, weights, payload, spectra, own, table, order):
    return pl.pallas_call(
        below_pass,
        out_shape=jax.ShapeDtypeStruct((DP, FR, SPAN), jnp.bfloat16),
        in_specs=[SMEM_SPEC] + [VMEM_SPEC] * 6,
        out_specs=VMEM_SPEC,
        scratch_shapes=[
            pltpu.SMEM((BLK + UNROLL,), jnp.int32),
            pltpu.VMEM((Q, FR, R), jnp.float32),
            pltpu.VMEM((Q, FR, R), jnp.float32),
            pltpu.VMEM((CHUNKS + 1, FR, 128), jnp.float32),
            pltpu.VMEM((Q, FR, R), jnp.float32),
        ],
        compiler_params=pltpu.CompilerParams(vmem_limit_bytes=VMEM_LIMIT),
        cost_estimate=pl.CostEstimate(
            flops=2 * 10**9, bytes_accessed=4 * 10**6, transcendentals=0
        ),
        name="gradient_parts",
    )(numbers, weights, payload, spectra, own, table, order)


def update(left_ref, parts_ref, synth_ref, old_ref, copies_ref, last_ref, total_ref):
    total = synth_ref[...]
    for d in range(DP):
        total = total + parts_ref[d].astype(jnp.float32)
    old = old_ref[...]
    new = jnp.maximum(old - TAU_STEP * total, 0.0)
    column = lax.broadcasted_iota(jnp.int32, old.shape, 1) + left_ref[0]
    extra = jnp.where(column >= HALO, 2.0 * new - old, 0.0).astype(jnp.bfloat16)
    for c in range(4):
        copies_ref[c] = extra
    last_ref[...] = extra[FR - TILE :]
    total_ref[...] = total[:, HALO:].astype(jnp.bfloat16)


def updated_columns(left, parts, synth, old):
    return pl.pallas_call(
        update,
        out_shape=(
            jax.ShapeDtypeStruct((4, FR, SPAN), jnp.bfloat16),
            jax.ShapeDtypeStruct((TILE, SPAN), jnp.bfloat16),
            jax.ShapeDtypeStruct((FR, PART), jnp.bfloat16),
        ),
        in_specs=[SMEM_SPEC] + [VMEM_SPEC] * 3,
        out_specs=(VMEM_SPEC,) * 3,
        compiler_params=pltpu.CompilerParams(vmem_limit_bytes=VMEM_LIMIT),
        name="updated_columns",
    )(left, parts, synth, old)


def shrink(
    channel_ref,
    extra_ref,
    above_ref,
    dual_ref,
    total_ref,
    filters_ref,
    out_ref,
    rows_ref,
    own_ref,
    norm_ref,
):
    for k in range(4):
        channel = (channel_ref[0] + 4 - k) & 3
        for j in range(PART // HALO):
            window = pl.ds(HALO * j, 2 * HALO)
            block = jnp.concatenate(
                [above_ref[channel, :, window], extra_ref[channel, :, window]], 0
            )
            rows_ref[...] = jnp.dot(
                block, filters_ref[0], preferred_element_type=jnp.float32
            ) + jnp.dot(block, filters_ref[1], preferred_element_type=jnp.float32)
            tile = pl.ds(HALO * j, HALO)
            for b in range(2):
                across = [rows_ref[TILE - i : TILE - i + FR, HALO * b : HALO * (b + 1)] for i in range(8)]
                for a, taps in enumerate((LOWPASS, HIGHPASS)):
                    value = taps[0] * across[0]
                    for i in range(1, 8):
                        value = value + taps[i] * across[i]
                    s = 2 * a + b
                    moved = (
                        dual_ref[channel, s, :, tile].astype(jnp.float32) + SIGMA_STEP * value
                    )
                    if k == 0:
                        own_ref[s, :, tile] = moved
                        norm_ref[s, :, tile] = moved * moved
                    elif k < 3:
                        norm_ref[s, :, tile] += moved * moved
                    else:
                        norm = norm_ref[s, :, tile] + moved * moved
                        scale = jnp.minimum(RADIUS * lax.rsqrt(norm), 1.0)
                        result = (own_ref[s, :, tile] * scale).astype(jnp.bfloat16)
                        for d in range(DP):
                            out_ref[d, s, :, tile] = result
    for d in range(DP):
        out_ref[d, 4] = total_ref[...]


def dual_columns(channel, extra, above, dual, total, filters):
    return pl.pallas_call(
        shrink,
        out_shape=jax.ShapeDtypeStruct((DP, 5, FR, PART), jnp.bfloat16),
        in_specs=[SMEM_SPEC] + [VMEM_SPEC] * 5,
        out_specs=VMEM_SPEC,
        scratch_shapes=[
            pltpu.VMEM((FR + TILE, 2 * HALO), jnp.float32),
            pltpu.VMEM((4, FR, PART), jnp.float32),
            pltpu.VMEM((4, FR, PART), jnp.float32),
        ],
        compiler_params=pltpu.CompilerParams(vmem_limit_bytes=VMEM_LIMIT),
        name="dual_columns",
    )(channel, extra, above, dual, total, filters)


def exchange(parts, axis):
    return lax.all_to_all(parts, axis, 0, 0)


def gather(block, axis):
    return exchange(jnp.broadcast_to(block, (lax.axis_size(axis),) + block.shape), axis)


def hop(block, distance):
    devices = range(lax.axis_size("facet"))
    route = [(i - distance, i) for i in devices if i - distance in devices]
    return lax.ppermute(block, "facet", route)


def synthesize(dual):
    summed = jnp.zeros((FR + 8, SPAN), jnp.float32)
    for a, row_taps in enumerate((LOWPASS, HIGHPASS)):
        across = jnp.zeros((FR, SPAN), jnp.float32)
        for b, col_taps in enumerate((LOWPASS, HIGHPASS)):
            for k in range(8):
                across = across + col_taps[k] * dual[2 * a + b][:, k : k + SPAN]
        padded = jnp.pad(across, ((8, 7), (0, 0)))
        for k in range(8):
            summed = summed + row_taps[k] * padded[k : k + FR + 8]
    return summed


def on_device(image, dual, payload, vis_weight, freq_start, tile_slot, live):
    table = jnp.asarray(tables())
    filters = jnp.asarray(column_filters())
    position = lax.axis_index("dp")
    own_rows = image[0]
    payload_below = hop(payload[0], -1)
    left = position * PART
    numbers = jnp.concatenate([freq_start, tile_slot, jnp.broadcast_to(live, (1, BLK))], 0)
    meta = jnp.concatenate([vis_weight[0].T.astype(jnp.float32), numbers.astype(jnp.float32)], 0)
    meta_below = hop(meta, -1)

    spectra, own, order = own_spectra(numbers, meta[:TILE], payload[0], table, own_rows)
    own_dual, order = lax.optimization_barrier((dual[:, 0], order))
    duals = gather(lax.dynamic_slice_in_dim(own_dual, left, PART, 2), "cube")
    terms = gradient_parts(
        meta_below[TILE:].astype(jnp.int32),
        meta_below[:TILE],
        payload_below,
        spectra,
        own,
        table,
        order,
    )
    own_dual, own_rows, terms = lax.optimization_barrier((own_dual, own_rows, terms))
    parts = exchange(terms, "dp")
    dual_slice = lax.dynamic_slice_in_dim(
        jnp.pad(own_dual, ((0, 0), (0, 0), (HALO, 128))), left, SPAN + 128, 2
    ).astype(jnp.float32)
    old = lax.dynamic_slice_in_dim(jnp.pad(own_rows, ((0, 0), (HALO, 0))), left, SPAN, 1)
    synth = synthesize(dual_slice)
    synth_below = hop(synth[:8], -1)
    synth = synth[8:] + jnp.pad(synth_below, ((FR - 8, 0), (0, 0)))
    extra_copies, last_rows, total = updated_columns(left[None], parts, synth, old)
    above = hop(last_rows, 1)
    extra = exchange(extra_copies, "cube")
    above = gather(above, "cube")
    channel = lax.axis_index("cube")
    result = dual_columns(channel[None], extra, above, duals, total, filters)
    whole = jnp.concatenate([part for part in exchange(result, "dp")], -1)
    dual_next = whole[:4]
    updated = jnp.maximum(own_rows - TAU_STEP * whole[4].astype(jnp.float32), 0.0)
    return (updated[None], dual_next[:, None])


def solution(mesh):
    return jax.shard_map(
        on_device,
        mesh=mesh,
        in_specs=(
            P("cube", "facet", None),
            P(None, "cube", "facet", None),
            P("cube", ("facet", "dp"), None, None),
            P("cube", ("facet", "dp"), None),
            P("cube", ("facet", "dp")),
            P("cube", ("facet", "dp")),
            P("cube", ("facet", "dp")),
        ),
        out_specs=(P("cube", "facet", None), P(None, "cube", "facet", None)),
        check_vma=False,
    )
```

```python
import functools
import math

import jax
import jax.numpy as jnp
import numpy as np
from jax import lax
from jax.experimental import pallas as pl
from jax.experimental.pallas import tpu as pltpu
from jax.sharding import PartitionSpec as P

LOWPASS = (
    0.2303778133088964,
    0.7148465705529155,
    0.6308807679298587,
    -0.027983769416859854,
    -0.18703481171909309,
    0.030841381835560764,
    0.0328830116668852,
    -0.010597401785069032,
)
HIGHPASS = (
    -0.010597401785069032,
    -0.0328830116668852,
    0.030841381835560764,
    0.18703481171909309,
    -0.027983769416859854,
    -0.6308807679298587,
    0.7148465705529155,
    -0.2303778133088964,
)
TAU_STEP = 0.5
SIGMA_STEP = 0.5
RADIUS = 3.0

W = 2560
TILE = 16
FR = 48
BLK = 64
PER = FR // TILE
Q = 20
R = 128
DP = 4
PART = W // DP
HALO = 128
SPAN = PART + HALO
CHUNKS = W // 64
UNROLL = 4
NUMBERS = SPAN + 2 * HALO
VMEM_LIMIT = 24 * 1024 * 1024
NORM = 1.0 / math.sqrt(W)
C1, C2 = math.cos(2 * math.pi / 5), math.cos(4 * math.pi / 5)
S1, S2 = math.sin(2 * math.pi / 5), math.sin(4 * math.pi / 5)


def tables():
    x = np.arange(W).reshape(R, Q).T
    angles = (x[:, :, None] * np.arange(R)[None, None, :] % W) * (2.0 * math.pi / W)
    table = np.concatenate([np.cos(angles), -np.sin(angles)], -1).astype(jnp.bfloat16)
    return table


def column_filters():
    band = np.zeros((2 * HALO, 2 * HALO), np.float32)
    for b, taps in enumerate((LOWPASS, HIGHPASS)):
        for k in range(8):
            j = np.arange(HALO)
            band[HALO + j - k, HALO * b + j] = taps[k]
    leading = band.astype(jnp.bfloat16)
    rest = (band - leading.astype(np.float32)).astype(jnp.bfloat16)
    return np.stack([leading, rest])


def times_i(value, sign):
    re, im = value
    return (-im, re) if sign > 0 else (im, -re)


def plus(u, v):
    return (u[0] + v[0], u[1] + v[1])


def minus(u, v):
    return (u[0] - v[0], u[1] - v[1])


def dft4(x, sign):
    a, b = plus(x[0], x[2]), minus(x[0], x[2])
    c, d = plus(x[1], x[3]), times_i(minus(x[1], x[3]), sign)
    return [plus(a, c), plus(b, d), minus(a, c), minus(b, d)]


def dft5(x, sign):
    t1, t2 = plus(x[1], x[4]), plus(x[2], x[3])
    t3, t4 = minus(x[1], x[4]), minus(x[2], x[3])
    m1 = tuple(z + C1 * u + C2 * v for z, u, v in zip(x[0], t1, t2))
    m2 = tuple(z + C2 * u + C1 * v for z, u, v in zip(x[0], t1, t2))
    n1 = times_i(tuple(S1 * u + S2 * v for u, v in zip(t3, t4)), sign)
    n2 = times_i(tuple(S2 * u - S1 * v for u, v in zip(t3, t4)), sign)
    return [plus(x[0], plus(t1, t2)), plus(m1, n1), plus(m2, n2), minus(m2, n2), minus(m1, n1)]


def dft20(x, sign):
    columns = [dft4([x[(5 * a + 4 * b) % 20] for a in range(4)], sign) for b in range(5)]
    out = [None] * 20
    for c in range(4):
        line = dft5([columns[b][c] for b in range(5)], sign)
        for e in range(5):
            out[(5 * c + 16 * e) % 20] = line[e]
    return out


def residue_order():
    y = lax.broadcasted_iota(jnp.int32, (PART, 128), 0)
    group = ((y.astype(jnp.float32) + 0.5) * (1.0 / Q)).astype(jnp.int32)
    target = (y - Q * group) * 32 + group
    lane = lax.broadcasted_iota(jnp.int32, (PART, 128), 1)
    tiles = [jnp.where(target == lane + 128 * j, 1.0, 0.0) for j in range(PART // 128)]
    return jnp.concatenate(tiles, 1).astype(jnp.bfloat16)


def add_blocks(base, numbers_ref, weights, payload_ref, spec_ref, grad_ref, list_ref):
    lane = lax.broadcasted_iota(jnp.int32, (1, 128), 1)
    half = lane & 63

    def collect(b, count):
        slot = numbers_ref[1, b] - base
        list_ref[count] = b
        return count + jnp.where((slot >= 0) & (slot < PER), 1, 0)

    count = lax.fori_loop(0, numbers_ref[2, 0], collect, 0)
    for u in range(UNROLL):
        list_ref[count + u] = list_ref[0]
    slot_lane = lax.broadcasted_iota(jnp.int32, (1, 128), 1)
    ones = jnp.ones((128, 128), jnp.bfloat16)

    def blocks(step, carry):
        places = [step * UNROLL + u for u in range(UNROLL)]
        numbers = [list_ref[place] for place in places]
        picked = [
            jnp.where(slot_lane == jnp.where(place < count, b, -1), weights, 0.0)
            for place, b in zip(places, numbers)
        ]
        factors = jnp.dot(
            jnp.concatenate(picked, 0).astype(jnp.bfloat16), ones, preferred_element_type=jnp.float32
        )
        found = []
        for u, b in enumerate(numbers):
            start = numbers_ref[0, b]
            slot = jnp.clip(numbers_ref[1, b] - base, 0, PER - 1)
            chunk = start >> 6
            offset = start & 63
            rows = pl.ds(pl.multiple_of(slot * TILE, TILE), TILE)
            first = pltpu.roll(spec_ref[chunk, rows, :], (128 - offset) & 127, 1)
            second = pltpu.roll(spec_ref[chunk + 1, rows, :], 64 - offset, 1)
            model = jnp.where(half < 64 - offset, first, second)
            misfit = factors[TILE * u : TILE * (u + 1)] * (
                model - payload_ref[b].astype(jnp.float32)
            )
            lower = jnp.where(half >= offset, pltpu.roll(misfit, offset, 1), 0.0)
            upper = jnp.where(half < offset, pltpu.roll(misfit, 64 + offset, 1), 0.0)
            found.append((chunk, rows, lower, upper))
        for chunk, rows, lower, upper in found:
            grad_ref[chunk, rows, :] += lower
            grad_ref[chunk + 1, rows, :] += upper
        return carry

    lax.fori_loop(0, (count + UNROLL - 1) // UNROLL, blocks, 0)


def own_pass(
    numbers_ref,
    weight_ref,
    payload_ref,
    table_ref,
    pixels_ref,
    spec_ref,
    grad_ref,
    order_ref,
    list_ref,
    re_ref,
    im_ref,
):
    lane = lax.broadcasted_iota(jnp.int32, (1, 128), 1)
    low = lane < 64
    quarter = lane >> 5

    order_ref[...] = residue_order()
    stacked = jnp.concatenate(
        [pixels_ref[:, PART * g : PART * (g + 1)].astype(jnp.bfloat16) for g in range(4)], 0
    )
    sorted_rows = jnp.dot(stacked, order_ref[...], preferred_element_type=jnp.float32)
    for j in range(5):
        tiles = [sorted_rows[FR * g : FR * (g + 1), 128 * j : 128 * (j + 1)] for g in range(4)]
        for p in range(4):
            turned = [
                tiles[g] if g == p else pltpu.roll(tiles[g], (32 * (g - p)) % 128, 1)
                for g in range(4)
            ]
            rows = turned[3]
            for g in range(3):
                rows = jnp.where(quarter == g, turned[g], rows)
            q = 4 * j + p
            partial = jnp.dot(
                rows.astype(jnp.bfloat16), table_ref[q], preferred_element_type=jnp.float32
            )
            re_ref[q] = partial[:, :R]
            im_ref[q] = partial[:, R:]

    def forward(i, carry):
        rows = pl.ds(pl.multiple_of(i * 8, 8), 8)
        spectrum = dft20([(re_ref[q, rows, :], im_ref[q, rows, :]) for q in range(Q)], -1)
        for k, (re, im) in enumerate(spectrum):
            re, im = re * NORM, im * NORM
            spec_ref[2 * k, rows, :] = jnp.where(low, re, pltpu.roll(im, 64, 1))
            spec_ref[2 * k + 1, rows, :] = jnp.where(low, pltpu.roll(re, 64, 1), im)
        return carry

    lax.fori_loop(0, FR // 8, forward, 0)
    spec_ref[CHUNKS] = spec_ref[0]
    grad_ref[...] = jnp.zeros_like(grad_ref)
    blank = jnp.zeros((TILE, 128 - BLK), jnp.float32)
    weights = jnp.concatenate([weight_ref[...].astype(jnp.float32), blank], 1)
    add_blocks(PER, numbers_ref, weights, payload_ref, spec_ref, grad_ref, list_ref)


def below_pass(
    numbers_ref,
    mail_ref,
    payload_ref,
    spec_ref,
    own_ref,
    table_ref,
    order_ref,
    out_ref,
    list_ref,
    re_ref,
    im_ref,
    grad_ref,
    tile_ref,
):
    lane = lax.broadcasted_iota(jnp.int32, (1, 128), 1)
    low = lane < 64
    quarter = lane >> 5
    grad_ref[...] = own_ref[...]
    weights = jnp.concatenate(
        [mail_ref[:, SPAN : SPAN + HALO], mail_ref[:, SPAN + HALO : NUMBERS]], 0
    )
    add_blocks(0, numbers_ref, weights, payload_ref, spec_ref, grad_ref, list_ref)
    grad_ref[0] += grad_ref[CHUNKS]

    def backward(i, carry):
        rows = pl.ds(pl.multiple_of(i * 8, 8), 8)
        spectrum = []
        for k in range(Q):
            even, odd = grad_ref[2 * k, rows, :], grad_ref[2 * k + 1, rows, :]
            spectrum.append(
                (
                    jnp.where(low, even, pltpu.roll(odd, 64, 1)),
                    jnp.where(low, pltpu.roll(even, 64, 1), odd),
                )
            )
        for q, (re, im) in enumerate(dft20(spectrum, 1)):
            re_ref[q, rows, :] = re * NORM
            im_ref[q, rows, :] = im * NORM
        return carry

    lax.fori_loop(0, FR // 8, backward, 0)
    for j in range(5):
        places = [[] for _ in range(4)]
        for p in range(4):
            q = 4 * j + p
            pair = jnp.concatenate([re_ref[q], im_ref[q]], 1).astype(jnp.bfloat16)
            rows = lax.dot_general(
                pair, table_ref[q], (((1,), (1,)), ((), ())), preferred_element_type=jnp.float32
            )
            for g in range(4):
                places[g].append(rows if g == p else pltpu.roll(rows, (32 * (p - g)) % 128, 1))
        for g in range(4):
            tile = places[g][3]
            for p in range(3):
                tile = jnp.where(quarter == p, places[g][p], tile)
            tile_ref[5 * g + j] = tile
    mixed = jnp.concatenate(
        [jnp.concatenate([tile_ref[5 * g + j] for j in range(5)], 1) for g in range(4)], 0
    ).astype(jnp.bfloat16)
    natural = lax.dot_general(
        mixed, order_ref[...], (((1,), (1,)), ((), ())), preferred_element_type=jnp.float32
    ).astype(jnp.bfloat16)
    out_ref[0, :, :HALO] = jnp.zeros((FR, HALO), jnp.bfloat16)
    for g in range(4):
        rows = natural[FR * g : FR * (g + 1)]
        out_ref[g, :, HALO:] = rows
        if g < 3:
            out_ref[g + 1, :, :HALO] = rows[:, PART - HALO :]


SMEM_SPEC = pl.BlockSpec(memory_space=pltpu.SMEM)
VMEM_SPEC = pl.BlockSpec(memory_space=pltpu.VMEM)
SPECTRA = jax.ShapeDtypeStruct((CHUNKS + 1, FR, 128), jnp.float32)


def own_spectra(numbers, weights, payload, table, pixels):
    return pl.pallas_call(
        own_pass,
        out_shape=(SPECTRA, SPECTRA, jax.ShapeDtypeStruct((PART, PART), jnp.bfloat16)),
        in_specs=[SMEM_SPEC] + [VMEM_SPEC] * 4,
        out_specs=(VMEM_SPEC,) * 3,
        scratch_shapes=[
            pltpu.SMEM((BLK + UNROLL,), jnp.int32),
            pltpu.VMEM((Q, FR, R), jnp.float32),
            pltpu.VMEM((Q, FR, R), jnp.float32),
        ],
        compiler_params=pltpu.CompilerParams(vmem_limit_bytes=VMEM_LIMIT),
        cost_estimate=pl.CostEstimate(
            flops=2 * 10**9, bytes_accessed=4 * 10**6, transcendentals=0
        ),
        name="own_spectra",
    )(numbers, weights, payload, table, pixels)


def gradient_parts(numbers, mail, payload, spectra, own, table, order):
    return pl.pallas_call(
        below_pass,
        out_shape=jax.ShapeDtypeStruct((DP, FR, SPAN), jnp.bfloat16),
        in_specs=[SMEM_SPEC] + [VMEM_SPEC] * 6,
        out_specs=VMEM_SPEC,
        scratch_shapes=[
            pltpu.SMEM((BLK + UNROLL,), jnp.int32),
            pltpu.VMEM((Q, FR, R), jnp.float32),
            pltpu.VMEM((Q, FR, R), jnp.float32),
            pltpu.VMEM((CHUNKS + 1, FR, 128), jnp.float32),
            pltpu.VMEM((Q, FR, R), jnp.float32),
        ],
        compiler_params=pltpu.CompilerParams(vmem_limit_bytes=VMEM_LIMIT),
        cost_estimate=pl.CostEstimate(
            flops=2 * 10**9, bytes_accessed=4 * 10**6, transcendentals=0
        ),
        name="gradient_parts",
    )(numbers, mail, payload, spectra, own, table, order)


def prepare(
    part_ref, numbers_ref, weight_ref, dual_ref, filters_ref, mail_ref, synth_ref, rows_ref
):
    part = part_ref[0]
    for a, taps in enumerate((LOWPASS, HIGHPASS)):
        rows_ref[a, :8] = jnp.zeros((8, SPAN), jnp.float32)
        rows_ref[a, 8 + FR :] = jnp.zeros((8, SPAN), jnp.float32)
        for j in range(SPAN // HALO + 1):
            place = (PART // HALO) * part - 1 + j
            inside = (place >= 0) & (place < W // HALO)
            columns = pl.ds(pl.multiple_of(jnp.clip(place, 0, W // HALO - 1) * HALO, HALO), HALO)
            pair = jnp.concatenate([dual_ref[2 * a + b, :, columns] for b in range(2)], 1)
            across = sum(
                lax.dot_general(
                    pair,
                    filters_ref[i],
                    (((1,), (1,)), ((), ())),
                    preferred_element_type=jnp.float32,
                )
                for i in range(2)
            )
            across = jnp.where(inside, across, 0.0)
            if j > 0:
                rows_ref[a, 8 : 8 + FR, HALO * (j - 1) : HALO * j] += across[:, :HALO]
            if j < SPAN // HALO:
                rows_ref[a, 8 : 8 + FR, HALO * j : HALO * (j + 1)] = across[:, HALO:]
    for j in range(SPAN // HALO):
        tile = pl.ds(HALO * j, HALO)
        value = 0.0
        for a, taps in enumerate((LOWPASS, HIGHPASS)):
            for k in range(8):
                value = value + taps[k] * rows_ref[a, k : k + FR + 8, tile]
        mail_ref[:, tile] = value[:8]
        synth_ref[:, tile] = value[8:]
    blank = jnp.zeros((8, 128 - BLK), jnp.float32)
    weights = weight_ref[...].astype(jnp.float32)
    for i in range(2):
        tile = pl.ds(SPAN + HALO * i, HALO)
        mail_ref[:, tile] = jnp.concatenate([weights[8 * i : 8 * i + 8], blank], 1)
    mail_ref[:, NUMBERS:] = jnp.zeros((8, HALO), jnp.float32)
    mail_ref[:3, NUMBERS : NUMBERS + BLK] = numbers_ref[...].astype(jnp.float32)


def prepared(part, numbers, weights, dual, filters):
    return pl.pallas_call(
        prepare,
        out_shape=(
            jax.ShapeDtypeStruct((8, NUMBERS + HALO), jnp.float32),
            jax.ShapeDtypeStruct((FR, SPAN), jnp.float32),
        ),
        in_specs=[SMEM_SPEC] + [VMEM_SPEC] * 4,
        out_specs=(VMEM_SPEC,) * 2,
        scratch_shapes=[pltpu.VMEM((2, FR + 16, SPAN), jnp.float32)],
        compiler_params=pltpu.CompilerParams(vmem_limit_bytes=VMEM_LIMIT),
        name="prepared",
    )(part, numbers, weights, dual, filters)


def hop(block, distance):
    devices = range(lax.axis_size("facet"))
    route = [(i - distance, i) for i in devices if i - distance in devices]
    return lax.ppermute(block, "facet", route)


def gathered_sum(parts):
    mixed = lax.all_to_all(parts, "dp", 0, 0)
    return jnp.sum(mixed.astype(jnp.float32), 0)


def analyze(extra):
    subbands = []
    for row_taps in (LOWPASS, HIGHPASS):
        filtered = sum(row_taps[k] * extra[8 - k : 8 - k + FR] for k in range(8))
        for col_taps in (LOWPASS, HIGHPASS):
            subbands.append(
                sum(col_taps[k] * filtered[:, HALO - k : HALO - k + PART] for k in range(8))
            )
    return jnp.stack(subbands)


def on_device(image, dual, payload, vis_weight, freq_start, tile_slot, live):
    table = jnp.asarray(tables())
    position = lax.axis_index("dp")
    own_rows = image[0]
    filters = jnp.asarray(column_filters())
    payload_below = hop(payload[0], -1)
    numbers = jnp.concatenate([freq_start, tile_slot, jnp.broadcast_to(live, (1, BLK))], 0)
    left = position * PART
    own_dual = lax.dynamic_slice_in_dim(dual[:, 0], left, PART, 2).astype(jnp.float32)
    old = lax.dynamic_slice_in_dim(
        jnp.pad(own_rows, ((0, 0), (HALO, 0))), left, SPAN, 1
    )

    weights = vis_weight[0].T
    spectra, own, order = own_spectra(numbers, weights, payload[0], table, own_rows)
    weights, order = lax.optimization_barrier((weights, order))
    mail, synth = prepared(position[None], numbers, weights, dual[:, 0], filters)
    mail_below = hop(mail, -1)
    numbers_below = mail_below[:3, NUMBERS : NUMBERS + BLK].astype(jnp.int32)
    terms = gradient_parts(
        numbers_below, mail_below, payload_below, spectra, own, table, order
    )
    synth = synth + jnp.pad(mail_below[:, :SPAN], ((FR - 8, 0), (0, 0)))
    total = gathered_sum(terms) + synth
    new = jnp.maximum(old - TAU_STEP * total, 0.0)
    column = lax.broadcasted_iota(jnp.int32, old.shape, 1) + left
    extra = jnp.where(column >= HALO, 2.0 * new - old, 0.0)
    extra_above = hop(extra[FR - 8 :].astype(jnp.bfloat16), 1).astype(jnp.float32)
    extra = jnp.concatenate([extra_above, extra], 0)

    shifted = own_dual + SIGMA_STEP * analyze(extra)
    squares = lax.all_gather((shifted * shifted).astype(jnp.bfloat16), "cube")
    norms = jnp.sqrt(jnp.sum(squares.astype(jnp.float32), 0))
    dual_part = (shifted * (RADIUS / jnp.maximum(norms, RADIUS))).astype(jnp.bfloat16)
    own_part = jnp.concatenate([dual_part, total[None, :, HALO:].astype(jnp.bfloat16)], 0)
    parts = lax.all_to_all(jnp.broadcast_to(own_part, (DP,) + own_part.shape), "dp", 0, 0)
    whole = jnp.concatenate([parts[d] for d in range(DP)], -1)
    dual_next = whole[:4]
    updated = jnp.maximum(own_rows - TAU_STEP * whole[4].astype(jnp.float32), 0.0)
    return (updated[None], dual_next[:, None])


def solution(mesh):
    return jax.shard_map(
        on_device,
        mesh=mesh,
        in_specs=(
            P("cube", "facet", None),
            P(None, "cube", "facet", None),
            P("cube", ("facet", "dp"), None, None),
            P("cube", ("facet", "dp"), None),
            P("cube", ("facet", "dp")),
            P("cube", ("facet", "dp")),
            P("cube", ("facet", "dp")),
        ),
        out_specs=(P("cube", "facet", None), P(None, "cube", "facet", None)),
        check_vma=False,
    )
```

```python
import functools
import math

import jax
import jax.numpy as jnp
import numpy as np
from jax import lax
from jax.experimental import pallas as pl
from jax.experimental.pallas import tpu as pltpu
from jax.sharding import PartitionSpec as P

LOWPASS = (
    0.2303778133088964,
    0.7148465705529155,
    0.6308807679298587,
    -0.027983769416859854,
    -0.18703481171909309,
    0.030841381835560764,
    0.0328830116668852,
    -0.010597401785069032,
)
HIGHPASS = (
    -0.010597401785069032,
    -0.0328830116668852,
    0.030841381835560764,
    0.18703481171909309,
    -0.027983769416859854,
    -0.6308807679298587,
    0.7148465705529155,
    -0.2303778133088964,
)
TAU_STEP = 0.5
SIGMA_STEP = 0.5
RADIUS = 3.0

W = 2560
TILE = 16
FR = 48
BLK = 64
PER = FR // TILE
Q = 20
R = 128
DP = 4
PART = W // DP
HALO = 128
SPAN = PART + HALO
CHUNKS = W // 64
UNROLL = 4
VMEM_LIMIT = 60 * 1024 * 1024
NORM = 1.0 / math.sqrt(W)
C1, C2 = math.cos(2 * math.pi / 5), math.cos(4 * math.pi / 5)
S1, S2 = math.sin(2 * math.pi / 5), math.sin(4 * math.pi / 5)


def tables():
    x = np.arange(W).reshape(R, Q).T
    angles = (x[:, :, None] * np.arange(R)[None, None, :] % W) * (2.0 * math.pi / W)
    table = np.concatenate([np.cos(angles), -np.sin(angles)], -1).astype(jnp.bfloat16)
    return table


def constants():
    return np.concatenate([tables().reshape(Q * R, 2 * R), column_filters().reshape(-1, 2 * HALO)])


def column_filters():
    band = np.zeros((2 * HALO, 2 * HALO), np.float32)
    for b, taps in enumerate((LOWPASS, HIGHPASS)):
        for k in range(8):
            j = np.arange(HALO)
            band[HALO + j - k, HALO * b + j] = taps[k]
    leading = band.astype(jnp.bfloat16)
    rest = (band - leading.astype(np.float32)).astype(jnp.bfloat16)
    return np.stack([leading, rest])


def times_i(value, sign):
    re, im = value
    return (-im, re) if sign > 0 else (im, -re)


def plus(u, v):
    return (u[0] + v[0], u[1] + v[1])


def minus(u, v):
    return (u[0] - v[0], u[1] - v[1])


def dft4(x, sign):
    a, b = plus(x[0], x[2]), minus(x[0], x[2])
    c, d = plus(x[1], x[3]), times_i(minus(x[1], x[3]), sign)
    return [plus(a, c), plus(b, d), minus(a, c), minus(b, d)]


def dft5(x, sign):
    t1, t2 = plus(x[1], x[4]), plus(x[2], x[3])
    t3, t4 = minus(x[1], x[4]), minus(x[2], x[3])
    m1 = tuple(z + C1 * u + C2 * v for z, u, v in zip(x[0], t1, t2))
    m2 = tuple(z + C2 * u + C1 * v for z, u, v in zip(x[0], t1, t2))
    n1 = times_i(tuple(S1 * u + S2 * v for u, v in zip(t3, t4)), sign)
    n2 = times_i(tuple(S2 * u - S1 * v for u, v in zip(t3, t4)), sign)
    return [plus(x[0], plus(t1, t2)), plus(m1, n1), plus(m2, n2), minus(m2, n2), minus(m1, n1)]


def dft20(x, sign):
    columns = [dft4([x[(5 * a + 4 * b) % 20] for a in range(4)], sign) for b in range(5)]
    out = [None] * 20
    for c in range(4):
        line = dft5([columns[b][c] for b in range(5)], sign)
        for e in range(5):
            out[(5 * c + 16 * e) % 20] = line[e]
    return out


def residue_order():
    y = lax.broadcasted_iota(jnp.int32, (PART, 128), 0)
    group = ((y.astype(jnp.float32) + 0.5) * (1.0 / Q)).astype(jnp.int32)
    target = (y - Q * group) * 32 + group
    lane = lax.broadcasted_iota(jnp.int32, (PART, 128), 1)
    tiles = [jnp.where(target == lane + 128 * j, 1.0, 0.0) for j in range(PART // 128)]
    return jnp.concatenate(tiles, 1).astype(jnp.bfloat16)


def add_blocks(base, start, slot, live, weights, payload_ref, spec_ref, grad_ref, list_ref):
    lane = lax.broadcasted_iota(jnp.int32, (1, 128), 1)
    half = lane & 63

    def collect(b, count):
        place = slot(b) - base
        list_ref[count] = b
        return count + jnp.where((place >= 0) & (place < PER), 1, 0)

    count = lax.fori_loop(0, live, collect, 0)
    for u in range(UNROLL):
        list_ref[count + u] = list_ref[0]
    slot_lane = lax.broadcasted_iota(jnp.int32, (1, 128), 1)
    ones = jnp.ones((128, 128), jnp.bfloat16)

    def blocks(step, carry):
        places = [step * UNROLL + u for u in range(UNROLL)]
        numbers = [list_ref[place] for place in places]
        picked = [
            jnp.where(slot_lane == jnp.where(place < count, b, -1), weights, 0.0)
            for place, b in zip(places, numbers)
        ]
        factors = jnp.dot(
            jnp.concatenate(picked, 0).astype(jnp.bfloat16), ones, preferred_element_type=jnp.float32
        )
        found = []
        for u, b in enumerate(numbers):
            chunk, offset = start(b)
            tile = jnp.clip(slot(b) - base, 0, PER - 1)
            rows = pl.ds(pl.multiple_of(tile * TILE, TILE), TILE)
            first = pltpu.roll(spec_ref[chunk, rows, :], (128 - offset) & 127, 1)
            second = pltpu.roll(spec_ref[chunk + 1, rows, :], 64 - offset, 1)
            model = jnp.where(half < 64 - offset, first, second)
            misfit = factors[TILE * u : TILE * (u + 1)] * (
                model - payload_ref[b].astype(jnp.float32)
            )
            lower = jnp.where(half >= offset, pltpu.roll(misfit, offset, 1), 0.0)
            upper = jnp.where(half < offset, pltpu.roll(misfit, 64 + offset, 1), 0.0)
            found.append((chunk, rows, lower, upper))
        for chunk, rows, lower, upper in found:
            grad_ref[chunk, rows, :] += lower
            grad_ref[chunk + 1, rows, :] += upper
        return carry

    lax.fori_loop(0, (count + UNROLL - 1) // UNROLL, blocks, 0)


def columns_back(part, rows, dual_ref, filters, rows_ref):
    for a in range(2):
        for j in range(SPAN // HALO + 1):
            place = (PART // HALO) * part - 1 + j
            inside = (place >= 0) & (place < W // HALO)
            columns = pl.ds(pl.multiple_of(jnp.clip(place, 0, W // HALO - 1) * HALO, HALO), HALO)
            pair = jnp.concatenate([dual_ref[2 * a + b, :rows, columns] for b in range(2)], 1)
            across = sum(
                lax.dot_general(
                    pair,
                    filters(i),
                    (((1,), (1,)), ((), ())),
                    preferred_element_type=jnp.float32,
                )
                for i in range(2)
            )
            across = jnp.where(inside, across, 0.0)
            if j > 0:
                rows_ref[a, 8 : 8 + rows, HALO * (j - 1) : HALO * j] += across[:, :HALO]
            if j < SPAN // HALO:
                rows_ref[a, 8 : 8 + rows, HALO * j : HALO * (j + 1)] = across[:, HALO:]


def rows_back(first, count, tile, rows_ref):
    value = 0.0
    for a, taps in enumerate((LOWPASS, HIGHPASS)):
        for k in range(8):
            value = value + taps[k] * rows_ref[a, 8 + first + k : 8 + first + k + count, tile]
    return value


def write_message(
    part_ref,
    starts_hbm,
    slots_hbm,
    live_hbm,
    weight_hbm,
    payload_hbm,
    dual_hbm,
    filters_hbm,
    out_ref,
    starts_ref,
    slots_ref,
    live_ref,
    weight_ref,
    dual_ref,
    filters_ref,
    rows_ref,
    sems,
):
    pairs = [
        (dual_hbm.at[:, :TILE, :], dual_ref),
        (filters_hbm.at[pl.ds(Q * R, 4 * HALO), :], filters_ref),
        (starts_hbm, starts_ref),
        (slots_hbm, slots_ref),
        (live_hbm, live_ref),
        (weight_hbm, weight_ref),
        (payload_hbm, out_ref.at[pl.ds(0, BLK)]),
    ]
    copies = [pltpu.make_async_copy(s, d, sems.at[i]) for i, (s, d) in enumerate(pairs)]
    for copy in copies:
        copy.start()
    rows_ref[:, :8, :] = jnp.zeros((2, 8, SPAN), jnp.float32)
    copies[0].wait()
    copies[1].wait()
    columns_back(
        part_ref[0],
        TILE,
        dual_ref,
        lambda i: filters_ref[2 * HALO * i : 2 * HALO * (i + 1)],
        rows_ref,
    )
    for i in range(SPAN // HALO // 2):
        pair = [rows_back(-8, 8, pl.ds(HALO * (2 * i + j), HALO), rows_ref) for j in range(2)]
        out_ref[BLK + 1 + i] = jnp.concatenate(pair, 0).astype(jnp.bfloat16)
    for copy in copies[2:6]:
        copy.wait()
    row = lax.broadcasted_iota(jnp.int32, (TILE, BLK), 0)
    starts = starts_ref[...]
    numbers = jnp.where(row == 0, starts >> 6, starts & 63)
    numbers = jnp.where(row == 2, slots_ref[...], numbers)
    numbers = jnp.where(row == 3, live_ref[0, 0], numbers)
    out_ref[BLK] = jnp.concatenate(
        [weight_ref[...].astype(jnp.float32), numbers.astype(jnp.float32)], 1
    ).astype(jnp.bfloat16)
    copies[6].wait()


def synthesis(part_ref, message_ref, dual_ref, constants_ref, synth_ref, rows_ref):
    columns_back(
        part_ref[0],
        FR,
        dual_ref,
        lambda i: constants_ref[Q * R + 2 * HALO * i : Q * R + 2 * HALO * (i + 1)],
        rows_ref,
    )
    rows_ref[:, 8 + FR :, :] = jnp.zeros((2, 8, SPAN), jnp.float32)
    for j in range(SPAN // HALO):
        tile = pl.ds(HALO * j, HALO)
        synth_ref[:, tile] = rows_back(0, FR, tile, rows_ref)
        below = message_ref[BLK + 1 + j // 2].astype(jnp.float32)
        synth_ref[FR - 8 :, tile] += below[8 * (j % 2) : 8 * (j % 2) + 8]


def own_pass(
    starts_hbm,
    slots_hbm,
    live_hbm,
    weight_hbm,
    payload_hbm,
    table_hbm,
    pixels_hbm,
    spec_ref,
    grad_ref,
    starts_ref,
    slots_ref,
    live_ref,
    list_ref,
    weight_ref,
    payload_ref,
    table_ref,
    pixels_ref,
    order_ref,
    re_ref,
    im_ref,
    sems,
):
    pairs = [
        (pixels_hbm, pixels_ref),
        (table_hbm.at[pl.ds(0, Q * R), :], table_ref),
        (weight_hbm, weight_ref),
        (payload_hbm, payload_ref),
        (starts_hbm, starts_ref),
        (slots_hbm, slots_ref),
        (live_hbm, live_ref),
    ]
    copies = [pltpu.make_async_copy(s, d, sems.at[i]) for i, (s, d) in enumerate(pairs)]
    for copy in copies:
        copy.start()
    lane = lax.broadcasted_iota(jnp.int32, (1, 128), 1)
    low = lane < 64
    quarter = lane >> 5

    order_ref[...] = residue_order()
    copies[0].wait()
    stacked = jnp.concatenate(
        [pixels_ref[:, PART * g : PART * (g + 1)].astype(jnp.bfloat16) for g in range(4)], 0
    )
    sorted_rows = jnp.dot(stacked, order_ref[...], preferred_element_type=jnp.float32)
    copies[1].wait()
    for j in range(5):
        tiles = [sorted_rows[FR * g : FR * (g + 1), 128 * j : 128 * (j + 1)] for g in range(4)]
        for p in range(4):
            turned = [
                tiles[g] if g == p else pltpu.roll(tiles[g], (32 * (g - p)) % 128, 1)
                for g in range(4)
            ]
            rows = turned[3]
            for g in range(3):
                rows = jnp.where(quarter == g, turned[g], rows)
            q = 4 * j + p
            partial = jnp.dot(
                rows.astype(jnp.bfloat16),
                table_ref[R * q : R * (q + 1)],
                preferred_element_type=jnp.float32,
            )
            re_ref[q] = partial[:, :R]
            im_ref[q] = partial[:, R:]

    def forward(i, carry):
        rows = pl.ds(pl.multiple_of(i * 8, 8), 8)
        spectrum = dft20([(re_ref[q, rows, :], im_ref[q, rows, :]) for q in range(Q)], -1)
        for k, (re, im) in enumerate(spectrum):
            re, im = re * NORM, im * NORM
            spec_ref[2 * k, rows, :] = jnp.where(low, re, pltpu.roll(im, 64, 1))
            spec_ref[2 * k + 1, rows, :] = jnp.where(low, pltpu.roll(re, 64, 1), im)
        return carry

    lax.fori_loop(0, FR // 8, forward, 0)
    spec_ref[CHUNKS] = spec_ref[0]
    grad_ref[...] = jnp.zeros_like(grad_ref)
    for copy in copies[2:]:
        copy.wait()
    blank = jnp.zeros((TILE, 128 - BLK), jnp.float32)
    weights = jnp.concatenate([weight_ref[...].astype(jnp.float32), blank], 1)
    add_blocks(
        PER,
        lambda b: (starts_ref[0, b] >> 6, starts_ref[0, b] & 63),
        lambda b: slots_ref[0, b],
        live_ref[0, 0],
        weights,
        payload_ref,
        spec_ref,
        grad_ref,
        list_ref,
    )


def below_pass(
    message_ref,
    spec_ref,
    own_ref,
    table_hbm,
    out_ref,
    list_ref,
    numbers_ref,
    vector_ref,
    table_ref,
    order_ref,
    re_ref,
    im_ref,
    grad_ref,
    tile_ref,
    sems,
):
    copy = pltpu.make_async_copy(table_hbm.at[pl.ds(0, Q * R), :], table_ref, sems.at[0])
    copy.start()
    meta = message_ref[BLK].astype(jnp.float32)
    vector_ref[...] = meta[:8].astype(jnp.int32)
    read = pltpu.make_async_copy(vector_ref, numbers_ref, sems.at[1])
    read.start()
    lane = lax.broadcasted_iota(jnp.int32, (1, 128), 1)
    low = lane < 64
    quarter = lane >> 5
    grad_ref[...] = own_ref[...]
    order_ref[...] = residue_order()
    read.wait()
    add_blocks(
        0,
        lambda b: (numbers_ref[0, BLK + b], numbers_ref[1, BLK + b]),
        lambda b: numbers_ref[2, BLK + b],
        numbers_ref[3, BLK],
        jnp.where(low, meta, 0.0),
        message_ref,
        spec_ref,
        grad_ref,
        list_ref,
    )
    grad_ref[0] += grad_ref[CHUNKS]

    def backward(i, carry):
        rows = pl.ds(pl.multiple_of(i * 8, 8), 8)
        spectrum = []
        for k in range(Q):
            even, odd = grad_ref[2 * k, rows, :], grad_ref[2 * k + 1, rows, :]
            spectrum.append(
                (
                    jnp.where(low, even, pltpu.roll(odd, 64, 1)),
                    jnp.where(low, pltpu.roll(even, 64, 1), odd),
                )
            )
        for q, (re, im) in enumerate(dft20(spectrum, 1)):
            re_ref[q, rows, :] = re * NORM
            im_ref[q, rows, :] = im * NORM
        return carry

    lax.fori_loop(0, FR // 8, backward, 0)
    copy.wait()
    for j in range(5):
        places = [[] for _ in range(4)]
        for p in range(4):
            q = 4 * j + p
            pair = jnp.concatenate([re_ref[q], im_ref[q]], 1).astype(jnp.bfloat16)
            rows = lax.dot_general(
                pair,
                table_ref[R * q : R * (q + 1)],
                (((1,), (1,)), ((), ())),
                preferred_element_type=jnp.float32,
            )
            for g in range(4):
                places[g].append(rows if g == p else pltpu.roll(rows, (32 * (p - g)) % 128, 1))
        for g in range(4):
            tile = places[g][3]
            for p in range(3):
                tile = jnp.where(quarter == p, places[g][p], tile)
            tile_ref[5 * g + j] = tile
    mixed = jnp.concatenate(
        [jnp.concatenate([tile_ref[5 * g + j] for j in range(5)], 1) for g in range(4)], 0
    ).astype(jnp.bfloat16)
    natural = lax.dot_general(
        mixed, order_ref[...], (((1,), (1,)), ((), ())), preferred_element_type=jnp.float32
    ).astype(jnp.bfloat16)
    out_ref[0, :, :HALO] = jnp.zeros((FR, HALO), jnp.bfloat16)
    for g in range(4):
        rows = natural[FR * g : FR * (g + 1)]
        out_ref[g, :, HALO:] = rows
        if g < 3:
            out_ref[g + 1, :, :HALO] = rows[:, PART - HALO :]


HBM_SPEC = pl.BlockSpec(memory_space=pltpu.HBM)
SMEM_SPEC = pl.BlockSpec(memory_space=pltpu.SMEM)
VMEM_SPEC = pl.BlockSpec(memory_space=pltpu.VMEM)
SPECTRA = jax.ShapeDtypeStruct((CHUNKS + 1, FR, 128), jnp.float32)


TABLE = pltpu.VMEM((Q * R, 2 * R), jnp.bfloat16)
PARAMS = pltpu.CompilerParams(vmem_limit_bytes=VMEM_LIMIT)
COST = pl.CostEstimate(flops=2 * 10**9, bytes_accessed=4 * 10**6, transcendentals=0)


def message(part, starts, slots, live, weights, payload, dual, table):
    return pl.pallas_call(
        write_message,
        out_shape=jax.ShapeDtypeStruct((BLK + 1 + SPAN // HALO // 2, TILE, 128), jnp.bfloat16),
        in_specs=[SMEM_SPEC] + [HBM_SPEC] * 7,
        out_specs=VMEM_SPEC,
        scratch_shapes=[
            pltpu.VMEM((1, BLK), jnp.int32),
            pltpu.VMEM((1, BLK), jnp.int32),
            pltpu.SMEM((1, 1), jnp.int32),
            pltpu.VMEM((TILE, BLK), jnp.bfloat16),
            pltpu.VMEM((4, TILE, W), jnp.bfloat16),
            pltpu.VMEM((4 * HALO, 2 * HALO), jnp.bfloat16),
            pltpu.VMEM((2, 8 + TILE, SPAN), jnp.float32),
            pltpu.SemaphoreType.DMA((7,)),
        ],
        compiler_params=PARAMS,
        name="message",
    )(part, starts, slots, live, weights, payload, dual, table)


def synthesized(part, received, dual, table):
    return pl.pallas_call(
        synthesis,
        out_shape=jax.ShapeDtypeStruct((FR, SPAN), jnp.float32),
        in_specs=[SMEM_SPEC] + [VMEM_SPEC] * 3,
        out_specs=VMEM_SPEC,
        scratch_shapes=[pltpu.VMEM((2, FR + 16, SPAN), jnp.float32)],
        compiler_params=pltpu.CompilerParams(vmem_limit_bytes=16 * 1024 * 1024),
        name="synthesized",
    )(part, received, dual, table)


def own_spectra(starts, slots, live, weights, payload, table, pixels):
    return pl.pallas_call(
        own_pass,
        out_shape=(SPECTRA, SPECTRA),
        in_specs=[HBM_SPEC] * 7,
        out_specs=(VMEM_SPEC,) * 2,
        scratch_shapes=[
            pltpu.SMEM((1, BLK), jnp.int32),
            pltpu.SMEM((1, BLK), jnp.int32),
            pltpu.SMEM((1, 1), jnp.int32),
            pltpu.SMEM((BLK + UNROLL,), jnp.int32),
            pltpu.VMEM((TILE, BLK), jnp.bfloat16),
            pltpu.VMEM((BLK, TILE, 128), jnp.bfloat16),
            TABLE,
            pltpu.VMEM((FR, W), jnp.float32),
            pltpu.VMEM((PART, PART), jnp.bfloat16),
            pltpu.VMEM((Q, FR, R), jnp.float32),
            pltpu.VMEM((Q, FR, R), jnp.float32),
            pltpu.SemaphoreType.DMA((7,)),
        ],
        compiler_params=PARAMS,
        cost_estimate=COST,
        name="own_spectra",
    )(starts, slots, live, weights, payload, table, pixels)


def gradient_parts(received, spectra, own, table):
    return pl.pallas_call(
        below_pass,
        out_shape=jax.ShapeDtypeStruct((DP, FR, SPAN), jnp.bfloat16),
        in_specs=[VMEM_SPEC] * 3 + [HBM_SPEC],
        out_specs=VMEM_SPEC,
        scratch_shapes=[
            pltpu.SMEM((BLK + UNROLL,), jnp.int32),
            pltpu.SMEM((8, 128), jnp.int32),
            pltpu.VMEM((8, 128), jnp.int32),
            TABLE,
            pltpu.VMEM((PART, PART), jnp.bfloat16),
            pltpu.VMEM((Q, FR, R), jnp.float32),
            pltpu.VMEM((Q, FR, R), jnp.float32),
            pltpu.VMEM((CHUNKS + 1, FR, 128), jnp.float32),
            pltpu.VMEM((Q, FR, R), jnp.float32),
            pltpu.SemaphoreType.DMA((2,)),
        ],
        compiler_params=PARAMS,
        cost_estimate=COST,
        name="gradient_parts",
    )(received, spectra, own, table)


def hop(block, distance):
    devices = range(lax.axis_size("facet"))
    route = [(i - distance, i) for i in devices if i - distance in devices]
    return lax.ppermute(block, "facet", route)


def gathered_sum(parts):
    mixed = lax.all_to_all(parts, "dp", 0, 0)
    return jnp.sum(mixed.astype(jnp.float32), 0)


def analyze(extra):
    subbands = []
    for row_taps in (LOWPASS, HIGHPASS):
        filtered = sum(row_taps[k] * extra[8 - k : 8 - k + FR] for k in range(8))
        for col_taps in (LOWPASS, HIGHPASS):
            subbands.append(
                sum(col_taps[k] * filtered[:, HALO - k : HALO - k + PART] for k in range(8))
            )
    return jnp.stack(subbands)


def on_device(image, dual, payload, vis_weight, freq_start, tile_slot, live):
    table = jnp.asarray(constants())
    position = lax.axis_index("dp")
    own_rows = image[0]
    part = position[None]
    weights = vis_weight[0].T
    received = hop(
        message(part, freq_start, tile_slot, live, weights, payload[0], dual[:, 0], table), -1
    )

    left = position * PART
    own_dual = lax.dynamic_slice_in_dim(dual[:, 0], left, PART, 2).astype(jnp.float32)
    old = lax.dynamic_slice_in_dim(
        jnp.pad(own_rows, ((0, 0), (HALO, 0))), left, SPAN, 1
    )

    spectra, own = own_spectra(
        freq_start, tile_slot, live, weights, payload[0], table, own_rows
    )
    terms = gradient_parts(received, spectra, own, table)
    terms, received = lax.optimization_barrier((terms, received))
    synth = synthesized(part, received, dual[:, 0], table)
    total = gathered_sum(terms) + synth
    new = jnp.maximum(old - TAU_STEP * total, 0.0)
    column = lax.broadcasted_iota(jnp.int32, old.shape, 1) + left
    extra = jnp.where(column >= HALO, 2.0 * new - old, 0.0)
    extra_above = hop(extra[FR - 8 :].astype(jnp.bfloat16), 1).astype(jnp.float32)
    extra = jnp.concatenate([extra_above, extra], 0)

    shifted = own_dual + SIGMA_STEP * analyze(extra)
    squares = lax.all_gather((shifted * shifted).astype(jnp.bfloat16), "cube")
    norms = jnp.sqrt(jnp.sum(squares.astype(jnp.float32), 0))
    dual_part = (shifted * (RADIUS / jnp.maximum(norms, RADIUS))).astype(jnp.bfloat16)
    own_part = jnp.concatenate([dual_part, total[None, :, HALO:].astype(jnp.bfloat16)], 0)
    parts = lax.all_to_all(jnp.broadcast_to(own_part, (DP,) + own_part.shape), "dp", 0, 0)
    whole = jnp.concatenate([parts[d] for d in range(DP)], -1)
    dual_next = whole[:4]
    updated = jnp.maximum(own_rows - TAU_STEP * whole[4].astype(jnp.float32), 0.0)
    return (updated[None], dual_next[:, None])


def solution(mesh):
    return jax.shard_map(
        on_device,
        mesh=mesh,
        in_specs=(
            P("cube", "facet", None),
            P(None, "cube", "facet", None),
            P("cube", ("facet", "dp"), None, None),
            P("cube", ("facet", "dp"), None),
            P("cube", ("facet", "dp")),
            P("cube", ("facet", "dp")),
            P("cube", ("facet", "dp")),
        ),
        out_specs=(P("cube", "facet", None), P(None, "cube", "facet", None)),
        check_vma=False,
    )
```

```python
import functools
import math

import jax
import jax.numpy as jnp
import numpy as np
from jax import lax
from jax.experimental import pallas as pl
from jax.experimental.pallas import tpu as pltpu
from jax.sharding import PartitionSpec as P

LOWPASS = (
    0.2303778133088964,
    0.7148465705529155,
    0.6308807679298587,
    -0.027983769416859854,
    -0.18703481171909309,
    0.030841381835560764,
    0.0328830116668852,
    -0.010597401785069032,
)
HIGHPASS = (
    -0.010597401785069032,
    -0.0328830116668852,
    0.030841381835560764,
    0.18703481171909309,
    -0.027983769416859854,
    -0.6308807679298587,
    0.7148465705529155,
    -0.2303778133088964,
)
TAU_STEP = 0.5
SIGMA_STEP = 0.5
RADIUS = 3.0

W = 2560
TILE = 16
FR = 48
BLK = 64
PER = FR // TILE
Q = 20
R = 128
DP = 4
PART = W // DP
HALO = 128
SPAN = PART + HALO
CHUNKS = W // 64
UNROLL = 4
VMEM_LIMIT = 60 * 1024 * 1024
NORM = 1.0 / math.sqrt(W)
C1, C2 = math.cos(2 * math.pi / 5), math.cos(4 * math.pi / 5)
S1, S2 = math.sin(2 * math.pi / 5), math.sin(4 * math.pi / 5)


def tables():
    x = np.arange(W).reshape(R, Q).T
    angles = (x[:, :, None] * np.arange(R)[None, None, :] % W) * (2.0 * math.pi / W)
    table = np.concatenate([np.cos(angles), -np.sin(angles)], -1).astype(jnp.bfloat16)
    return table


def constants():
    return np.concatenate([tables().reshape(Q * R, 2 * R), column_filters().reshape(-1, 2 * HALO)])


def column_filters():
    band = np.zeros((2 * HALO, 2 * HALO), np.float32)
    for b, taps in enumerate((LOWPASS, HIGHPASS)):
        for k in range(8):
            j = np.arange(HALO)
            band[HALO + j - k, HALO * b + j] = taps[k]
    leading = band.astype(jnp.bfloat16)
    rest = (band - leading.astype(np.float32)).astype(jnp.bfloat16)
    return np.stack([leading, rest])


def times_i(value, sign):
    re, im = value
    return (-im, re) if sign > 0 else (im, -re)


def plus(u, v):
    return (u[0] + v[0], u[1] + v[1])


def minus(u, v):
    return (u[0] - v[0], u[1] - v[1])


def dft4(x, sign):
    a, b = plus(x[0], x[2]), minus(x[0], x[2])
    c, d = plus(x[1], x[3]), times_i(minus(x[1], x[3]), sign)
    return [plus(a, c), plus(b, d), minus(a, c), minus(b, d)]


def dft5(x, sign):
    t1, t2 = plus(x[1], x[4]), plus(x[2], x[3])
    t3, t4 = minus(x[1], x[4]), minus(x[2], x[3])
    m1 = tuple(z + C1 * u + C2 * v for z, u, v in zip(x[0], t1, t2))
    m2 = tuple(z + C2 * u + C1 * v for z, u, v in zip(x[0], t1, t2))
    n1 = times_i(tuple(S1 * u + S2 * v for u, v in zip(t3, t4)), sign)
    n2 = times_i(tuple(S2 * u - S1 * v for u, v in zip(t3, t4)), sign)
    return [plus(x[0], plus(t1, t2)), plus(m1, n1), plus(m2, n2), minus(m2, n2), minus(m1, n1)]


def dft20(x, sign):
    columns = [dft4([x[(5 * a + 4 * b) % 20] for a in range(4)], sign) for b in range(5)]
    out = [None] * 20
    for c in range(4):
        line = dft5([columns[b][c] for b in range(5)], sign)
        for e in range(5):
            out[(5 * c + 16 * e) % 20] = line[e]
    return out


def residue_order():
    y = lax.broadcasted_iota(jnp.int32, (PART, 128), 0)
    group = ((y.astype(jnp.float32) + 0.5) * (1.0 / Q)).astype(jnp.int32)
    target = (y - Q * group) * 32 + group
    lane = lax.broadcasted_iota(jnp.int32, (PART, 128), 1)
    tiles = [jnp.where(target == lane + 128 * j, 1.0, 0.0) for j in range(PART // 128)]
    return jnp.concatenate(tiles, 1).astype(jnp.bfloat16)


def add_blocks(base, start, slot, live, weights, payload_ref, spec_ref, grad_ref, list_ref):
    lane = lax.broadcasted_iota(jnp.int32, (1, 128), 1)
    half = lane & 63

    def collect(b, count):
        place = slot(b) - base
        list_ref[count] = b
        return count + jnp.where((place >= 0) & (place < PER), 1, 0)

    count = lax.fori_loop(0, live, collect, 0)
    for u in range(UNROLL):
        list_ref[count + u] = list_ref[0]
    slot_lane = lax.broadcasted_iota(jnp.int32, (1, 128), 1)
    ones = jnp.ones((128, 128), jnp.bfloat16)

    def blocks(step, carry):
        places = [step * UNROLL + u for u in range(UNROLL)]
        numbers = [list_ref[place] for place in places]
        picked = [
            jnp.where(slot_lane == jnp.where(place < count, b, -1), weights, 0.0)
            for place, b in zip(places, numbers)
        ]
        factors = jnp.dot(
            jnp.concatenate(picked, 0).astype(jnp.bfloat16), ones, preferred_element_type=jnp.float32
        )
        found = []
        for u, b in enumerate(numbers):
            chunk, offset = start(b)
            tile = jnp.clip(slot(b) - base, 0, PER - 1)
            rows = pl.ds(pl.multiple_of(tile * TILE, TILE), TILE)
            first = pltpu.roll(spec_ref[chunk, rows, :], (128 - offset) & 127, 1)
            second = pltpu.roll(spec_ref[chunk + 1, rows, :], 64 - offset, 1)
            model = jnp.where(half < 64 - offset, first, second)
            misfit = factors[TILE * u : TILE * (u + 1)] * (
                model - payload_ref[b].astype(jnp.float32)
            )
            lower = jnp.where(half >= offset, pltpu.roll(misfit, offset, 1), 0.0)
            upper = jnp.where(half < offset, pltpu.roll(misfit, 64 + offset, 1), 0.0)
            found.append((chunk, rows, lower, upper))
        for chunk, rows, lower, upper in found:
            grad_ref[chunk, rows, :] += lower
            grad_ref[chunk + 1, rows, :] += upper
        return carry

    lax.fori_loop(0, (count + UNROLL - 1) // UNROLL, blocks, 0)


def columns_back(part, rows, dual_ref, filters, rows_ref):
    tiles = SPAN // HALO + 1
    blocks = []
    for j in range(tiles):
        place = (PART // HALO) * part - 1 + j
        inside = (place >= 0) & (place < W // HALO)
        columns = pl.ds(pl.multiple_of(jnp.clip(place, 0, W // HALO - 1) * HALO, HALO), HALO)
        for a in range(2):
            pair = jnp.concatenate([dual_ref[2 * a + b, :rows, columns] for b in range(2)], 1)
            blocks.append(jnp.where(inside, pair, jnp.zeros_like(pair)))
    stacked = jnp.concatenate(blocks, 0)
    across = sum(
        lax.dot_general(
            stacked, filters(i), (((1,), (1,)), ((), ())), preferred_element_type=jnp.float32
        )
        for i in range(2)
    )
    for j in range(tiles - 1):
        for a in range(2):
            here, right = [across[rows * (2 * i + a) : rows * (2 * i + a + 1)] for i in (j, j + 1)]
            rows_ref[a, 8 : 8 + rows, HALO * j : HALO * (j + 1)] = (
                here[:, HALO:] + right[:, :HALO]
            )


def rows_back(first, count, tile, rows_ref):
    value = 0.0
    for a, taps in enumerate((LOWPASS, HIGHPASS)):
        for k in range(8):
            value = value + taps[k] * rows_ref[a, 8 + first + k : 8 + first + k + count, tile]
    return value


def write_message(
    part_ref,
    starts_hbm,
    slots_hbm,
    live_hbm,
    weight_hbm,
    dual_hbm,
    filters_hbm,
    out_ref,
    starts_ref,
    slots_ref,
    live_ref,
    weight_ref,
    dual_ref,
    filters_ref,
    rows_ref,
    sems,
):
    pairs = [
        (dual_hbm.at[:, :TILE, :], dual_ref),
        (filters_hbm.at[pl.ds(Q * R, 4 * HALO), :], filters_ref),
        (starts_hbm, starts_ref),
        (slots_hbm, slots_ref),
        (live_hbm, live_ref),
        (weight_hbm, weight_ref),
    ]
    copies = [pltpu.make_async_copy(s, d, sems.at[i]) for i, (s, d) in enumerate(pairs)]
    for copy in copies:
        copy.start()
    rows_ref[:, :8, :] = jnp.zeros((2, 8, SPAN), jnp.float32)
    copies[0].wait()
    copies[1].wait()
    columns_back(
        part_ref[0],
        TILE,
        dual_ref,
        lambda i: filters_ref[2 * HALO * i : 2 * HALO * (i + 1)],
        rows_ref,
    )
    for i in range(SPAN // HALO // 2):
        pair = [rows_back(-8, 8, pl.ds(HALO * (2 * i + j), HALO), rows_ref) for j in range(2)]
        out_ref[1 + i] = jnp.concatenate(pair, 0).astype(jnp.bfloat16)
    for copy in copies[2:]:
        copy.wait()
    row = lax.broadcasted_iota(jnp.int32, (TILE, BLK), 0)
    starts = starts_ref[...]
    numbers = jnp.where(row == 0, starts >> 6, starts & 63)
    numbers = jnp.where(row == 2, slots_ref[...], numbers)
    numbers = jnp.where(row == 3, live_ref[0, 0], numbers)
    out_ref[0] = jnp.concatenate(
        [weight_ref[...].astype(jnp.float32), numbers.astype(jnp.float32)], 1
    ).astype(jnp.bfloat16)


def synthesis(part_ref, message_ref, dual_ref, constants_ref, synth_ref, rows_ref):
    columns_back(
        part_ref[0],
        FR,
        dual_ref,
        lambda i: constants_ref[Q * R + 2 * HALO * i : Q * R + 2 * HALO * (i + 1)],
        rows_ref,
    )
    rows_ref[:, 8 + FR :, :] = jnp.zeros((2, 8, SPAN), jnp.float32)
    for j in range(SPAN // HALO):
        tile = pl.ds(HALO * j, HALO)
        synth_ref[:, tile] = rows_back(0, FR, tile, rows_ref)
        below = message_ref[1 + j // 2].astype(jnp.float32)
        synth_ref[FR - 8 :, tile] += below[8 * (j % 2) : 8 * (j % 2) + 8]


def own_pass(
    starts_hbm,
    slots_hbm,
    live_hbm,
    weight_hbm,
    payload_hbm,
    table_hbm,
    pixels_hbm,
    spec_ref,
    grad_ref,
    starts_ref,
    slots_ref,
    live_ref,
    list_ref,
    weight_ref,
    payload_ref,
    table_ref,
    pixels_ref,
    order_ref,
    re_ref,
    im_ref,
    sems,
):
    pairs = [
        (pixels_hbm, pixels_ref),
        (table_hbm.at[pl.ds(0, Q * R), :], table_ref),
        (weight_hbm, weight_ref),
        (payload_hbm, payload_ref),
        (starts_hbm, starts_ref),
        (slots_hbm, slots_ref),
        (live_hbm, live_ref),
    ]
    copies = [pltpu.make_async_copy(s, d, sems.at[i]) for i, (s, d) in enumerate(pairs)]
    for copy in copies:
        copy.start()
    lane = lax.broadcasted_iota(jnp.int32, (1, 128), 1)
    low = lane < 64
    quarter = lane >> 5

    order_ref[...] = residue_order()
    copies[0].wait()
    stacked = jnp.concatenate(
        [pixels_ref[:, PART * g : PART * (g + 1)].astype(jnp.bfloat16) for g in range(4)], 0
    )
    sorted_rows = jnp.dot(stacked, order_ref[...], preferred_element_type=jnp.float32)
    copies[1].wait()
    for j in range(5):
        tiles = [sorted_rows[FR * g : FR * (g + 1), 128 * j : 128 * (j + 1)] for g in range(4)]
        for p in range(4):
            turned = [
                tiles[g] if g == p else pltpu.roll(tiles[g], (32 * (g - p)) % 128, 1)
                for g in range(4)
            ]
            rows = turned[3]
            for g in range(3):
                rows = jnp.where(quarter == g, turned[g], rows)
            q = 4 * j + p
            partial = jnp.dot(
                rows.astype(jnp.bfloat16),
                table_ref[R * q : R * (q + 1)],
                preferred_element_type=jnp.float32,
            )
            re_ref[q] = partial[:, :R]
            im_ref[q] = partial[:, R:]

    def forward(i, carry):
        rows = pl.ds(pl.multiple_of(i * 8, 8), 8)
        spectrum = dft20([(re_ref[q, rows, :], im_ref[q, rows, :]) for q in range(Q)], -1)
        for k, (re, im) in enumerate(spectrum):
            re, im = re * NORM, im * NORM
            spec_ref[2 * k, rows, :] = jnp.where(low, re, pltpu.roll(im, 64, 1))
            spec_ref[2 * k + 1, rows, :] = jnp.where(low, pltpu.roll(re, 64, 1), im)
        return carry

    lax.fori_loop(0, FR // 8, forward, 0)
    spec_ref[CHUNKS] = spec_ref[0]
    grad_ref[...] = jnp.zeros_like(grad_ref)
    for copy in copies[2:]:
        copy.wait()
    blank = jnp.zeros((TILE, 128 - BLK), jnp.float32)
    weights = jnp.concatenate([weight_ref[...].astype(jnp.float32), blank], 1)
    add_blocks(
        PER,
        lambda b: (starts_ref[0, b] >> 6, starts_ref[0, b] & 63),
        lambda b: slots_ref[0, b],
        live_ref[0, 0],
        weights,
        payload_ref,
        spec_ref,
        grad_ref,
        list_ref,
    )


def below_pass(
    message_hbm,
    payload_hbm,
    spec_hbm,
    own_hbm,
    table_hbm,
    out_ref,
    list_ref,
    numbers_ref,
    vector_ref,
    message_ref,
    payload_ref,
    spec_ref,
    grad_ref,
    table_ref,
    order_ref,
    re_ref,
    im_ref,
    tile_ref,
    sems,
):
    pairs = [
        (message_hbm.at[0], message_ref),
        (spec_hbm, spec_ref),
        (own_hbm, grad_ref),
        (payload_hbm, payload_ref),
        (table_hbm.at[pl.ds(0, Q * R), :], table_ref),
    ]
    copies = [pltpu.make_async_copy(s, d, sems.at[i]) for i, (s, d) in enumerate(pairs)]
    for copy in copies:
        copy.start()
    lane = lax.broadcasted_iota(jnp.int32, (1, 128), 1)
    low = lane < 64
    quarter = lane >> 5
    copies[0].wait()
    meta = message_ref[...].astype(jnp.float32)
    vector_ref[...] = meta[:8].astype(jnp.int32)
    read = pltpu.make_async_copy(vector_ref, numbers_ref, sems.at[5])
    read.start()
    order_ref[...] = residue_order()
    read.wait()
    for copy in copies[1:4]:
        copy.wait()
    add_blocks(
        0,
        lambda b: (numbers_ref[0, BLK + b], numbers_ref[1, BLK + b]),
        lambda b: numbers_ref[2, BLK + b],
        numbers_ref[3, BLK],
        jnp.where(low, meta, 0.0),
        payload_ref,
        spec_ref,
        grad_ref,
        list_ref,
    )
    grad_ref[0] += grad_ref[CHUNKS]

    def backward(i, carry):
        rows = pl.ds(pl.multiple_of(i * 8, 8), 8)
        spectrum = []
        for k in range(Q):
            even, odd = grad_ref[2 * k, rows, :], grad_ref[2 * k + 1, rows, :]
            spectrum.append(
                (
                    jnp.where(low, even, pltpu.roll(odd, 64, 1)),
                    jnp.where(low, pltpu.roll(even, 64, 1), odd),
                )
            )
        for q, (re, im) in enumerate(dft20(spectrum, 1)):
            re_ref[q, rows, :] = re * NORM
            im_ref[q, rows, :] = im * NORM
        return carry

    lax.fori_loop(0, FR // 8, backward, 0)
    copies[4].wait()
    for j in range(5):
        places = [[] for _ in range(4)]
        for p in range(4):
            q = 4 * j + p
            pair = jnp.concatenate([re_ref[q], im_ref[q]], 1).astype(jnp.bfloat16)
            rows = lax.dot_general(
                pair,
                table_ref[R * q : R * (q + 1)],
                (((1,), (1,)), ((), ())),
                preferred_element_type=jnp.float32,
            )
            for g in range(4):
                places[g].append(rows if g == p else pltpu.roll(rows, (32 * (p - g)) % 128, 1))
        for g in range(4):
            tile = places[g][3]
            for p in range(3):
                tile = jnp.where(quarter == p, places[g][p], tile)
            tile_ref[5 * g + j] = tile
    mixed = jnp.concatenate(
        [jnp.concatenate([tile_ref[5 * g + j] for j in range(5)], 1) for g in range(4)], 0
    ).astype(jnp.bfloat16)
    natural = lax.dot_general(
        mixed, order_ref[...], (((1,), (1,)), ((), ())), preferred_element_type=jnp.float32
    ).astype(jnp.bfloat16)
    out_ref[0, :, :HALO] = jnp.zeros((FR, HALO), jnp.bfloat16)
    for g in range(4):
        rows = natural[FR * g : FR * (g + 1)]
        out_ref[g, :, HALO:] = rows
        if g < 3:
            out_ref[g + 1, :, :HALO] = rows[:, PART - HALO :]


HBM_SPEC = pl.BlockSpec(memory_space=pltpu.HBM)
SMEM_SPEC = pl.BlockSpec(memory_space=pltpu.SMEM)
VMEM_SPEC = pl.BlockSpec(memory_space=pltpu.VMEM)
SPECTRA = jax.ShapeDtypeStruct((CHUNKS + 1, FR, 128), jnp.float32)


TABLE = pltpu.VMEM((Q * R, 2 * R), jnp.bfloat16)
PARAMS = pltpu.CompilerParams(vmem_limit_bytes=VMEM_LIMIT)
COST = pl.CostEstimate(flops=2 * 10**9, bytes_accessed=4 * 10**6, transcendentals=0)


def message(part, starts, slots, live, weights, dual, table):
    return pl.pallas_call(
        write_message,
        out_shape=jax.ShapeDtypeStruct((1 + SPAN // HALO // 2, TILE, 128), jnp.bfloat16),
        in_specs=[SMEM_SPEC] + [HBM_SPEC] * 6,
        out_specs=VMEM_SPEC,
        scratch_shapes=[
            pltpu.VMEM((1, BLK), jnp.int32),
            pltpu.VMEM((1, BLK), jnp.int32),
            pltpu.SMEM((1, 1), jnp.int32),
            pltpu.VMEM((TILE, BLK), jnp.bfloat16),
            pltpu.VMEM((4, TILE, W), jnp.bfloat16),
            pltpu.VMEM((4 * HALO, 2 * HALO), jnp.bfloat16),
            pltpu.VMEM((2, 8 + TILE, SPAN), jnp.float32),
            pltpu.SemaphoreType.DMA((6,)),
        ],
        compiler_params=PARAMS,
        name="message",
    )(part, starts, slots, live, weights, dual, table)


def synthesized(part, received, dual, table):
    return pl.pallas_call(
        synthesis,
        out_shape=jax.ShapeDtypeStruct((FR, SPAN), jnp.float32),
        in_specs=[SMEM_SPEC] + [VMEM_SPEC] * 3,
        out_specs=VMEM_SPEC,
        scratch_shapes=[pltpu.VMEM((2, FR + 16, SPAN), jnp.float32)],
        compiler_params=pltpu.CompilerParams(vmem_limit_bytes=16 * 1024 * 1024),
        name="synthesized",
    )(part, received, dual, table)


def own_spectra(starts, slots, live, weights, payload, table, pixels):
    return pl.pallas_call(
        own_pass,
        out_shape=(SPECTRA, SPECTRA),
        in_specs=[HBM_SPEC] * 7,
        out_specs=(VMEM_SPEC,) * 2,
        scratch_shapes=[
            pltpu.SMEM((1, BLK), jnp.int32),
            pltpu.SMEM((1, BLK), jnp.int32),
            pltpu.SMEM((1, 1), jnp.int32),
            pltpu.SMEM((BLK + UNROLL,), jnp.int32),
            pltpu.VMEM((TILE, BLK), jnp.bfloat16),
            pltpu.VMEM((BLK, TILE, 128), jnp.bfloat16),
            TABLE,
            pltpu.VMEM((FR, W), jnp.float32),
            pltpu.VMEM((PART, PART), jnp.bfloat16),
            pltpu.VMEM((Q, FR, R), jnp.float32),
            pltpu.VMEM((Q, FR, R), jnp.float32),
            pltpu.SemaphoreType.DMA((7,)),
        ],
        compiler_params=PARAMS,
        cost_estimate=COST,
        name="own_spectra",
    )(starts, slots, live, weights, payload, table, pixels)


def gradient_parts(received, payload, spectra, own, table):
    return pl.pallas_call(
        below_pass,
        out_shape=jax.ShapeDtypeStruct((DP, FR, SPAN), jnp.bfloat16),
        in_specs=[HBM_SPEC] * 5,
        out_specs=VMEM_SPEC,
        scratch_shapes=[
            pltpu.SMEM((BLK + UNROLL,), jnp.int32),
            pltpu.SMEM((8, 128), jnp.int32),
            pltpu.VMEM((8, 128), jnp.int32),
            pltpu.VMEM((TILE, 128), jnp.bfloat16),
            pltpu.VMEM((BLK, TILE, 128), jnp.bfloat16),
            pltpu.VMEM((CHUNKS + 1, FR, 128), jnp.float32),
            pltpu.VMEM((CHUNKS + 1, FR, 128), jnp.float32),
            TABLE,
            pltpu.VMEM((PART, PART), jnp.bfloat16),
            pltpu.VMEM((Q, FR, R), jnp.float32),
            pltpu.VMEM((Q, FR, R), jnp.float32),
            pltpu.VMEM((Q, FR, R), jnp.float32),
            pltpu.SemaphoreType.DMA((6,)),
        ],
        compiler_params=PARAMS,
        cost_estimate=COST,
        name="gradient_parts",
    )(received, payload, spectra, own, table)


def finish(parts_ref, pixels_ref, image_hbm, dual_hbm, image_ref, sems):
    copies = []
    for d in range(DP):
        tile = pl.ds(PART * d, PART)
        copies.append(
            pltpu.make_async_copy(
                parts_ref.at[d, pl.ds(0, 4)], dual_hbm.at[:, :, tile], sems.at[d]
            )
        )
        copies[-1].start()
    for d in range(DP):
        tile = pl.ds(PART * d, PART)
        descent = parts_ref[d, 4].astype(jnp.float32)
        image_ref[:, tile] = jnp.maximum(pixels_ref[:, tile] - TAU_STEP * descent, 0.0)
    copies.append(pltpu.make_async_copy(image_ref, image_hbm, sems.at[DP]))
    copies[-1].start()
    for copy in copies:
        copy.wait()


def finished(parts, pixels):
    return pl.pallas_call(
        finish,
        out_shape=(
            jax.ShapeDtypeStruct((FR, W), jnp.float32),
            jax.ShapeDtypeStruct((4, FR, W), jnp.bfloat16),
        ),
        in_specs=[VMEM_SPEC] * 2,
        out_specs=(HBM_SPEC,) * 2,
        scratch_shapes=[pltpu.VMEM((FR, W), jnp.float32), pltpu.SemaphoreType.DMA((DP + 1,))],
        compiler_params=pltpu.CompilerParams(vmem_limit_bytes=16 * 1024 * 1024),
        name="finished",
    )(parts, pixels)


def hop(block, distance):
    devices = range(lax.axis_size("facet"))
    route = [(i - distance, i) for i in devices if i - distance in devices]
    return lax.ppermute(block, "facet", route)


def gathered_sum(parts):
    mixed = lax.all_to_all(parts, "dp", 0, 0)
    return jnp.sum(mixed.astype(jnp.float32), 0)


def analyze(extra):
    subbands = []
    for row_taps in (LOWPASS, HIGHPASS):
        filtered = sum(row_taps[k] * extra[8 - k : 8 - k + FR] for k in range(8))
        for col_taps in (LOWPASS, HIGHPASS):
            subbands.append(
                sum(col_taps[k] * filtered[:, HALO - k : HALO - k + PART] for k in range(8))
            )
    return jnp.stack(subbands)


def on_device(image, dual, payload, vis_weight, freq_start, tile_slot, live):
    table = jnp.asarray(constants())
    position = lax.axis_index("dp")
    own_rows = image[0]
    part = position[None]
    weights = vis_weight[0].T
    payload_below = hop(payload[0], -1)
    received = hop(
        message(part, freq_start, tile_slot, live, weights, dual[:, 0], table), -1
    )

    left = position * PART
    own_dual = lax.dynamic_slice_in_dim(dual[:, 0], left, PART, 2).astype(jnp.float32)
    old = lax.dynamic_slice_in_dim(
        jnp.pad(own_rows, ((0, 0), (HALO, 0))), left, SPAN, 1
    )

    spectra, own = own_spectra(
        freq_start, tile_slot, live, weights, payload[0], table, own_rows
    )
    terms = gradient_parts(received, payload_below, spectra, own, table)
    terms, received = lax.optimization_barrier((terms, received))
    synth = synthesized(part, received, dual[:, 0], table)
    total = gathered_sum(terms) + synth
    new = jnp.maximum(old - TAU_STEP * total, 0.0)
    column = lax.broadcasted_iota(jnp.int32, old.shape, 1) + left
    extra = jnp.where(column >= HALO, 2.0 * new - old, 0.0)
    extra_above = hop(extra[FR - 8 :].astype(jnp.bfloat16), 1).astype(jnp.float32)
    extra = jnp.concatenate([extra_above, extra], 0)

    shifted = own_dual + SIGMA_STEP * analyze(extra)
    squares = lax.all_gather((shifted * shifted).astype(jnp.bfloat16), "cube")
    norms = jnp.sqrt(jnp.sum(squares.astype(jnp.float32), 0))
    dual_part = (shifted * (RADIUS / jnp.maximum(norms, RADIUS))).astype(jnp.bfloat16)
    own_part = jnp.concatenate([dual_part, total[None, :, HALO:].astype(jnp.bfloat16)], 0)
    parts = lax.all_to_all(jnp.broadcast_to(own_part, (DP,) + own_part.shape), "dp", 0, 0)
    updated, dual_next = finished(parts, own_rows)
    return (updated[None], dual_next[:, None])


def solution(mesh):
    return jax.shard_map(
        on_device,
        mesh=mesh,
        in_specs=(
            P("cube", "facet", None),
            P(None, "cube", "facet", None),
            P("cube", ("facet", "dp"), None, None),
            P("cube", ("facet", "dp"), None),
            P("cube", ("facet", "dp")),
            P("cube", ("facet", "dp")),
            P("cube", ("facet", "dp")),
        ),
        out_specs=(P("cube", "facet", None), P(None, "cube", "facet", None)),
        check_vma=False,
    )
```

```python
import functools
import math

import jax
import jax.numpy as jnp
import numpy as np
from jax import lax
from jax.experimental import pallas as pl
from jax.experimental.pallas import tpu as pltpu
from jax.sharding import PartitionSpec as P

LOWPASS = (
    0.2303778133088964,
    0.7148465705529155,
    0.6308807679298587,
    -0.027983769416859854,
    -0.18703481171909309,
    0.030841381835560764,
    0.0328830116668852,
    -0.010597401785069032,
)
HIGHPASS = (
    -0.010597401785069032,
    -0.0328830116668852,
    0.030841381835560764,
    0.18703481171909309,
    -0.027983769416859854,
    -0.6308807679298587,
    0.7148465705529155,
    -0.2303778133088964,
)
TAU_STEP = 0.5
SIGMA_STEP = 0.5
RADIUS = 3.0

W = 2560
TILE = 16
FR = 48
BLK = 64
PER = FR // TILE
Q = 20
R = 128
DP = 4
PART = W // DP
HALO = 128
SPAN = PART + HALO
CHUNKS = W // 64
UNROLL = 8
VMEM_LIMIT = 60 * 1024 * 1024
NORM = 1.0 / math.sqrt(W)
C1, C2 = math.cos(2 * math.pi / 5), math.cos(4 * math.pi / 5)
S1, S2 = math.sin(2 * math.pi / 5), math.sin(4 * math.pi / 5)


def tables():
    x = np.arange(W).reshape(R, Q).T
    angles = (x[:, :, None] * np.arange(R)[None, None, :] % W) * (2.0 * math.pi / W)
    table = np.concatenate([np.cos(angles), -np.sin(angles)], -1).astype(jnp.bfloat16)
    return table


def constants():
    table = tables()
    return np.concatenate([table.reshape(Q * R, 2 * R), column_filters().reshape(-1, 2 * HALO)])


def flipped_table():
    return tables().transpose(0, 2, 1).reshape(2 * Q * R, R)


def column_filters():
    band = np.zeros((2 * HALO, 2 * HALO), np.float32)
    for b, taps in enumerate((LOWPASS, HIGHPASS)):
        for k in range(8):
            j = np.arange(HALO)
            band[HALO + j - k, HALO * b + j] = taps[k]
    leading = band.astype(jnp.bfloat16)
    rest = (band - leading.astype(np.float32)).astype(jnp.bfloat16)
    return np.stack([leading, rest])


def times_i(value, sign):
    re, im = value
    return (-im, re) if sign > 0 else (im, -re)


def plus(u, v):
    return (u[0] + v[0], u[1] + v[1])


def minus(u, v):
    return (u[0] - v[0], u[1] - v[1])


def dft4(x, sign):
    a, b = plus(x[0], x[2]), minus(x[0], x[2])
    c, d = plus(x[1], x[3]), times_i(minus(x[1], x[3]), sign)
    return [plus(a, c), plus(b, d), minus(a, c), minus(b, d)]


def dft5(x, sign):
    t1, t2 = plus(x[1], x[4]), plus(x[2], x[3])
    t3, t4 = minus(x[1], x[4]), minus(x[2], x[3])
    m1 = tuple(z + C1 * u + C2 * v for z, u, v in zip(x[0], t1, t2))
    m2 = tuple(z + C2 * u + C1 * v for z, u, v in zip(x[0], t1, t2))
    n1 = times_i(tuple(S1 * u + S2 * v for u, v in zip(t3, t4)), sign)
    n2 = times_i(tuple(S2 * u - S1 * v for u, v in zip(t3, t4)), sign)
    return [plus(x[0], plus(t1, t2)), plus(m1, n1), plus(m2, n2), minus(m2, n2), minus(m1, n1)]


def dft20(x, sign):
    columns = [dft4([x[(5 * a + 4 * b) % 20] for a in range(4)], sign) for b in range(5)]
    out = [None] * 20
    for c in range(4):
        line = dft5([columns[b][c] for b in range(5)], sign)
        for e in range(5):
            out[(5 * c + 16 * e) % 20] = line[e]
    return out


def residue_order():
    y = lax.broadcasted_iota(jnp.int32, (PART, 128), 0)
    group = ((y.astype(jnp.float32) + 0.5) * (1.0 / Q)).astype(jnp.int32)
    target = (y - Q * group) * 32 + group
    lane = lax.broadcasted_iota(jnp.int32, (PART, 128), 1)
    tiles = [jnp.where(target == lane + 128 * j, 1.0, 0.0) for j in range(PART // 128)]
    return jnp.concatenate(tiles, 1).astype(jnp.bfloat16)


def natural_order():
    row = lax.broadcasted_iota(jnp.int32, (PART, 128), 0)
    tiles = []
    for j in range(PART // 128):
        y = lax.broadcasted_iota(jnp.int32, (1, 128), 1) + 128 * j
        group = ((y.astype(jnp.float32) + 0.5) * (1.0 / Q)).astype(jnp.int32)
        tiles.append(jnp.where(row == (y - Q * group) * 32 + group, 1.0, 0.0))
    return jnp.concatenate(tiles, 1).astype(jnp.bfloat16)


def add_blocks(base, start, slot, live, weights, payload_ref, spec_ref, grad_ref, list_ref):
    lane = lax.broadcasted_iota(jnp.int32, (1, 128), 1)
    half = lane & 63

    def collect(b, count):
        place = slot(b) - base
        list_ref[count] = b
        return count + jnp.where((place >= 0) & (place < PER), 1, 0)

    count = lax.fori_loop(0, live, collect, 0)
    for u in range(UNROLL):
        list_ref[count + u] = list_ref[0]
    slot_lane = lax.broadcasted_iota(jnp.int32, (1, 128), 1)
    ones = jnp.ones((128, 128), jnp.bfloat16)

    def blocks(step, carry):
        places = [step * UNROLL + u for u in range(UNROLL)]
        numbers = [list_ref[place] for place in places]
        picked = [
            jnp.where(slot_lane == jnp.where(place < count, b, -1), weights, 0.0)
            for place, b in zip(places, numbers)
        ]
        factors = jnp.dot(
            jnp.concatenate(picked, 0).astype(jnp.bfloat16), ones, preferred_element_type=jnp.float32
        )
        found = []
        for u, b in enumerate(numbers):
            chunk, offset = start(b)
            tile = jnp.clip(slot(b) - base, 0, PER - 1)
            rows = pl.ds(pl.multiple_of(tile * TILE, TILE), TILE)
            first = pltpu.roll(spec_ref[chunk, rows, :].astype(jnp.float32), (128 - offset) & 127, 1)
            second = pltpu.roll(spec_ref[chunk + 1, rows, :].astype(jnp.float32), 64 - offset, 1)
            model = jnp.where(half < 64 - offset, first, second)
            misfit = factors[TILE * u : TILE * (u + 1)] * (
                model - payload_ref[b].astype(jnp.float32)
            )
            lower = jnp.where(half >= offset, pltpu.roll(misfit, offset, 1), 0.0)
            upper = jnp.where(half < offset, pltpu.roll(misfit, 64 + offset, 1), 0.0)
            found.append((chunk, rows, lower, upper))
        for chunk, rows, lower, upper in found:
            grad_ref[chunk, rows, :] += lower
            grad_ref[chunk + 1, rows, :] += upper
        return carry

    lax.fori_loop(0, (count + UNROLL - 1) // UNROLL, blocks, 0)


def columns_back(part, rows, dual_ref, filters, rows_ref):
    tiles = SPAN // HALO + 1
    blocks = []
    for j in range(tiles):
        place = (PART // HALO) * part - 1 + j
        inside = (place >= 0) & (place < W // HALO)
        columns = pl.ds(pl.multiple_of(jnp.clip(place, 0, W // HALO - 1) * HALO, HALO), HALO)
        for a in range(2):
            pair = jnp.concatenate([dual_ref[2 * a + b, :rows, columns] for b in range(2)], 1)
            blocks.append(jnp.where(inside, pair, jnp.zeros_like(pair)))
    stacked = jnp.concatenate(blocks, 0)
    across = sum(
        lax.dot_general(
            stacked, filters(i), (((1,), (1,)), ((), ())), preferred_element_type=jnp.float32
        )
        for i in range(2)
    )
    for j in range(tiles - 1):
        for a in range(2):
            here, right = [across[rows * (2 * i + a) : rows * (2 * i + a + 1)] for i in (j, j + 1)]
            rows_ref[a, 8 : 8 + rows, HALO * j : HALO * (j + 1)] = (
                here[:, HALO:] + right[:, :HALO]
            )


def rows_back(first, count, tile, rows_ref):
    value = 0.0
    for a, taps in enumerate((LOWPASS, HIGHPASS)):
        for k in range(8):
            value = value + taps[k] * rows_ref[a, 8 + first + k : 8 + first + k + count, tile]
    return value


def write_message(
    part_ref,
    starts_hbm,
    slots_hbm,
    live_hbm,
    weight_hbm,
    dual_hbm,
    filters_hbm,
    out_ref,
    starts_ref,
    slots_ref,
    live_ref,
    weight_ref,
    dual_ref,
    filters_ref,
    rows_ref,
    sems,
):
    pairs = [
        (dual_hbm.at[:, :TILE, :], dual_ref),
        (filters_hbm.at[pl.ds(Q * R, 4 * HALO), :], filters_ref),
        (starts_hbm, starts_ref),
        (slots_hbm, slots_ref),
        (live_hbm, live_ref),
        (weight_hbm, weight_ref),
    ]
    copies = [pltpu.make_async_copy(s, d, sems.at[i]) for i, (s, d) in enumerate(pairs)]
    for copy in copies:
        copy.start()
    rows_ref[:, :8, :] = jnp.zeros((2, 8, SPAN), jnp.float32)
    copies[0].wait()
    copies[1].wait()
    columns_back(
        part_ref[0],
        TILE,
        dual_ref,
        lambda i: filters_ref[2 * HALO * i : 2 * HALO * (i + 1)],
        rows_ref,
    )
    for i in range(SPAN // HALO // 2):
        pair = [rows_back(-8, 8, pl.ds(HALO * (2 * i + j), HALO), rows_ref) for j in range(2)]
        out_ref[1 + i] = jnp.concatenate(pair, 0).astype(jnp.bfloat16)
    for copy in copies[2:]:
        copy.wait()
    row = lax.broadcasted_iota(jnp.int32, (TILE, BLK), 0)
    starts = starts_ref[...]
    numbers = jnp.where(row == 0, starts >> 6, starts & 63)
    numbers = jnp.where(row == 2, slots_ref[...], numbers)
    numbers = jnp.where(row == 3, live_ref[0, 0], numbers)
    out_ref[0] = jnp.concatenate(
        [weight_ref[...].astype(jnp.float32), numbers.astype(jnp.float32)], 1
    ).astype(jnp.bfloat16)


def synthesis(part_ref, message_ref, dual_ref, constants_ref, synth_ref, rows_ref):
    columns_back(
        part_ref[0],
        FR,
        dual_ref,
        lambda i: constants_ref[Q * R + 2 * HALO * i : Q * R + 2 * HALO * (i + 1)],
        rows_ref,
    )
    rows_ref[:, 8 + FR :, :] = jnp.zeros((2, 8, SPAN), jnp.float32)
    for j in range(SPAN // HALO):
        tile = pl.ds(HALO * j, HALO)
        synth_ref[:, tile] = rows_back(0, FR, tile, rows_ref)
        below = message_ref[1 + j // 2].astype(jnp.float32)
        synth_ref[FR - 8 :, tile] += below[8 * (j % 2) : 8 * (j % 2) + 8]


def own_pass(
    starts_hbm,
    slots_hbm,
    live_hbm,
    weight_hbm,
    payload_hbm,
    table_hbm,
    pixels_hbm,
    spec_ref,
    own_ref,
    starts_ref,
    slots_ref,
    live_ref,
    list_ref,
    weight_ref,
    payload_ref,
    table_ref,
    pixels_ref,
    order_ref,
    re_ref,
    im_ref,
    grad_ref,
    sems,
):
    pairs = [
        (pixels_hbm, pixels_ref),
        (table_hbm.at[pl.ds(0, Q * R), :], table_ref),
        (weight_hbm, weight_ref),
        (payload_hbm, payload_ref),
        (starts_hbm, starts_ref),
        (slots_hbm, slots_ref),
        (live_hbm, live_ref),
    ]
    copies = [pltpu.make_async_copy(s, d, sems.at[i]) for i, (s, d) in enumerate(pairs)]
    for copy in copies:
        copy.start()
    lane = lax.broadcasted_iota(jnp.int32, (1, 128), 1)
    low = lane < 64
    quarter = lane >> 5

    order_ref[...] = residue_order()
    copies[0].wait()
    stacked = jnp.concatenate(
        [pixels_ref[:, PART * g : PART * (g + 1)].astype(jnp.bfloat16) for g in range(4)], 0
    )
    sorted_rows = jnp.dot(stacked, order_ref[...], preferred_element_type=jnp.float32)
    copies[1].wait()
    for j in range(5):
        tiles = [sorted_rows[FR * g : FR * (g + 1), 128 * j : 128 * (j + 1)] for g in range(4)]
        for p in range(4):
            turned = [
                tiles[g] if g == p else pltpu.roll(tiles[g], (32 * (g - p)) % 128, 1)
                for g in range(4)
            ]
            rows = turned[3]
            for g in range(3):
                rows = jnp.where(quarter == g, turned[g], rows)
            q = 4 * j + p
            partial = jnp.dot(
                rows.astype(jnp.bfloat16),
                table_ref[R * q : R * (q + 1)],
                preferred_element_type=jnp.float32,
            )
            re_ref[q] = partial[:, :R]
            im_ref[q] = partial[:, R:]

    def forward(i, carry):
        for j in range(2):
            rows = pl.ds(pl.multiple_of(i * TILE + 8 * j, 8), 8)
            spectrum = dft20([(re_ref[q, rows, :], im_ref[q, rows, :]) for q in range(Q)], -1)
            for k, (re, im) in enumerate(spectrum):
                re, im = re * NORM, im * NORM
                grad_ref[2 * k, rows, :] = jnp.where(low, re, pltpu.roll(im, 64, 1))
                grad_ref[2 * k + 1, rows, :] = jnp.where(low, pltpu.roll(re, 64, 1), im)
        return carry

    lax.fori_loop(0, FR // TILE, forward, 0)
    spec_ref[:CHUNKS] = grad_ref[:CHUNKS].astype(jnp.bfloat16)
    spec_ref[CHUNKS] = spec_ref[0]
    grad_ref[...] = jnp.zeros_like(grad_ref)
    for copy in copies[2:]:
        copy.wait()
    blank = jnp.zeros((TILE, 128 - BLK), jnp.float32)
    weights = jnp.concatenate([weight_ref[...].astype(jnp.float32), blank], 1)
    add_blocks(
        PER,
        lambda b: (starts_ref[0, b] >> 6, starts_ref[0, b] & 63),
        lambda b: slots_ref[0, b],
        live_ref[0, 0],
        weights,
        payload_ref,
        spec_ref,
        grad_ref,
        list_ref,
    )
    own_ref[...] = grad_ref[...].astype(jnp.bfloat16)


def below_pass(
    message_hbm,
    payload_hbm,
    spec_hbm,
    own_hbm,
    table_hbm,
    out_ref,
    list_ref,
    numbers_ref,
    vector_ref,
    message_ref,
    payload_ref,
    spec_ref,
    own_ref,
    grad_ref,
    table_ref,
    order_ref,
    re_ref,
    im_ref,
    tile_ref,
    sems,
):
    pairs = [
        (message_hbm.at[0], message_ref),
        (spec_hbm, spec_ref),
        (own_hbm, own_ref),
        (payload_hbm, payload_ref),
        (table_hbm, table_ref),
    ]
    copies = [pltpu.make_async_copy(s, d, sems.at[i]) for i, (s, d) in enumerate(pairs)]
    for copy in copies:
        copy.start()
    lane = lax.broadcasted_iota(jnp.int32, (1, 128), 1)
    low = lane < 64
    quarter = lane >> 5
    copies[0].wait()
    meta = message_ref[...].astype(jnp.float32)
    vector_ref[...] = meta[:8].astype(jnp.int32)
    read = pltpu.make_async_copy(vector_ref, numbers_ref, sems.at[5])
    read.start()
    order_ref[...] = natural_order()
    read.wait()
    for copy in copies[1:4]:
        copy.wait()
    grad_ref[...] = own_ref[...].astype(jnp.float32)
    add_blocks(
        0,
        lambda b: (numbers_ref[0, BLK + b], numbers_ref[1, BLK + b]),
        lambda b: numbers_ref[2, BLK + b],
        numbers_ref[3, BLK],
        jnp.where(low, meta, 0.0),
        payload_ref,
        spec_ref,
        grad_ref,
        list_ref,
    )
    grad_ref[0] += grad_ref[CHUNKS]

    def backward(i, carry):
        rows = pl.ds(pl.multiple_of(i * 8, 8), 8)
        spectrum = []
        for k in range(Q):
            even, odd = grad_ref[2 * k, rows, :], grad_ref[2 * k + 1, rows, :]
            spectrum.append(
                (
                    jnp.where(low, even, pltpu.roll(odd, 64, 1)),
                    jnp.where(low, pltpu.roll(even, 64, 1), odd),
                )
            )
        for q, (re, im) in enumerate(dft20(spectrum, 1)):
            re_ref[q, rows, :] = re * NORM
            im_ref[q, rows, :] = im * NORM
        return carry

    lax.fori_loop(0, FR // 8, backward, 0)
    copies[4].wait()
    for j in range(5):
        places = [[] for _ in range(4)]
        for p in range(4):
            q = 4 * j + p
            pair = jnp.concatenate([re_ref[q], im_ref[q]], 1).astype(jnp.bfloat16)
            rows = jnp.dot(
                pair, table_ref[2 * R * q : 2 * R * (q + 1)], preferred_element_type=jnp.float32
            )
            for g in range(4):
                places[g].append(rows if g == p else pltpu.roll(rows, (32 * (p - g)) % 128, 1))
        for g in range(4):
            tile = places[g][3]
            for p in range(3):
                tile = jnp.where(quarter == p, places[g][p], tile)
            tile_ref[5 * g + j] = tile
    mixed = jnp.concatenate(
        [jnp.concatenate([tile_ref[5 * g + j] for j in range(5)], 1) for g in range(4)], 0
    ).astype(jnp.bfloat16)
    natural = jnp.dot(
        mixed, order_ref[...], preferred_element_type=jnp.float32
    ).astype(jnp.bfloat16)
    out_ref[0, :, :HALO] = jnp.zeros((FR, HALO), jnp.bfloat16)
    for g in range(4):
        rows = natural[FR * g : FR * (g + 1)]
        out_ref[g, :, HALO:] = rows
        if g < 3:
            out_ref[g + 1, :, :HALO] = rows[:, PART - HALO :]


HBM_SPEC = pl.BlockSpec(memory_space=pltpu.HBM)
SMEM_SPEC = pl.BlockSpec(memory_space=pltpu.SMEM)
VMEM_SPEC = pl.BlockSpec(memory_space=pltpu.VMEM)
SPECTRA = jax.ShapeDtypeStruct((CHUNKS + 1, FR, 128), jnp.bfloat16)


TABLE = pltpu.VMEM((Q * R, 2 * R), jnp.bfloat16)
PARAMS = pltpu.CompilerParams(vmem_limit_bytes=VMEM_LIMIT)
COST = pl.CostEstimate(flops=2 * 10**9, bytes_accessed=4 * 10**6, transcendentals=0)


def message(part, starts, slots, live, weights, dual, table):
    return pl.pallas_call(
        write_message,
        out_shape=jax.ShapeDtypeStruct((1 + SPAN // HALO // 2, TILE, 128), jnp.bfloat16),
        in_specs=[SMEM_SPEC] + [HBM_SPEC] * 6,
        out_specs=VMEM_SPEC,
        scratch_shapes=[
            pltpu.VMEM((1, BLK), jnp.int32),
            pltpu.VMEM((1, BLK), jnp.int32),
            pltpu.SMEM((1, 1), jnp.int32),
            pltpu.VMEM((TILE, BLK), jnp.bfloat16),
            pltpu.VMEM((4, TILE, W), jnp.bfloat16),
            pltpu.VMEM((4 * HALO, 2 * HALO), jnp.bfloat16),
            pltpu.VMEM((2, 8 + TILE, SPAN), jnp.float32),
            pltpu.SemaphoreType.DMA((6,)),
        ],
        compiler_params=PARAMS,
        name="message",
    )(part, starts, slots, live, weights, dual, table)


def synthesized(part, received, dual, table):
    return pl.pallas_call(
        synthesis,
        out_shape=jax.ShapeDtypeStruct((FR, SPAN), jnp.float32),
        in_specs=[SMEM_SPEC] + [VMEM_SPEC] * 3,
        out_specs=VMEM_SPEC,
        scratch_shapes=[pltpu.VMEM((2, FR + 16, SPAN), jnp.float32)],
        compiler_params=pltpu.CompilerParams(vmem_limit_bytes=16 * 1024 * 1024),
        name="synthesized",
    )(part, received, dual, table)


def own_spectra(starts, slots, live, weights, payload, table, pixels):
    return pl.pallas_call(
        own_pass,
        out_shape=(SPECTRA, SPECTRA),
        in_specs=[HBM_SPEC] * 7,
        out_specs=(VMEM_SPEC,) * 2,
        scratch_shapes=[
            pltpu.SMEM((1, BLK), jnp.int32),
            pltpu.SMEM((1, BLK), jnp.int32),
            pltpu.SMEM((1, 1), jnp.int32),
            pltpu.SMEM((BLK + UNROLL,), jnp.int32),
            pltpu.VMEM((TILE, BLK), jnp.bfloat16),
            pltpu.VMEM((BLK, TILE, 128), jnp.bfloat16),
            TABLE,
            pltpu.VMEM((FR, W), jnp.float32),
            pltpu.VMEM((PART, PART), jnp.bfloat16),
            pltpu.VMEM((Q, FR, R), jnp.float32),
            pltpu.VMEM((Q, FR, R), jnp.float32),
            pltpu.VMEM((CHUNKS + 1, FR, 128), jnp.float32),
            pltpu.SemaphoreType.DMA((7,)),
        ],
        compiler_params=PARAMS,
        cost_estimate=COST,
        name="own_spectra",
    )(starts, slots, live, weights, payload, table, pixels)


def gradient_parts(received, payload, spectra, own, table):
    return pl.pallas_call(
        below_pass,
        out_shape=jax.ShapeDtypeStruct((DP, FR, SPAN), jnp.bfloat16),
        in_specs=[HBM_SPEC] * 5,
        out_specs=VMEM_SPEC,
        scratch_shapes=[
            pltpu.SMEM((BLK + UNROLL,), jnp.int32),
            pltpu.SMEM((8, 128), jnp.int32),
            pltpu.VMEM((8, 128), jnp.int32),
            pltpu.VMEM((TILE, 128), jnp.bfloat16),
            pltpu.VMEM((BLK, TILE, 128), jnp.bfloat16),
            pltpu.VMEM((CHUNKS + 1, FR, 128), jnp.bfloat16),
            pltpu.VMEM((CHUNKS + 1, FR, 128), jnp.bfloat16),
            pltpu.VMEM((CHUNKS + 1, FR, 128), jnp.float32),
            pltpu.VMEM((2 * Q * R, R), jnp.bfloat16),
            pltpu.VMEM((PART, PART), jnp.bfloat16),
            pltpu.VMEM((Q, FR, R), jnp.float32),
            pltpu.VMEM((Q, FR, R), jnp.float32),
            pltpu.VMEM((Q, FR, R), jnp.float32),
            pltpu.SemaphoreType.DMA((6,)),
        ],
        compiler_params=PARAMS,
        cost_estimate=COST,
        name="gradient_parts",
    )(received, payload, spectra, own, table)


def finish(parts_ref, pixels_ref, image_hbm, dual_hbm, image_ref, sems):
    copies = []
    for d in range(DP):
        tile = pl.ds(PART * d, PART)
        copies.append(
            pltpu.make_async_copy(
                parts_ref.at[d, pl.ds(0, 4)], dual_hbm.at[:, :, tile], sems.at[d]
            )
        )
        copies[-1].start()
    for d in range(DP):
        tile = pl.ds(PART * d, PART)
        descent = parts_ref[d, 4].astype(jnp.float32)
        image_ref[:, tile] = jnp.maximum(pixels_ref[:, tile] - TAU_STEP * descent, 0.0)
    copies.append(pltpu.make_async_copy(image_ref, image_hbm, sems.at[DP]))
    copies[-1].start()
    for copy in copies:
        copy.wait()


def finished(parts, pixels):
    return pl.pallas_call(
        finish,
        out_shape=(
            jax.ShapeDtypeStruct((FR, W), jnp.float32),
            jax.ShapeDtypeStruct((4, FR, W), jnp.bfloat16),
        ),
        in_specs=[VMEM_SPEC] * 2,
        out_specs=(HBM_SPEC,) * 2,
        scratch_shapes=[pltpu.VMEM((FR, W), jnp.float32), pltpu.SemaphoreType.DMA((DP + 1,))],
        compiler_params=pltpu.CompilerParams(vmem_limit_bytes=16 * 1024 * 1024),
        name="finished",
    )(parts, pixels)


def hop(block, distance):
    devices = range(lax.axis_size("facet"))
    route = [(i - distance, i) for i in devices if i - distance in devices]
    return lax.ppermute(block, "facet", route)


def gathered_sum(parts):
    mixed = lax.all_to_all(parts, "dp", 0, 0)
    return jnp.sum(mixed.astype(jnp.float32), 0)


def analyze(extra):
    subbands = []
    for row_taps in (LOWPASS, HIGHPASS):
        filtered = sum(row_taps[k] * extra[8 - k : 8 - k + FR] for k in range(8))
        for col_taps in (LOWPASS, HIGHPASS):
            subbands.append(
                sum(col_taps[k] * filtered[:, HALO - k : HALO - k + PART] for k in range(8))
            )
    return jnp.stack(subbands)


def on_device(image, dual, payload, vis_weight, freq_start, tile_slot, live):
    table, flipped = jnp.asarray(constants()), jnp.asarray(flipped_table())
    position = lax.axis_index("dp")
    own_rows = image[0]
    part = position[None]
    weights = vis_weight[0].T
    payload_below = hop(payload[0], -1)
    received = hop(
        message(part, freq_start, tile_slot, live, weights, dual[:, 0], table), -1
    )

    left = position * PART
    own_dual = lax.dynamic_slice_in_dim(dual[:, 0], left, PART, 2).astype(jnp.float32)
    old = lax.dynamic_slice_in_dim(
        jnp.pad(own_rows, ((0, 0), (HALO, 0))), left, SPAN, 1
    )

    spectra, own = own_spectra(
        freq_start, tile_slot, live, weights, payload[0], table, own_rows
    )
    terms = gradient_parts(received, payload_below, spectra, own, flipped)
    terms, received = lax.optimization_barrier((terms, received))
    synth = synthesized(part, received, dual[:, 0], table)
    total = gathered_sum(terms) + synth
    new = jnp.maximum(old - TAU_STEP * total, 0.0)
    column = lax.broadcasted_iota(jnp.int32, old.shape, 1) + left
    extra = jnp.where(column >= HALO, 2.0 * new - old, 0.0)
    extra_above = hop(extra[FR - 8 :].astype(jnp.bfloat16), 1).astype(jnp.float32)
    extra = jnp.concatenate([extra_above, extra], 0)

    shifted = own_dual + SIGMA_STEP * analyze(extra)
    squares = lax.all_gather((shifted * shifted).astype(jnp.bfloat16), "cube")
    norms = jnp.sqrt(jnp.sum(squares.astype(jnp.float32), 0))
    dual_part = (shifted * (RADIUS / jnp.maximum(norms, RADIUS))).astype(jnp.bfloat16)
    own_part = jnp.concatenate([dual_part, total[None, :, HALO:].astype(jnp.bfloat16)], 0)
    parts = lax.all_to_all(jnp.broadcast_to(own_part, (DP,) + own_part.shape), "dp", 0, 0)
    updated, dual_next = finished(parts, own_rows)
    return (updated[None], dual_next[:, None])


def solution(mesh):
    return jax.shard_map(
        on_device,
        mesh=mesh,
        in_specs=(
            P("cube", "facet", None),
            P(None, "cube", "facet", None),
            P("cube", ("facet", "dp"), None, None),
            P("cube", ("facet", "dp"), None),
            P("cube", ("facet", "dp")),
            P("cube", ("facet", "dp")),
            P("cube", ("facet", "dp")),
        ),
        out_specs=(P("cube", "facet", None), P(None, "cube", "facet", None)),
        check_vma=False,
    )
```

```python
import functools
import math

import jax
import jax.numpy as jnp
import numpy as np
from jax import lax
from jax.experimental import pallas as pl
from jax.experimental.pallas import tpu as pltpu
from jax.sharding import PartitionSpec as P

LOWPASS = (
    0.2303778133088964,
    0.7148465705529155,
    0.6308807679298587,
    -0.027983769416859854,
    -0.18703481171909309,
    0.030841381835560764,
    0.0328830116668852,
    -0.010597401785069032,
)
HIGHPASS = (
    -0.010597401785069032,
    -0.0328830116668852,
    0.030841381835560764,
    0.18703481171909309,
    -0.027983769416859854,
    -0.6308807679298587,
    0.7148465705529155,
    -0.2303778133088964,
)
TAU_STEP = 0.5
SIGMA_STEP = 0.5
RADIUS = 3.0

W = 2560
TILE = 16
FR = 48
BLK = 64
PER = FR // TILE
Q = 20
R = 128
DP = 4
PART = W // DP
HALO = 128
SPAN = PART + HALO
CHUNKS = W // 64
UNROLL = 16
VMEM_LIMIT = 60 * 1024 * 1024
NORM = 1.0 / math.sqrt(W)
C1, C2 = math.cos(2 * math.pi / 5), math.cos(4 * math.pi / 5)
S1, S2 = math.sin(2 * math.pi / 5), math.sin(4 * math.pi / 5)


def tables():
    x = np.arange(W).reshape(R, Q).T
    angles = (x[:, :, None] * np.arange(R)[None, None, :] % W) * (2.0 * math.pi / W)
    table = np.concatenate([np.cos(angles), -np.sin(angles)], -1).astype(jnp.bfloat16)
    return table


def constants():
    table = tables()
    return np.concatenate([table.reshape(Q * R, 2 * R), column_filters().reshape(-1, 2 * HALO)])


def flipped_table():
    return tables().transpose(0, 2, 1).reshape(2 * Q * R, R)


def column_filters():
    band = np.zeros((2 * HALO, 2 * HALO), np.float32)
    for b, taps in enumerate((LOWPASS, HIGHPASS)):
        for k in range(8):
            j = np.arange(HALO)
            band[HALO + j - k, HALO * b + j] = taps[k]
    leading = band.astype(jnp.bfloat16)
    rest = (band - leading.astype(np.float32)).astype(jnp.bfloat16)
    return np.stack([leading, rest])


def times_i(value, sign):
    re, im = value
    return (-im, re) if sign > 0 else (im, -re)


def plus(u, v):
    return (u[0] + v[0], u[1] + v[1])


def minus(u, v):
    return (u[0] - v[0], u[1] - v[1])


def dft4(x, sign):
    a, b = plus(x[0], x[2]), minus(x[0], x[2])
    c, d = plus(x[1], x[3]), times_i(minus(x[1], x[3]), sign)
    return [plus(a, c), plus(b, d), minus(a, c), minus(b, d)]


def dft5(x, sign):
    t1, t2 = plus(x[1], x[4]), plus(x[2], x[3])
    t3, t4 = minus(x[1], x[4]), minus(x[2], x[3])
    m1 = tuple(z + C1 * u + C2 * v for z, u, v in zip(x[0], t1, t2))
    m2 = tuple(z + C2 * u + C1 * v for z, u, v in zip(x[0], t1, t2))
    n1 = times_i(tuple(S1 * u + S2 * v for u, v in zip(t3, t4)), sign)
    n2 = times_i(tuple(S2 * u - S1 * v for u, v in zip(t3, t4)), sign)
    return [plus(x[0], plus(t1, t2)), plus(m1, n1), plus(m2, n2), minus(m2, n2), minus(m1, n1)]


def dft20(x, sign):
    columns = [dft4([x[(5 * a + 4 * b) % 20] for a in range(4)], sign) for b in range(5)]
    out = [None] * 20
    for c in range(4):
        line = dft5([columns[b][c] for b in range(5)], sign)
        for e in range(5):
            out[(5 * c + 16 * e) % 20] = line[e]
    return out


def residue_order():
    y = lax.broadcasted_iota(jnp.int32, (PART, 128), 0)
    group = ((y.astype(jnp.float32) + 0.5) * (1.0 / Q)).astype(jnp.int32)
    target = (y - Q * group) * 32 + group
    lane = lax.broadcasted_iota(jnp.int32, (PART, 128), 1)
    tiles = [jnp.where(target == lane + 128 * j, 1.0, 0.0) for j in range(PART // 128)]
    return jnp.concatenate(tiles, 1).astype(jnp.bfloat16)


def natural_order():
    row = lax.broadcasted_iota(jnp.int32, (PART, 128), 0)
    tiles = []
    for j in range(PART // 128):
        y = lax.broadcasted_iota(jnp.int32, (1, 128), 1) + 128 * j
        group = ((y.astype(jnp.float32) + 0.5) * (1.0 / Q)).astype(jnp.int32)
        tiles.append(jnp.where(row == (y - Q * group) * 32 + group, 1.0, 0.0))
    return jnp.concatenate(tiles, 1).astype(jnp.bfloat16)


def add_blocks(base, start, slot, live, weights, payload_ref, spec_ref, grad_ref, list_ref):
    lane = lax.broadcasted_iota(jnp.int32, (1, 128), 1)
    half = lane & 63

    def collect(b, count):
        place = slot(b) - base
        list_ref[count] = b
        return count + jnp.where((place >= 0) & (place < PER), 1, 0)

    count = lax.fori_loop(0, live, collect, 0)
    for u in range(UNROLL):
        list_ref[count + u] = list_ref[0]
    slot_lane = lax.broadcasted_iota(jnp.int32, (1, 128), 1)
    ones = jnp.ones((128, 128), jnp.bfloat16)

    def blocks(step, carry):
        places = [step * UNROLL + u for u in range(UNROLL)]
        numbers = [list_ref[place] for place in places]
        picked = [
            jnp.where(slot_lane == jnp.where(place < count, b, -1), weights, 0.0)
            for place, b in zip(places, numbers)
        ]
        factors = jnp.dot(
            jnp.concatenate(picked, 0).astype(jnp.bfloat16), ones, preferred_element_type=jnp.float32
        )
        found = []
        for u, b in enumerate(numbers):
            chunk, offset = start(b)
            tile = jnp.clip(slot(b) - base, 0, PER - 1)
            rows = pl.ds(pl.multiple_of(tile * TILE, TILE), TILE)
            first = pltpu.roll(spec_ref[chunk, rows, :].astype(jnp.float32), (128 - offset) & 127, 1)
            second = pltpu.roll(spec_ref[chunk + 1, rows, :].astype(jnp.float32), 64 - offset, 1)
            model = jnp.where(half < 64 - offset, first, second)
            misfit = factors[TILE * u : TILE * (u + 1)] * (
                model - payload_ref[b].astype(jnp.float32)
            )
            lower = jnp.where(half >= offset, pltpu.roll(misfit, offset, 1), 0.0)
            upper = jnp.where(half < offset, pltpu.roll(misfit, 64 + offset, 1), 0.0)
            found.append((chunk, rows, lower, upper))
        for chunk, rows, lower, upper in found:
            grad_ref[chunk, rows, :] += lower
            grad_ref[chunk + 1, rows, :] += upper
        return carry

    lax.fori_loop(0, (count + UNROLL - 1) // UNROLL, blocks, 0)


def columns_back(part, rows, dual_ref, filters, rows_ref):
    tiles = SPAN // HALO + 1
    blocks = []
    for j in range(tiles):
        place = (PART // HALO) * part - 1 + j
        inside = (place >= 0) & (place < W // HALO)
        columns = pl.ds(pl.multiple_of(jnp.clip(place, 0, W // HALO - 1) * HALO, HALO), HALO)
        for a in range(2):
            pair = jnp.concatenate([dual_ref[2 * a + b, :rows, columns] for b in range(2)], 1)
            blocks.append(jnp.where(inside, pair, jnp.zeros_like(pair)))
    stacked = jnp.concatenate(blocks, 0)
    across = sum(
        lax.dot_general(
            stacked, filters(i), (((1,), (1,)), ((), ())), preferred_element_type=jnp.float32
        )
        for i in range(2)
    )
    for j in range(tiles - 1):
        for a in range(2):
            here, right = [across[rows * (2 * i + a) : rows * (2 * i + a + 1)] for i in (j, j + 1)]
            rows_ref[a, 8 : 8 + rows, HALO * j : HALO * (j + 1)] = (
                here[:, HALO:] + right[:, :HALO]
            )


def rows_back(first, count, tile, rows_ref):
    value = 0.0
    for a, taps in enumerate((LOWPASS, HIGHPASS)):
        for k in range(8):
            value = value + taps[k] * rows_ref[a, 8 + first + k : 8 + first + k + count, tile]
    return value


def fill_message(part, starts, slots, live, weights, dual_ref, filters_ref, rows_ref, out_ref):
    rows_ref[:, :8, :] = jnp.zeros((2, 8, SPAN), jnp.float32)
    columns_back(
        part,
        TILE,
        dual_ref,
        lambda i: filters_ref[2 * HALO * i : 2 * HALO * (i + 1)],
        rows_ref,
    )
    for i in range(SPAN // HALO // 2):
        pair = [rows_back(-8, 8, pl.ds(HALO * (2 * i + j), HALO), rows_ref) for j in range(2)]
        out_ref[1 + i] = jnp.concatenate(pair, 0).astype(jnp.bfloat16)
    row = lax.broadcasted_iota(jnp.int32, (TILE, BLK), 0)
    numbers = jnp.where(row == 0, starts >> 6, starts & 63)
    numbers = jnp.where(row == 2, slots, numbers)
    numbers = jnp.where(row == 3, live, numbers)
    out_ref[0] = jnp.concatenate([weights, numbers.astype(jnp.float32)], 1).astype(jnp.bfloat16)


def synthesis(part_ref, message_ref, dual_ref, constants_ref, synth_ref, rows_ref):
    columns_back(
        part_ref[0],
        FR,
        dual_ref,
        lambda i: constants_ref[Q * R + 2 * HALO * i : Q * R + 2 * HALO * (i + 1)],
        rows_ref,
    )
    rows_ref[:, 8 + FR :, :] = jnp.zeros((2, 8, SPAN), jnp.float32)
    for j in range(SPAN // HALO):
        tile = pl.ds(HALO * j, HALO)
        synth_ref[:, tile] = rows_back(0, FR, tile, rows_ref)
        below = message_ref[1 + j // 2].astype(jnp.float32)
        synth_ref[FR - 8 :, tile] += below[8 * (j % 2) : 8 * (j % 2) + 8]


def own_pass(
    part_ref,
    starts_hbm,
    slots_hbm,
    live_hbm,
    weight_hbm,
    payload_hbm,
    table_hbm,
    pixels_hbm,
    dual_hbm,
    spec_ref,
    own_ref,
    message_ref,
    starts_ref,
    slots_ref,
    live_ref,
    list_ref,
    starts_vec,
    slots_vec,
    dual_ref,
    filters_ref,
    rows_ref,
    weight_ref,
    payload_ref,
    table_ref,
    pixels_ref,
    order_ref,
    re_ref,
    im_ref,
    grad_ref,
    sems,
):
    pairs = [
        (pixels_hbm, pixels_ref),
        (table_hbm.at[pl.ds(0, Q * R), :], table_ref),
        (weight_hbm, weight_ref),
        (payload_hbm, payload_ref),
        (starts_hbm, starts_ref),
        (slots_hbm, slots_ref),
        (live_hbm, live_ref),
        (starts_hbm, starts_vec),
        (slots_hbm, slots_vec),
        (dual_hbm.at[:, :TILE, :], dual_ref),
        (table_hbm.at[pl.ds(Q * R, 4 * HALO), :], filters_ref),
    ]
    copies = [pltpu.make_async_copy(s, d, sems.at[i]) for i, (s, d) in enumerate(pairs)]
    for copy in copies:
        copy.start()
    lane = lax.broadcasted_iota(jnp.int32, (1, 128), 1)
    low = lane < 64
    quarter = lane >> 5

    order_ref[...] = residue_order()
    copies[0].wait()
    stacked = jnp.concatenate(
        [pixels_ref[:, PART * g : PART * (g + 1)].astype(jnp.bfloat16) for g in range(4)], 0
    )
    sorted_rows = jnp.dot(stacked, order_ref[...], preferred_element_type=jnp.float32)
    copies[1].wait()
    for j in range(5):
        tiles = [sorted_rows[FR * g : FR * (g + 1), 128 * j : 128 * (j + 1)] for g in range(4)]
        for p in range(4):
            turned = [
                tiles[g] if g == p else pltpu.roll(tiles[g], (32 * (g - p)) % 128, 1)
                for g in range(4)
            ]
            rows = turned[3]
            for g in range(3):
                rows = jnp.where(quarter == g, turned[g], rows)
            q = 4 * j + p
            partial = jnp.dot(
                rows.astype(jnp.bfloat16),
                table_ref[R * q : R * (q + 1)],
                preferred_element_type=jnp.float32,
            )
            re_ref[q] = partial[:, :R]
            im_ref[q] = partial[:, R:]

    def forward(i, carry):
        for j in range(2):
            rows = pl.ds(pl.multiple_of(i * TILE + 8 * j, 8), 8)
            spectrum = dft20([(re_ref[q, rows, :], im_ref[q, rows, :]) for q in range(Q)], -1)
            for k, (re, im) in enumerate(spectrum):
                re, im = re * NORM, im * NORM
                grad_ref[2 * k, rows, :] = jnp.where(low, re, pltpu.roll(im, 64, 1))
                grad_ref[2 * k + 1, rows, :] = jnp.where(low, pltpu.roll(re, 64, 1), im)
        return carry

    lax.fori_loop(0, FR // TILE, forward, 0)
    spec_ref[:CHUNKS] = grad_ref[:CHUNKS].astype(jnp.bfloat16)
    spec_ref[CHUNKS] = spec_ref[0]
    grad_ref[...] = jnp.zeros_like(grad_ref)
    for copy in copies[2:]:
        copy.wait()
    blank = jnp.zeros((TILE, 128 - BLK), jnp.float32)
    weights = weight_ref[...].astype(jnp.float32)
    fill_message(
        part_ref[0],
        starts_vec[...],
        slots_vec[...],
        live_ref[0, 0],
        weights,
        dual_ref,
        filters_ref,
        rows_ref,
        message_ref,
    )
    weights = jnp.concatenate([weights, blank], 1)
    add_blocks(
        PER,
        lambda b: (starts_ref[0, b] >> 6, starts_ref[0, b] & 63),
        lambda b: slots_ref[0, b],
        live_ref[0, 0],
        weights,
        payload_ref,
        spec_ref,
        grad_ref,
        list_ref,
    )
    own_ref[...] = grad_ref[...].astype(jnp.bfloat16)


def below_pass(
    message_hbm,
    payload_hbm,
    spec_hbm,
    own_hbm,
    table_hbm,
    out_ref,
    list_ref,
    numbers_ref,
    vector_ref,
    message_ref,
    payload_ref,
    spec_ref,
    own_ref,
    grad_ref,
    table_ref,
    order_ref,
    re_ref,
    im_ref,
    tile_ref,
    sems,
):
    pairs = [
        (message_hbm.at[0], message_ref),
        (spec_hbm, spec_ref),
        (own_hbm, own_ref),
        (payload_hbm, payload_ref),
        (table_hbm, table_ref),
    ]
    copies = [pltpu.make_async_copy(s, d, sems.at[i]) for i, (s, d) in enumerate(pairs)]
    for copy in copies:
        copy.start()
    lane = lax.broadcasted_iota(jnp.int32, (1, 128), 1)
    low = lane < 64
    quarter = lane >> 5
    copies[0].wait()
    meta = message_ref[...].astype(jnp.float32)
    vector_ref[...] = meta[:8].astype(jnp.int32)
    read = pltpu.make_async_copy(vector_ref, numbers_ref, sems.at[5])
    read.start()
    order_ref[...] = natural_order()
    read.wait()
    for copy in copies[1:4]:
        copy.wait()
    grad_ref[...] = own_ref[...].astype(jnp.float32)
    add_blocks(
        0,
        lambda b: (numbers_ref[0, BLK + b], numbers_ref[1, BLK + b]),
        lambda b: numbers_ref[2, BLK + b],
        numbers_ref[3, BLK],
        jnp.where(low, meta, 0.0),
        payload_ref,
        spec_ref,
        grad_ref,
        list_ref,
    )
    grad_ref[0] += grad_ref[CHUNKS]

    def backward(i, carry):
        rows = pl.ds(pl.multiple_of(i * 8, 8), 8)
        spectrum = []
        for k in range(Q):
            even, odd = grad_ref[2 * k, rows, :], grad_ref[2 * k + 1, rows, :]
            spectrum.append(
                (
                    jnp.where(low, even, pltpu.roll(odd, 64, 1)),
                    jnp.where(low, pltpu.roll(even, 64, 1), odd),
                )
            )
        for q, (re, im) in enumerate(dft20(spectrum, 1)):
            re_ref[q, rows, :] = re * NORM
            im_ref[q, rows, :] = im * NORM
        return carry

    lax.fori_loop(0, FR // 8, backward, 0)
    copies[4].wait()
    for j in range(5):
        places = [[] for _ in range(4)]
        for p in range(4):
            q = 4 * j + p
            pair = jnp.concatenate([re_ref[q], im_ref[q]], 1).astype(jnp.bfloat16)
            rows = jnp.dot(
                pair, table_ref[2 * R * q : 2 * R * (q + 1)], preferred_element_type=jnp.float32
            )
            for g in range(4):
                places[g].append(rows if g == p else pltpu.roll(rows, (32 * (p - g)) % 128, 1))
        for g in range(4):
            tile = places[g][3]
            for p in range(3):
                tile = jnp.where(quarter == p, places[g][p], tile)
            tile_ref[5 * g + j] = tile
    mixed = jnp.concatenate(
        [jnp.concatenate([tile_ref[5 * g + j] for j in range(5)], 1) for g in range(4)], 0
    ).astype(jnp.bfloat16)
    natural = jnp.dot(
        mixed, order_ref[...], preferred_element_type=jnp.float32
    ).astype(jnp.bfloat16)
    out_ref[0, :, :HALO] = jnp.zeros((FR, HALO), jnp.bfloat16)
    for g in range(4):
        rows = natural[FR * g : FR * (g + 1)]
        out_ref[g, :, HALO:] = rows
        if g < 3:
            out_ref[g + 1, :, :HALO] = rows[:, PART - HALO :]


HBM_SPEC = pl.BlockSpec(memory_space=pltpu.HBM)
SMEM_SPEC = pl.BlockSpec(memory_space=pltpu.SMEM)
VMEM_SPEC = pl.BlockSpec(memory_space=pltpu.VMEM)
SPECTRA = jax.ShapeDtypeStruct((CHUNKS + 1, FR, 128), jnp.bfloat16)


TABLE = pltpu.VMEM((Q * R, 2 * R), jnp.bfloat16)
PARAMS = pltpu.CompilerParams(vmem_limit_bytes=VMEM_LIMIT)
COST = pl.CostEstimate(flops=2 * 10**9, bytes_accessed=4 * 10**6, transcendentals=0)


def synthesized(part, received, dual, table):
    return pl.pallas_call(
        synthesis,
        out_shape=jax.ShapeDtypeStruct((FR, SPAN), jnp.float32),
        in_specs=[SMEM_SPEC] + [VMEM_SPEC] * 3,
        out_specs=VMEM_SPEC,
        scratch_shapes=[pltpu.VMEM((2, FR + 16, SPAN), jnp.float32)],
        compiler_params=pltpu.CompilerParams(vmem_limit_bytes=16 * 1024 * 1024),
        name="synthesized",
    )(part, received, dual, table)


def own_spectra(part, starts, slots, live, weights, payload, table, pixels, dual):
    return pl.pallas_call(
        own_pass,
        out_shape=(
            SPECTRA,
            SPECTRA,
            jax.ShapeDtypeStruct((1 + SPAN // HALO // 2, TILE, 128), jnp.bfloat16),
        ),
        in_specs=[SMEM_SPEC] + [HBM_SPEC] * 8,
        out_specs=(VMEM_SPEC,) * 3,
        scratch_shapes=[
            pltpu.SMEM((1, BLK), jnp.int32),
            pltpu.SMEM((1, BLK), jnp.int32),
            pltpu.SMEM((1, 1), jnp.int32),
            pltpu.SMEM((BLK + UNROLL,), jnp.int32),
            pltpu.VMEM((1, BLK), jnp.int32),
            pltpu.VMEM((1, BLK), jnp.int32),
            pltpu.VMEM((4, TILE, W), jnp.bfloat16),
            pltpu.VMEM((4 * HALO, 2 * HALO), jnp.bfloat16),
            pltpu.VMEM((2, 8 + TILE, SPAN), jnp.float32),
            pltpu.VMEM((TILE, BLK), jnp.bfloat16),
            pltpu.VMEM((BLK, TILE, 128), jnp.bfloat16),
            TABLE,
            pltpu.VMEM((FR, W), jnp.float32),
            pltpu.VMEM((PART, PART), jnp.bfloat16),
            pltpu.VMEM((Q, FR, R), jnp.float32),
            pltpu.VMEM((Q, FR, R), jnp.float32),
            pltpu.VMEM((CHUNKS + 1, FR, 128), jnp.float32),
            pltpu.SemaphoreType.DMA((11,)),
        ],
        compiler_params=PARAMS,
        cost_estimate=COST,
        name="own_spectra",
    )(part, starts, slots, live, weights, payload, table, pixels, dual)


def gradient_parts(received, payload, spectra, own, table):
    return pl.pallas_call(
        below_pass,
        out_shape=jax.ShapeDtypeStruct((DP, FR, SPAN), jnp.bfloat16),
        in_specs=[HBM_SPEC] * 5,
        out_specs=VMEM_SPEC,
        scratch_shapes=[
            pltpu.SMEM((BLK + UNROLL,), jnp.int32),
            pltpu.SMEM((8, 128), jnp.int32),
            pltpu.VMEM((8, 128), jnp.int32),
            pltpu.VMEM((TILE, 128), jnp.bfloat16),
            pltpu.VMEM((BLK, TILE, 128), jnp.bfloat16),
            pltpu.VMEM((CHUNKS + 1, FR, 128), jnp.bfloat16),
            pltpu.VMEM((CHUNKS + 1, FR, 128), jnp.bfloat16),
            pltpu.VMEM((CHUNKS + 1, FR, 128), jnp.float32),
            pltpu.VMEM((2 * Q * R, R), jnp.bfloat16),
            pltpu.VMEM((PART, PART), jnp.bfloat16),
            pltpu.VMEM((Q, FR, R), jnp.float32),
            pltpu.VMEM((Q, FR, R), jnp.float32),
            pltpu.VMEM((Q, FR, R), jnp.float32),
            pltpu.SemaphoreType.DMA((6,)),
        ],
        compiler_params=PARAMS,
        cost_estimate=COST,
        name="gradient_parts",
    )(received, payload, spectra, own, table)


def finish(parts_ref, pixels_ref, image_hbm, dual_hbm, image_ref, sems):
    copies = []
    for d in range(DP):
        tile = pl.ds(PART * d, PART)
        copies.append(
            pltpu.make_async_copy(
                parts_ref.at[d, pl.ds(0, 4)], dual_hbm.at[:, :, tile], sems.at[d]
            )
        )
        copies[-1].start()
    for d in range(DP):
        tile = pl.ds(PART * d, PART)
        descent = parts_ref[d, 4].astype(jnp.float32)
        image_ref[:, tile] = jnp.maximum(pixels_ref[:, tile] - TAU_STEP * descent, 0.0)
    copies.append(pltpu.make_async_copy(image_ref, image_hbm, sems.at[DP]))
    copies[-1].start()
    for copy in copies:
        copy.wait()


def finished(parts, pixels):
    return pl.pallas_call(
        finish,
        out_shape=(
            jax.ShapeDtypeStruct((FR, W), jnp.float32),
            jax.ShapeDtypeStruct((4, FR, W), jnp.bfloat16),
        ),
        in_specs=[VMEM_SPEC] * 2,
        out_specs=(HBM_SPEC,) * 2,
        scratch_shapes=[pltpu.VMEM((FR, W), jnp.float32), pltpu.SemaphoreType.DMA((DP + 1,))],
        compiler_params=pltpu.CompilerParams(vmem_limit_bytes=16 * 1024 * 1024),
        name="finished",
    )(parts, pixels)


def hop(block, distance):
    devices = range(lax.axis_size("facet"))
    route = [(i - distance, i) for i in devices if i - distance in devices]
    return lax.ppermute(block, "facet", route)


def gathered_sum(parts):
    mixed = lax.all_to_all(parts, "dp", 0, 0)
    return jnp.sum(mixed.astype(jnp.float32), 0)


def analyze(extra):
    subbands = []
    for row_taps in (LOWPASS, HIGHPASS):
        filtered = sum(row_taps[k] * extra[8 - k : 8 - k + FR] for k in range(8))
        for col_taps in (LOWPASS, HIGHPASS):
            subbands.append(
                sum(col_taps[k] * filtered[:, HALO - k : HALO - k + PART] for k in range(8))
            )
    return jnp.stack(subbands)


def on_device(image, dual, payload, vis_weight, freq_start, tile_slot, live):
    table, flipped = jnp.asarray(constants()), jnp.asarray(flipped_table())
    position = lax.axis_index("dp")
    own_rows = image[0]
    part = position[None]
    weights = vis_weight[0].T
    payload_below = hop(payload[0], -1)
    left = position * PART
    own_dual = lax.dynamic_slice_in_dim(dual[:, 0], left, PART, 2).astype(jnp.float32)
    old = lax.dynamic_slice_in_dim(
        jnp.pad(own_rows, ((0, 0), (HALO, 0))), left, SPAN, 1
    )

    spectra, own, sent = own_spectra(
        part, freq_start, tile_slot, live, weights, payload[0], table, own_rows, dual[:, 0]
    )
    received = hop(sent, -1)
    terms = gradient_parts(received, payload_below, spectra, own, flipped)
    terms, received = lax.optimization_barrier((terms, received))
    synth = synthesized(part, received, dual[:, 0], table)
    total = gathered_sum(terms) + synth
    new = jnp.maximum(old - TAU_STEP * total, 0.0)
    column = lax.broadcasted_iota(jnp.int32, old.shape, 1) + left
    extra = jnp.where(column >= HALO, 2.0 * new - old, 0.0)
    extra_above = hop(extra[FR - 8 :].astype(jnp.bfloat16), 1).astype(jnp.float32)
    extra = jnp.concatenate([extra_above, extra], 0)

    shifted = own_dual + SIGMA_STEP * analyze(extra)
    squares = lax.all_gather((shifted * shifted).astype(jnp.bfloat16), "cube")
    norms = jnp.sqrt(jnp.sum(squares.astype(jnp.float32), 0))
    dual_part = (shifted * (RADIUS / jnp.maximum(norms, RADIUS))).astype(jnp.bfloat16)
    own_part = jnp.concatenate([dual_part, total[None, :, HALO:].astype(jnp.bfloat16)], 0)
    parts = lax.all_to_all(jnp.broadcast_to(own_part, (DP,) + own_part.shape), "dp", 0, 0)
    updated, dual_next = finished(parts, own_rows)
    return (updated[None], dual_next[:, None])


def solution(mesh):
    return jax.shard_map(
        on_device,
        mesh=mesh,
        in_specs=(
            P("cube", "facet", None),
            P(None, "cube", "facet", None),
            P("cube", ("facet", "dp"), None, None),
            P("cube", ("facet", "dp"), None),
            P("cube", ("facet", "dp")),
            P("cube", ("facet", "dp")),
            P("cube", ("facet", "dp")),
        ),
        out_specs=(P("cube", "facet", None), P(None, "cube", "facet", None)),
        check_vma=False,
    )
```

```python
import functools
import math

import jax
import jax.numpy as jnp
import numpy as np
from jax import lax
from jax.experimental import pallas as pl
from jax.experimental.pallas import tpu as pltpu
from jax.sharding import PartitionSpec as P

LOWPASS = (
    0.2303778133088964,
    0.7148465705529155,
    0.6308807679298587,
    -0.027983769416859854,
    -0.18703481171909309,
    0.030841381835560764,
    0.0328830116668852,
    -0.010597401785069032,
)
HIGHPASS = (
    -0.010597401785069032,
    -0.0328830116668852,
    0.030841381835560764,
    0.18703481171909309,
    -0.027983769416859854,
    -0.6308807679298587,
    0.7148465705529155,
    -0.2303778133088964,
)
TAU_STEP = 0.5
SIGMA_STEP = 0.5
RADIUS = 3.0

W = 2560
TILE = 16
FR = 48
BLK = 64
PER = FR // TILE
Q = 20
R = 128
DP = 4
PART = W // DP
HALO = 128
SPAN = PART + HALO
CHUNKS = W // 64
UNROLL = 16
VMEM_LIMIT = 60 * 1024 * 1024
NORM = 1.0 / math.sqrt(W)
C1, C2 = math.cos(2 * math.pi / 5), math.cos(4 * math.pi / 5)
S1, S2 = math.sin(2 * math.pi / 5), math.sin(4 * math.pi / 5)


def tables():
    x = np.arange(W).reshape(R, Q).T
    angles = (x[:, :, None] * np.arange(R)[None, None, :] % W) * (2.0 * math.pi / W)
    table = np.concatenate([np.cos(angles), -np.sin(angles)], -1).astype(jnp.bfloat16)
    return table


def constants():
    table = tables()
    return np.concatenate([table.reshape(Q * R, 2 * R), column_filters().reshape(-1, 2 * HALO)])


def flipped_table():
    return tables().transpose(0, 2, 1).reshape(2 * Q * R, R)


def column_filters():
    band = np.zeros((2 * HALO, 2 * HALO), np.float32)
    for b, taps in enumerate((LOWPASS, HIGHPASS)):
        for k in range(8):
            j = np.arange(HALO)
            band[HALO + j - k, HALO * b + j] = taps[k]
    leading = band.astype(jnp.bfloat16)
    rest = (band - leading.astype(np.float32)).astype(jnp.bfloat16)
    return np.stack([leading, rest])


def times_i(value, sign):
    re, im = value
    return (-im, re) if sign > 0 else (im, -re)


def plus(u, v):
    return (u[0] + v[0], u[1] + v[1])


def minus(u, v):
    return (u[0] - v[0], u[1] - v[1])


def dft4(x, sign):
    a, b = plus(x[0], x[2]), minus(x[0], x[2])
    c, d = plus(x[1], x[3]), times_i(minus(x[1], x[3]), sign)
    return [plus(a, c), plus(b, d), minus(a, c), minus(b, d)]


def dft5(x, sign):
    t1, t2 = plus(x[1], x[4]), plus(x[2], x[3])
    t3, t4 = minus(x[1], x[4]), minus(x[2], x[3])
    m1 = tuple(z + C1 * u + C2 * v for z, u, v in zip(x[0], t1, t2))
    m2 = tuple(z + C2 * u + C1 * v for z, u, v in zip(x[0], t1, t2))
    n1 = times_i(tuple(S1 * u + S2 * v for u, v in zip(t3, t4)), sign)
    n2 = times_i(tuple(S2 * u - S1 * v for u, v in zip(t3, t4)), sign)
    return [plus(x[0], plus(t1, t2)), plus(m1, n1), plus(m2, n2), minus(m2, n2), minus(m1, n1)]


def dft20(x, sign):
    columns = [dft4([x[(5 * a + 4 * b) % 20] for a in range(4)], sign) for b in range(5)]
    out = [None] * 20
    for c in range(4):
        line = dft5([columns[b][c] for b in range(5)], sign)
        for e in range(5):
            out[(5 * c + 16 * e) % 20] = line[e]
    return out


def residue_order():
    y = lax.broadcasted_iota(jnp.int32, (PART, 128), 0)
    group = ((y.astype(jnp.float32) + 0.5) * (1.0 / Q)).astype(jnp.int32)
    target = (y - Q * group) * 32 + group
    lane = lax.broadcasted_iota(jnp.int32, (PART, 128), 1)
    tiles = [jnp.where(target == lane + 128 * j, 1.0, 0.0) for j in range(PART // 128)]
    return jnp.concatenate(tiles, 1).astype(jnp.bfloat16)


def natural_order():
    row = lax.broadcasted_iota(jnp.int32, (PART, 128), 0)
    tiles = []
    for j in range(PART // 128):
        y = lax.broadcasted_iota(jnp.int32, (1, 128), 1) + 128 * j
        group = ((y.astype(jnp.float32) + 0.5) * (1.0 / Q)).astype(jnp.int32)
        tiles.append(jnp.where(row == (y - Q * group) * 32 + group, 1.0, 0.0))
    return jnp.concatenate(tiles, 1).astype(jnp.bfloat16)


def add_blocks(base, start, slot, live, weights, payload_ref, spec_ref, grad_ref, list_ref):
    lane = lax.broadcasted_iota(jnp.int32, (1, 128), 1)
    half = lane & 63

    def collect(b, count):
        place = slot(b) - base
        list_ref[count] = b
        return count + jnp.where((place >= 0) & (place < PER), 1, 0)

    count = lax.fori_loop(0, live, collect, 0)
    for u in range(UNROLL):
        list_ref[count + u] = list_ref[0]
    slot_lane = lax.broadcasted_iota(jnp.int32, (1, 128), 1)
    ones = jnp.ones((128, 128), jnp.bfloat16)

    def blocks(step, carry):
        places = [step * UNROLL + u for u in range(UNROLL)]
        numbers = [list_ref[place] for place in places]
        picked = [
            jnp.where(slot_lane == jnp.where(place < count, b, -1), weights, 0.0)
            for place, b in zip(places, numbers)
        ]
        factors = jnp.dot(
            jnp.concatenate(picked, 0).astype(jnp.bfloat16), ones, preferred_element_type=jnp.float32
        )
        found = []
        for u, b in enumerate(numbers):
            chunk, offset = start(b)
            tile = jnp.clip(slot(b) - base, 0, PER - 1)
            rows = pl.ds(pl.multiple_of(tile * TILE, TILE), TILE)
            first = pltpu.roll(spec_ref[chunk, rows, :].astype(jnp.float32), (128 - offset) & 127, 1)
            second = pltpu.roll(spec_ref[chunk + 1, rows, :].astype(jnp.float32), 64 - offset, 1)
            model = jnp.where(half < 64 - offset, first, second)
            misfit = factors[TILE * u : TILE * (u + 1)] * (
                model - payload_ref[b].astype(jnp.float32)
            )
            lower = jnp.where(half >= offset, pltpu.roll(misfit, offset, 1), 0.0)
            upper = jnp.where(half < offset, pltpu.roll(misfit, 64 + offset, 1), 0.0)
            found.append((chunk, rows, lower, upper))
        for chunk, rows, lower, upper in found:
            grad_ref[chunk, rows, :] += lower
            grad_ref[chunk + 1, rows, :] += upper
        return carry

    lax.fori_loop(0, (count + UNROLL - 1) // UNROLL, blocks, 0)


def columns_back(part, rows, dual_ref, filters, rows_ref):
    tiles = SPAN // HALO + 1
    blocks = []
    for j in range(tiles):
        place = (PART // HALO) * part - 1 + j
        inside = (place >= 0) & (place < W // HALO)
        columns = pl.ds(pl.multiple_of(jnp.clip(place, 0, W // HALO - 1) * HALO, HALO), HALO)
        for a in range(2):
            pair = jnp.concatenate([dual_ref[2 * a + b, :rows, columns] for b in range(2)], 1)
            blocks.append(jnp.where(inside, pair, jnp.zeros_like(pair)))
    stacked = jnp.concatenate(blocks, 0)
    across = sum(
        lax.dot_general(
            stacked, filters(i), (((1,), (1,)), ((), ())), preferred_element_type=jnp.float32
        )
        for i in range(2)
    )
    for j in range(tiles - 1):
        for a in range(2):
            here, right = [across[rows * (2 * i + a) : rows * (2 * i + a + 1)] for i in (j, j + 1)]
            rows_ref[a, 8 : 8 + rows, HALO * j : HALO * (j + 1)] = (
                here[:, HALO:] + right[:, :HALO]
            )


def rows_back(first, count, tile, rows_ref):
    value = 0.0
    for a, taps in enumerate((LOWPASS, HIGHPASS)):
        for k in range(8):
            value = value + taps[k] * rows_ref[a, 8 + first + k : 8 + first + k + count, tile]
    return value


def fill_message(part, starts, slots, live, weights, dual_ref, filters_ref, rows_ref, out_ref):
    rows_ref[:, :8, :] = jnp.zeros((2, 8, SPAN), jnp.float32)
    columns_back(
        part,
        TILE,
        dual_ref,
        lambda i: filters_ref[2 * HALO * i : 2 * HALO * (i + 1)],
        rows_ref,
    )
    for i in range(SPAN // HALO // 2):
        pair = [rows_back(-8, 8, pl.ds(HALO * (2 * i + j), HALO), rows_ref) for j in range(2)]
        out_ref[1 + i] = jnp.concatenate(pair, 0).astype(jnp.bfloat16)
    row = lax.broadcasted_iota(jnp.int32, (TILE, BLK), 0)
    numbers = jnp.where(row == 0, starts >> 6, starts & 63)
    numbers = jnp.where(row == 2, slots, numbers)
    numbers = jnp.where(row == 3, live, numbers)
    out_ref[0] = jnp.concatenate([weights, numbers.astype(jnp.float32)], 1).astype(jnp.bfloat16)


def synthesis(part_ref, message_ref, dual_ref, constants_ref, synth_ref, rows_ref):
    columns_back(
        part_ref[0],
        FR,
        dual_ref,
        lambda i: constants_ref[Q * R + 2 * HALO * i : Q * R + 2 * HALO * (i + 1)],
        rows_ref,
    )
    rows_ref[:, 8 + FR :, :] = jnp.zeros((2, 8, SPAN), jnp.float32)
    for j in range(SPAN // HALO):
        tile = pl.ds(HALO * j, HALO)
        synth_ref[:, tile] = rows_back(0, FR, tile, rows_ref)
        below = message_ref[1 + j // 2].astype(jnp.float32)
        synth_ref[FR - 8 :, tile] += below[8 * (j % 2) : 8 * (j % 2) + 8]


def own_pass(
    part_ref,
    starts_hbm,
    slots_hbm,
    live_hbm,
    weight_hbm,
    payload_hbm,
    table_hbm,
    pixels_hbm,
    dual_hbm,
    spec_ref,
    own_ref,
    message_ref,
    starts_ref,
    slots_ref,
    live_ref,
    list_ref,
    starts_vec,
    slots_vec,
    dual_ref,
    filters_ref,
    rows_ref,
    weight_ref,
    payload_ref,
    table_ref,
    pixels_ref,
    order_ref,
    re_ref,
    im_ref,
    grad_ref,
    sems,
):
    pairs = [
        (pixels_hbm, pixels_ref),
        (table_hbm.at[pl.ds(0, Q * R), :], table_ref),
        (weight_hbm, weight_ref),
        (payload_hbm, payload_ref),
        (starts_hbm, starts_ref),
        (slots_hbm, slots_ref),
        (live_hbm, live_ref),
        (starts_hbm, starts_vec),
        (slots_hbm, slots_vec),
        (dual_hbm.at[:, :TILE, :], dual_ref),
        (table_hbm.at[pl.ds(Q * R, 4 * HALO), :], filters_ref),
    ]
    copies = [pltpu.make_async_copy(s, d, sems.at[i]) for i, (s, d) in enumerate(pairs)]
    for copy in copies:
        copy.start()
    lane = lax.broadcasted_iota(jnp.int32, (1, 128), 1)
    low = lane < 64
    quarter = lane >> 5

    order_ref[...] = residue_order()
    copies[0].wait()
    stacked = jnp.concatenate(
        [pixels_ref[:, PART * g : PART * (g + 1)].astype(jnp.bfloat16) for g in range(4)], 0
    )
    sorted_rows = jnp.dot(stacked, order_ref[...], preferred_element_type=jnp.float32)
    copies[1].wait()
    for j in range(5):
        tiles = [sorted_rows[FR * g : FR * (g + 1), 128 * j : 128 * (j + 1)] for g in range(4)]
        for p in range(4):
            turned = [
                tiles[g] if g == p else pltpu.roll(tiles[g], (32 * (g - p)) % 128, 1)
                for g in range(4)
            ]
            rows = turned[3]
            for g in range(3):
                rows = jnp.where(quarter == g, turned[g], rows)
            q = 4 * j + p
            partial = jnp.dot(
                rows.astype(jnp.bfloat16),
                table_ref[R * q : R * (q + 1)],
                preferred_element_type=jnp.float32,
            )
            re_ref[q] = partial[:, :R]
            im_ref[q] = partial[:, R:]

    def forward(i, carry):
        for j in range(2):
            rows = pl.ds(pl.multiple_of(i * TILE + 8 * j, 8), 8)
            spectrum = dft20([(re_ref[q, rows, :], im_ref[q, rows, :]) for q in range(Q)], -1)
            for k, (re, im) in enumerate(spectrum):
                re, im = re * NORM, im * NORM
                grad_ref[2 * k, rows, :] = jnp.where(low, re, pltpu.roll(im, 64, 1))
                grad_ref[2 * k + 1, rows, :] = jnp.where(low, pltpu.roll(re, 64, 1), im)
        return carry

    lax.fori_loop(0, FR // TILE, forward, 0)
    spec_ref[:CHUNKS] = grad_ref[:CHUNKS].astype(jnp.bfloat16)
    spec_ref[CHUNKS] = spec_ref[0]
    grad_ref[...] = jnp.zeros_like(grad_ref)
    for copy in copies[2:]:
        copy.wait()
    blank = jnp.zeros((TILE, 128 - BLK), jnp.float32)
    weights = weight_ref[...].astype(jnp.float32)
    fill_message(
        part_ref[0],
        starts_vec[...],
        slots_vec[...],
        live_ref[0, 0],
        weights,
        dual_ref,
        filters_ref,
        rows_ref,
        message_ref,
    )
    weights = jnp.concatenate([weights, blank], 1)
    add_blocks(
        PER,
        lambda b: (starts_ref[0, b] >> 6, starts_ref[0, b] & 63),
        lambda b: slots_ref[0, b],
        live_ref[0, 0],
        weights,
        payload_ref,
        spec_ref,
        grad_ref,
        list_ref,
    )
    own_ref[...] = grad_ref[...].astype(jnp.bfloat16)


def below_pass(
    message_hbm,
    payload_hbm,
    spec_hbm,
    own_hbm,
    table_hbm,
    out_ref,
    list_ref,
    numbers_ref,
    vector_ref,
    message_ref,
    payload_ref,
    spec_ref,
    own_ref,
    grad_ref,
    table_ref,
    order_ref,
    re_ref,
    im_ref,
    tile_ref,
    sems,
):
    pairs = [
        (message_hbm.at[0], message_ref),
        (spec_hbm, spec_ref),
        (own_hbm, own_ref),
        (payload_hbm, payload_ref),
        (table_hbm, table_ref),
    ]
    copies = [pltpu.make_async_copy(s, d, sems.at[i]) for i, (s, d) in enumerate(pairs)]
    for copy in copies:
        copy.start()
    lane = lax.broadcasted_iota(jnp.int32, (1, 128), 1)
    low = lane < 64
    quarter = lane >> 5
    copies[0].wait()
    meta = message_ref[...].astype(jnp.float32)
    vector_ref[...] = meta[:8].astype(jnp.int32)
    read = pltpu.make_async_copy(vector_ref, numbers_ref, sems.at[5])
    read.start()
    order_ref[...] = natural_order()
    read.wait()
    for copy in copies[1:4]:
        copy.wait()
    grad_ref[...] = own_ref[...].astype(jnp.float32)
    add_blocks(
        0,
        lambda b: (numbers_ref[0, BLK + b], numbers_ref[1, BLK + b]),
        lambda b: numbers_ref[2, BLK + b],
        numbers_ref[3, BLK],
        jnp.where(low, meta, 0.0),
        payload_ref,
        spec_ref,
        grad_ref,
        list_ref,
    )
    grad_ref[0] += grad_ref[CHUNKS]

    def backward(i, carry):
        rows = pl.ds(pl.multiple_of(i * 8, 8), 8)
        spectrum = []
        for k in range(Q):
            even, odd = grad_ref[2 * k, rows, :], grad_ref[2 * k + 1, rows, :]
            spectrum.append(
                (
                    jnp.where(low, even, pltpu.roll(odd, 64, 1)),
                    jnp.where(low, pltpu.roll(even, 64, 1), odd),
                )
            )
        for q, (re, im) in enumerate(dft20(spectrum, 1)):
            re_ref[q, rows, :] = re * NORM
            im_ref[q, rows, :] = im * NORM
        return carry

    lax.fori_loop(0, FR // 8, backward, 0)
    copies[4].wait()
    for j in range(5):
        places = [[] for _ in range(4)]
        for p in range(4):
            q = 4 * j + p
            pair = jnp.concatenate([re_ref[q], im_ref[q]], 1).astype(jnp.bfloat16)
            rows = jnp.dot(
                pair, table_ref[2 * R * q : 2 * R * (q + 1)], preferred_element_type=jnp.float32
            )
            for g in range(4):
                places[g].append(rows if g == p else pltpu.roll(rows, (32 * (p - g)) % 128, 1))
        for g in range(4):
            tile = places[g][3]
            for p in range(3):
                tile = jnp.where(quarter == p, places[g][p], tile)
            tile_ref[5 * g + j] = tile
    mixed = jnp.concatenate(
        [jnp.concatenate([tile_ref[5 * g + j] for j in range(5)], 1) for g in range(4)], 0
    ).astype(jnp.bfloat16)
    natural = jnp.dot(
        mixed, order_ref[...], preferred_element_type=jnp.float32
    ).astype(jnp.bfloat16)
    out_ref[0, :, :HALO] = jnp.zeros((FR, HALO), jnp.bfloat16)
    for g in range(4):
        rows = natural[FR * g : FR * (g + 1)]
        out_ref[g, :, HALO:] = rows
        if g < 3:
            out_ref[g + 1, :, :HALO] = rows[:, PART - HALO :]


HBM_SPEC = pl.BlockSpec(memory_space=pltpu.HBM)
SMEM_SPEC = pl.BlockSpec(memory_space=pltpu.SMEM)
VMEM_SPEC = pl.BlockSpec(memory_space=pltpu.VMEM)
SPECTRA = jax.ShapeDtypeStruct((CHUNKS + 1, FR, 128), jnp.bfloat16)


TABLE = pltpu.VMEM((Q * R, 2 * R), jnp.bfloat16)
PARAMS = pltpu.CompilerParams(vmem_limit_bytes=VMEM_LIMIT)
COST = pl.CostEstimate(flops=2 * 10**9, bytes_accessed=4 * 10**6, transcendentals=0)


def synthesized(part, received, dual, table):
    return pl.pallas_call(
        synthesis,
        out_shape=jax.ShapeDtypeStruct((FR, SPAN), jnp.float32),
        in_specs=[SMEM_SPEC] + [VMEM_SPEC] * 3,
        out_specs=VMEM_SPEC,
        scratch_shapes=[pltpu.VMEM((2, FR + 16, SPAN), jnp.float32)],
        compiler_params=pltpu.CompilerParams(vmem_limit_bytes=16 * 1024 * 1024),
        name="synthesized",
    )(part, received, dual, table)


def own_spectra(part, starts, slots, live, weights, payload, table, pixels, dual):
    return pl.pallas_call(
        own_pass,
        out_shape=(
            SPECTRA,
            SPECTRA,
            jax.ShapeDtypeStruct((1 + SPAN // HALO // 2, TILE, 128), jnp.bfloat16),
        ),
        in_specs=[SMEM_SPEC] + [HBM_SPEC] * 8,
        out_specs=(VMEM_SPEC,) * 3,
        scratch_shapes=[
            pltpu.SMEM((1, BLK), jnp.int32),
            pltpu.SMEM((1, BLK), jnp.int32),
            pltpu.SMEM((1, 1), jnp.int32),
            pltpu.SMEM((BLK + UNROLL,), jnp.int32),
            pltpu.VMEM((1, BLK), jnp.int32),
            pltpu.VMEM((1, BLK), jnp.int32),
            pltpu.VMEM((4, TILE, W), jnp.bfloat16),
            pltpu.VMEM((4 * HALO, 2 * HALO), jnp.bfloat16),
            pltpu.VMEM((2, 8 + TILE, SPAN), jnp.float32),
            pltpu.VMEM((TILE, BLK), jnp.bfloat16),
            pltpu.VMEM((BLK, TILE, 128), jnp.bfloat16),
            TABLE,
            pltpu.VMEM((FR, W), jnp.float32),
            pltpu.VMEM((PART, PART), jnp.bfloat16),
            pltpu.VMEM((Q, FR, R), jnp.float32),
            pltpu.VMEM((Q, FR, R), jnp.float32),
            pltpu.VMEM((CHUNKS + 1, FR, 128), jnp.float32),
            pltpu.SemaphoreType.DMA((11,)),
        ],
        compiler_params=PARAMS,
        cost_estimate=COST,
        name="own_spectra",
    )(part, starts, slots, live, weights, payload, table, pixels, dual)


def gradient_parts(received, payload, spectra, own, table):
    return pl.pallas_call(
        below_pass,
        out_shape=jax.ShapeDtypeStruct((DP, FR, SPAN), jnp.bfloat16),
        in_specs=[HBM_SPEC] * 5,
        out_specs=VMEM_SPEC,
        scratch_shapes=[
            pltpu.SMEM((BLK + UNROLL,), jnp.int32),
            pltpu.SMEM((8, 128), jnp.int32),
            pltpu.VMEM((8, 128), jnp.int32),
            pltpu.VMEM((TILE, 128), jnp.bfloat16),
            pltpu.VMEM((BLK, TILE, 128), jnp.bfloat16),
            pltpu.VMEM((CHUNKS + 1, FR, 128), jnp.bfloat16),
            pltpu.VMEM((CHUNKS + 1, FR, 128), jnp.bfloat16),
            pltpu.VMEM((CHUNKS + 1, FR, 128), jnp.float32),
            pltpu.VMEM((2 * Q * R, R), jnp.bfloat16),
            pltpu.VMEM((PART, PART), jnp.bfloat16),
            pltpu.VMEM((Q, FR, R), jnp.float32),
            pltpu.VMEM((Q, FR, R), jnp.float32),
            pltpu.VMEM((Q, FR, R), jnp.float32),
            pltpu.SemaphoreType.DMA((6,)),
        ],
        compiler_params=PARAMS,
        cost_estimate=COST,
        name="gradient_parts",
    )(received, payload, spectra, own, table)


def finish(parts_ref, pixels_ref, image_hbm, dual_hbm, image_ref, sems):
    copies = []
    for d in range(DP):
        tile = pl.ds(PART * d, PART)
        copies.append(
            pltpu.make_async_copy(
                parts_ref.at[d, pl.ds(0, 4)], dual_hbm.at[:, :, tile], sems.at[d]
            )
        )
        copies[-1].start()
    for d in range(DP):
        tile = pl.ds(PART * d, PART)
        descent = parts_ref[d, 4].astype(jnp.float32)
        image_ref[:, tile] = jnp.maximum(pixels_ref[:, tile] - TAU_STEP * descent, 0.0)
    copies.append(pltpu.make_async_copy(image_ref, image_hbm, sems.at[DP]))
    copies[-1].start()
    for copy in copies:
        copy.wait()


def finished(parts, pixels):
    return pl.pallas_call(
        finish,
        out_shape=(
            jax.ShapeDtypeStruct((FR, W), jnp.float32),
            jax.ShapeDtypeStruct((4, FR, W), jnp.bfloat16),
        ),
        in_specs=[VMEM_SPEC] * 2,
        out_specs=(HBM_SPEC,) * 2,
        scratch_shapes=[pltpu.VMEM((FR, W), jnp.float32), pltpu.SemaphoreType.DMA((DP + 1,))],
        compiler_params=pltpu.CompilerParams(vmem_limit_bytes=16 * 1024 * 1024),
        name="finished",
    )(parts, pixels)


def hop(block, distance):
    devices = range(lax.axis_size("facet"))
    route = [(i - distance, i) for i in devices if i - distance in devices]
    return lax.ppermute(block, "facet", route)


def gathered_sum(parts):
    mixed = lax.all_to_all(parts, "dp", 0, 0)
    return jnp.sum(mixed.astype(jnp.float32), 0)


def analyze(extra, first, count):
    subbands = []
    for row_taps in (LOWPASS, HIGHPASS):
        filtered = sum(row_taps[k] * extra[first - k : first - k + count] for k in range(8))
        for col_taps in (LOWPASS, HIGHPASS):
            subbands.append(
                sum(col_taps[k] * filtered[:, HALO - k : HALO - k + PART] for k in range(8))
            )
    return jnp.stack(subbands)


def on_device(image, dual, payload, vis_weight, freq_start, tile_slot, live):
    table, flipped = jnp.asarray(constants()), jnp.asarray(flipped_table())
    position = lax.axis_index("dp")
    own_rows = image[0]
    part = position[None]
    weights = vis_weight[0].T
    payload_below = hop(payload[0], -1)
    left = position * PART
    own_dual = lax.dynamic_slice_in_dim(dual[:, 0], left, PART, 2).astype(jnp.float32)
    old = lax.dynamic_slice_in_dim(
        jnp.pad(own_rows, ((0, 0), (HALO, 0))), left, SPAN, 1
    )

    spectra, own, sent = own_spectra(
        part, freq_start, tile_slot, live, weights, payload[0], table, own_rows, dual[:, 0]
    )
    received = hop(sent, -1)
    terms = gradient_parts(received, payload_below, spectra, own, flipped)
    terms, received = lax.optimization_barrier((terms, received))
    synth = synthesized(part, received, dual[:, 0], table)
    total = gathered_sum(terms) + synth
    new = jnp.maximum(old - TAU_STEP * total, 0.0)
    column = lax.broadcasted_iota(jnp.int32, old.shape, 1) + left
    extra = jnp.where(column >= HALO, 2.0 * new - old, 0.0)
    extra_above = hop(extra[FR - 8 :].astype(jnp.bfloat16), 1).astype(jnp.float32)
    lower = own_dual[:, 8:] + SIGMA_STEP * analyze(extra, 8, FR - 8)
    lower, extra_above = lax.optimization_barrier((lower, extra_above))
    top = jnp.concatenate([extra_above, extra[:8]], 0)
    upper = own_dual[:, :8] + SIGMA_STEP * analyze(top, 8, 8)
    shifted = jnp.concatenate([upper, lower], 1)
    squares = lax.all_gather((shifted * shifted).astype(jnp.bfloat16), "cube")
    norms = jnp.sqrt(jnp.sum(squares.astype(jnp.float32), 0))
    dual_part = (shifted * (RADIUS / jnp.maximum(norms, RADIUS))).astype(jnp.bfloat16)
    own_part = jnp.concatenate([dual_part, total[None, :, HALO:].astype(jnp.bfloat16)], 0)
    parts = lax.all_to_all(jnp.broadcast_to(own_part, (DP,) + own_part.shape), "dp", 0, 0)
    updated, dual_next = finished(parts, own_rows)
    return (updated[None], dual_next[:, None])


def solution(mesh):
    return jax.shard_map(
        on_device,
        mesh=mesh,
        in_specs=(
            P("cube", "facet", None),
            P(None, "cube", "facet", None),
            P("cube", ("facet", "dp"), None, None),
            P("cube", ("facet", "dp"), None),
            P("cube", ("facet", "dp")),
            P("cube", ("facet", "dp")),
            P("cube", ("facet", "dp")),
        ),
        out_specs=(P("cube", "facet", None), P(None, "cube", "facet", None)),
        check_vma=False,
    )
```

```python
import functools
import math

import jax
import jax.numpy as jnp
import numpy as np
from jax import lax
from jax.experimental import pallas as pl
from jax.experimental.pallas import tpu as pltpu
from jax.sharding import PartitionSpec as P

LOWPASS = (
    0.2303778133088964,
    0.7148465705529155,
    0.6308807679298587,
    -0.027983769416859854,
    -0.18703481171909309,
    0.030841381835560764,
    0.0328830116668852,
    -0.010597401785069032,
)
HIGHPASS = (
    -0.010597401785069032,
    -0.0328830116668852,
    0.030841381835560764,
    0.18703481171909309,
    -0.027983769416859854,
    -0.6308807679298587,
    0.7148465705529155,
    -0.2303778133088964,
)
TAU_STEP = 0.5
SIGMA_STEP = 0.5
RADIUS = 3.0

W = 2560
TILE = 16
FR = 48
BLK = 64
PER = FR // TILE
Q = 20
R = 128
DP = 4
PART = W // DP
HALO = 128
SPAN = PART + HALO
CHUNKS = W // 64
UNROLL = 16
VMEM_LIMIT = 60 * 1024 * 1024
NORM = 1.0 / math.sqrt(W)
C1, C2 = math.cos(2 * math.pi / 5), math.cos(4 * math.pi / 5)
S1, S2 = math.sin(2 * math.pi / 5), math.sin(4 * math.pi / 5)


def tables():
    x = np.arange(W).reshape(R, Q).T
    angles = (x[:, :, None] * np.arange(R)[None, None, :] % W) * (2.0 * math.pi / W)
    table = np.concatenate([np.cos(angles), -np.sin(angles)], -1).astype(jnp.bfloat16)
    return table


def constants():
    table = tables()
    return np.concatenate([table.reshape(Q * R, 2 * R), column_filters().reshape(-1, 2 * HALO)])


def flipped_table():
    return tables().transpose(0, 2, 1).reshape(2 * Q * R, R)


def column_filters():
    band = np.zeros((2 * HALO, 2 * HALO), np.float32)
    for b, taps in enumerate((LOWPASS, HIGHPASS)):
        for k in range(8):
            j = np.arange(HALO)
            band[HALO + j - k, HALO * b + j] = taps[k]
    leading = band.astype(jnp.bfloat16)
    rest = (band - leading.astype(np.float32)).astype(jnp.bfloat16)
    return np.stack([leading, rest])


def times_i(value, sign):
    re, im = value
    return (-im, re) if sign > 0 else (im, -re)


def plus(u, v):
    return (u[0] + v[0], u[1] + v[1])


def minus(u, v):
    return (u[0] - v[0], u[1] - v[1])


def dft4(x, sign):
    a, b = plus(x[0], x[2]), minus(x[0], x[2])
    c, d = plus(x[1], x[3]), times_i(minus(x[1], x[3]), sign)
    return [plus(a, c), plus(b, d), minus(a, c), minus(b, d)]


def dft5(x, sign):
    t1, t2 = plus(x[1], x[4]), plus(x[2], x[3])
    t3, t4 = minus(x[1], x[4]), minus(x[2], x[3])
    m1 = tuple(z + C1 * u + C2 * v for z, u, v in zip(x[0], t1, t2))
    m2 = tuple(z + C2 * u + C1 * v for z, u, v in zip(x[0], t1, t2))
    n1 = times_i(tuple(S1 * u + S2 * v for u, v in zip(t3, t4)), sign)
    n2 = times_i(tuple(S2 * u - S1 * v for u, v in zip(t3, t4)), sign)
    return [plus(x[0], plus(t1, t2)), plus(m1, n1), plus(m2, n2), minus(m2, n2), minus(m1, n1)]


def dft20(x, sign):
    columns = [dft4([x[(5 * a + 4 * b) % 20] for a in range(4)], sign) for b in range(5)]
    out = [None] * 20
    for c in range(4):
        line = dft5([columns[b][c] for b in range(5)], sign)
        for e in range(5):
            out[(5 * c + 16 * e) % 20] = line[e]
    return out


def residue_order():
    y = lax.broadcasted_iota(jnp.int32, (PART, 128), 0)
    group = ((y.astype(jnp.float32) + 0.5) * (1.0 / Q)).astype(jnp.int32)
    target = (y - Q * group) * 32 + group
    lane = lax.broadcasted_iota(jnp.int32, (PART, 128), 1)
    tiles = [jnp.where(target == lane + 128 * j, 1.0, 0.0) for j in range(PART // 128)]
    return jnp.concatenate(tiles, 1).astype(jnp.bfloat16)


def natural_order():
    row = lax.broadcasted_iota(jnp.int32, (PART, 128), 0)
    tiles = []
    for j in range(PART // 128):
        y = lax.broadcasted_iota(jnp.int32, (1, 128), 1) + 128 * j
        group = ((y.astype(jnp.float32) + 0.5) * (1.0 / Q)).astype(jnp.int32)
        tiles.append(jnp.where(row == (y - Q * group) * 32 + group, 1.0, 0.0))
    return jnp.concatenate(tiles, 1).astype(jnp.bfloat16)


def add_blocks(base, start, slot, live, weights, payload_ref, spec_ref, grad_ref, list_ref):
    lane = lax.broadcasted_iota(jnp.int32, (1, 128), 1)
    half = lane & 63

    def collect(b, count):
        place = slot(b) - base
        list_ref[count] = b
        return count + jnp.where((place >= 0) & (place < PER), 1, 0)

    count = lax.fori_loop(0, live, collect, 0)
    for u in range(UNROLL):
        list_ref[count + u] = list_ref[0]
    slot_lane = lax.broadcasted_iota(jnp.int32, (1, 128), 1)
    ones = jnp.ones((128, 128), jnp.bfloat16)

    def blocks(step, carry):
        places = [step * UNROLL + u for u in range(UNROLL)]
        numbers = [list_ref[place] for place in places]
        picked = [
            jnp.where(slot_lane == jnp.where(place < count, b, -1), weights, 0.0)
            for place, b in zip(places, numbers)
        ]
        factors = jnp.dot(
            jnp.concatenate(picked, 0).astype(jnp.bfloat16), ones, preferred_element_type=jnp.float32
        )
        found = []
        for u, b in enumerate(numbers):
            chunk, offset = start(b)
            tile = jnp.clip(slot(b) - base, 0, PER - 1)
            rows = pl.ds(pl.multiple_of(tile * TILE, TILE), TILE)
            first = pltpu.roll(spec_ref[chunk, rows, :].astype(jnp.float32), (128 - offset) & 127, 1)
            second = pltpu.roll(spec_ref[chunk + 1, rows, :].astype(jnp.float32), 64 - offset, 1)
            model = jnp.where(half < 64 - offset, first, second)
            misfit = factors[TILE * u : TILE * (u + 1)] * (
                model - payload_ref[b].astype(jnp.float32)
            )
            lower = jnp.where(half >= offset, pltpu.roll(misfit, offset, 1), 0.0)
            upper = jnp.where(half < offset, pltpu.roll(misfit, 64 + offset, 1), 0.0)
            found.append((chunk, rows, lower, upper))
        for chunk, rows, lower, upper in found:
            grad_ref[chunk, rows, :] += lower
            grad_ref[chunk + 1, rows, :] += upper
        return carry

    lax.fori_loop(0, (count + UNROLL - 1) // UNROLL, blocks, 0)


def columns_back(part, rows, dual_ref, filters, rows_ref):
    tiles = SPAN // HALO + 1
    blocks = []
    for j in range(tiles):
        place = (PART // HALO) * part - 1 + j
        inside = (place >= 0) & (place < W // HALO)
        columns = pl.ds(pl.multiple_of(jnp.clip(place, 0, W // HALO - 1) * HALO, HALO), HALO)
        for a in range(2):
            pair = jnp.concatenate([dual_ref[2 * a + b, :rows, columns] for b in range(2)], 1)
            blocks.append(jnp.where(inside, pair, jnp.zeros_like(pair)))
    stacked = jnp.concatenate(blocks, 0)
    across = sum(
        lax.dot_general(
            stacked, filters(i), (((1,), (1,)), ((), ())), preferred_element_type=jnp.float32
        )
        for i in range(2)
    )
    for j in range(tiles - 1):
        for a in range(2):
            here, right = [across[rows * (2 * i + a) : rows * (2 * i + a + 1)] for i in (j, j + 1)]
            rows_ref[a, 8 : 8 + rows, HALO * j : HALO * (j + 1)] = (
                here[:, HALO:] + right[:, :HALO]
            )


def rows_back(first, count, tile, rows_ref):
    value = 0.0
    for a, taps in enumerate((LOWPASS, HIGHPASS)):
        for k in range(8):
            value = value + taps[k] * rows_ref[a, 8 + first + k : 8 + first + k + count, tile]
    return value


def write_message(
    part_ref,
    starts_hbm,
    slots_hbm,
    live_hbm,
    weight_hbm,
    dual_hbm,
    filters_hbm,
    out_ref,
    starts_ref,
    slots_ref,
    live_ref,
    weight_ref,
    dual_ref,
    filters_ref,
    rows_ref,
    sems,
):
    pairs = [
        (dual_hbm.at[:, :TILE, :], dual_ref),
        (filters_hbm.at[pl.ds(Q * R, 4 * HALO), :], filters_ref),
        (starts_hbm, starts_ref),
        (slots_hbm, slots_ref),
        (live_hbm, live_ref),
        (weight_hbm, weight_ref),
    ]
    copies = [pltpu.make_async_copy(s, d, sems.at[i]) for i, (s, d) in enumerate(pairs)]
    for copy in copies:
        copy.start()
    rows_ref[:, :8, :] = jnp.zeros((2, 8, SPAN), jnp.float32)
    copies[0].wait()
    copies[1].wait()
    columns_back(
        part_ref[0],
        TILE,
        dual_ref,
        lambda i: filters_ref[2 * HALO * i : 2 * HALO * (i + 1)],
        rows_ref,
    )
    for i in range(SPAN // HALO // 2):
        pair = [rows_back(-8, 8, pl.ds(HALO * (2 * i + j), HALO), rows_ref) for j in range(2)]
        out_ref[1 + i] = jnp.concatenate(pair, 0).astype(jnp.bfloat16)
    for copy in copies[2:]:
        copy.wait()
    row = lax.broadcasted_iota(jnp.int32, (TILE, BLK), 0)
    starts = starts_ref[...]
    numbers = jnp.where(row == 0, starts >> 6, starts & 63)
    numbers = jnp.where(row == 2, slots_ref[...], numbers)
    numbers = jnp.where(row == 3, live_ref[0, 0], numbers)
    out_ref[0] = jnp.concatenate(
        [weight_ref[...].astype(jnp.float32), numbers.astype(jnp.float32)], 1
    ).astype(jnp.bfloat16)


def synthesis(part_ref, message_ref, dual_ref, constants_ref, synth_ref, rows_ref):
    columns_back(
        part_ref[0],
        FR,
        dual_ref,
        lambda i: constants_ref[Q * R + 2 * HALO * i : Q * R + 2 * HALO * (i + 1)],
        rows_ref,
    )
    rows_ref[:, 8 + FR :, :] = jnp.zeros((2, 8, SPAN), jnp.float32)
    for j in range(SPAN // HALO):
        tile = pl.ds(HALO * j, HALO)
        synth_ref[:, tile] = rows_back(0, FR, tile, rows_ref)
        below = message_ref[1 + j // 2].astype(jnp.float32)
        synth_ref[FR - 8 :, tile] += below[8 * (j % 2) : 8 * (j % 2) + 8]


def own_pass(
    starts_hbm,
    slots_hbm,
    live_hbm,
    weight_hbm,
    payload_hbm,
    table_hbm,
    pixels_hbm,
    spec_ref,
    own_ref,
    starts_ref,
    slots_ref,
    live_ref,
    list_ref,
    weight_ref,
    payload_ref,
    table_ref,
    pixels_ref,
    order_ref,
    re_ref,
    im_ref,
    grad_ref,
    sems,
):
    pairs = [
        (pixels_hbm, pixels_ref),
        (table_hbm.at[pl.ds(0, Q * R), :], table_ref),
        (weight_hbm, weight_ref),
        (payload_hbm, payload_ref),
        (starts_hbm, starts_ref),
        (slots_hbm, slots_ref),
        (live_hbm, live_ref),
    ]
    copies = [pltpu.make_async_copy(s, d, sems.at[i]) for i, (s, d) in enumerate(pairs)]
    for copy in copies:
        copy.start()
    lane = lax.broadcasted_iota(jnp.int32, (1, 128), 1)
    low = lane < 64
    quarter = lane >> 5

    order_ref[...] = residue_order()
    copies[0].wait()
    stacked = jnp.concatenate(
        [pixels_ref[:, PART * g : PART * (g + 1)].astype(jnp.bfloat16) for g in range(4)], 0
    )
    sorted_rows = jnp.dot(stacked, order_ref[...], preferred_element_type=jnp.float32)
    copies[1].wait()
    for j in range(5):
        tiles = [sorted_rows[FR * g : FR * (g + 1), 128 * j : 128 * (j + 1)] for g in range(4)]
        for p in range(4):
            turned = [
                tiles[g] if g == p else pltpu.roll(tiles[g], (32 * (g - p)) % 128, 1)
                for g in range(4)
            ]
            rows = turned[3]
            for g in range(3):
                rows = jnp.where(quarter == g, turned[g], rows)
            q = 4 * j + p
            partial = jnp.dot(
                rows.astype(jnp.bfloat16),
                table_ref[R * q : R * (q + 1)],
                preferred_element_type=jnp.float32,
            )
            re_ref[q] = partial[:, :R]
            im_ref[q] = partial[:, R:]

    def forward(i, carry):
        for j in range(2):
            rows = pl.ds(pl.multiple_of(i * TILE + 8 * j, 8), 8)
            spectrum = dft20([(re_ref[q, rows, :], im_ref[q, rows, :]) for q in range(Q)], -1)
            for k, (re, im) in enumerate(spectrum):
                re, im = re * NORM, im * NORM
                grad_ref[2 * k, rows, :] = jnp.where(low, re, pltpu.roll(im, 64, 1))
                grad_ref[2 * k + 1, rows, :] = jnp.where(low, pltpu.roll(re, 64, 1), im)
        return carry

    lax.fori_loop(0, FR // TILE, forward, 0)
    spec_ref[:CHUNKS] = grad_ref[:CHUNKS].astype(jnp.bfloat16)
    spec_ref[CHUNKS] = spec_ref[0]
    grad_ref[...] = jnp.zeros_like(grad_ref)
    for copy in copies[2:]:
        copy.wait()
    blank = jnp.zeros((TILE, 128 - BLK), jnp.float32)
    weights = jnp.concatenate([weight_ref[...].astype(jnp.float32), blank], 1)
    add_blocks(
        PER,
        lambda b: (starts_ref[0, b] >> 6, starts_ref[0, b] & 63),
        lambda b: slots_ref[0, b],
        live_ref[0, 0],
        weights,
        payload_ref,
        spec_ref,
        grad_ref,
        list_ref,
    )
    own_ref[...] = grad_ref[...].astype(jnp.bfloat16)


def below_pass(
    message_hbm,
    payload_hbm,
    spec_hbm,
    own_hbm,
    table_hbm,
    out_ref,
    list_ref,
    numbers_ref,
    vector_ref,
    message_ref,
    payload_ref,
    spec_ref,
    own_ref,
    grad_ref,
    table_ref,
    order_ref,
    re_ref,
    im_ref,
    tile_ref,
    sems,
):
    pairs = [
        (message_hbm.at[0], message_ref),
        (spec_hbm, spec_ref),
        (own_hbm, own_ref),
        (payload_hbm, payload_ref),
        (table_hbm, table_ref),
    ]
    copies = [pltpu.make_async_copy(s, d, sems.at[i]) for i, (s, d) in enumerate(pairs)]
    for copy in copies:
        copy.start()
    lane = lax.broadcasted_iota(jnp.int32, (1, 128), 1)
    low = lane < 64
    quarter = lane >> 5
    copies[0].wait()
    meta = message_ref[...].astype(jnp.float32)
    vector_ref[...] = meta[:8].astype(jnp.int32)
    read = pltpu.make_async_copy(vector_ref, numbers_ref, sems.at[5])
    read.start()
    order_ref[...] = natural_order()
    read.wait()
    for copy in copies[1:4]:
        copy.wait()
    grad_ref[...] = own_ref[...].astype(jnp.float32)
    add_blocks(
        0,
        lambda b: (numbers_ref[0, BLK + b], numbers_ref[1, BLK + b]),
        lambda b: numbers_ref[2, BLK + b],
        numbers_ref[3, BLK],
        jnp.where(low, meta, 0.0),
        payload_ref,
        spec_ref,
        grad_ref,
        list_ref,
    )
    grad_ref[0] += grad_ref[CHUNKS]

    def backward(i, carry):
        rows = pl.ds(pl.multiple_of(i * 8, 8), 8)
        spectrum = []
        for k in range(Q):
            even, odd = grad_ref[2 * k, rows, :], grad_ref[2 * k + 1, rows, :]
            spectrum.append(
                (
                    jnp.where(low, even, pltpu.roll(odd, 64, 1)),
                    jnp.where(low, pltpu.roll(even, 64, 1), odd),
                )
            )
        for q, (re, im) in enumerate(dft20(spectrum, 1)):
            re_ref[q, rows, :] = re * NORM
            im_ref[q, rows, :] = im * NORM
        return carry

    lax.fori_loop(0, FR // 8, backward, 0)
    copies[4].wait()
    for j in range(5):
        places = [[] for _ in range(4)]
        for p in range(4):
            q = 4 * j + p
            pair = jnp.concatenate([re_ref[q], im_ref[q]], 1).astype(jnp.bfloat16)
            rows = jnp.dot(
                pair, table_ref[2 * R * q : 2 * R * (q + 1)], preferred_element_type=jnp.float32
            )
            for g in range(4):
                places[g].append(rows if g == p else pltpu.roll(rows, (32 * (p - g)) % 128, 1))
        for g in range(4):
            tile = places[g][3]
            for p in range(3):
                tile = jnp.where(quarter == p, places[g][p], tile)
            tile_ref[5 * g + j] = tile
    mixed = jnp.concatenate(
        [jnp.concatenate([tile_ref[5 * g + j] for j in range(5)], 1) for g in range(4)], 0
    ).astype(jnp.bfloat16)
    natural = jnp.dot(
        mixed, order_ref[...], preferred_element_type=jnp.float32
    ).astype(jnp.bfloat16)
    out_ref[0, :, :HALO] = jnp.zeros((FR, HALO), jnp.bfloat16)
    for g in range(4):
        rows = natural[FR * g : FR * (g + 1)]
        out_ref[g, :, HALO:] = rows
        if g < 3:
            out_ref[g + 1, :, :HALO] = rows[:, PART - HALO :]


HBM_SPEC = pl.BlockSpec(memory_space=pltpu.HBM)
SMEM_SPEC = pl.BlockSpec(memory_space=pltpu.SMEM)
VMEM_SPEC = pl.BlockSpec(memory_space=pltpu.VMEM)
SPECTRA = jax.ShapeDtypeStruct((CHUNKS + 1, FR, 128), jnp.bfloat16)


TABLE = pltpu.VMEM((Q * R, 2 * R), jnp.bfloat16)
PARAMS = pltpu.CompilerParams(vmem_limit_bytes=VMEM_LIMIT)
COST = pl.CostEstimate(flops=2 * 10**9, bytes_accessed=4 * 10**6, transcendentals=0)


def message(part, starts, slots, live, weights, dual, table):
    return pl.pallas_call(
        write_message,
        out_shape=jax.ShapeDtypeStruct((1 + SPAN // HALO // 2, TILE, 128), jnp.bfloat16),
        in_specs=[SMEM_SPEC] + [HBM_SPEC] * 6,
        out_specs=VMEM_SPEC,
        scratch_shapes=[
            pltpu.VMEM((1, BLK), jnp.int32),
            pltpu.VMEM((1, BLK), jnp.int32),
            pltpu.SMEM((1, 1), jnp.int32),
            pltpu.VMEM((TILE, BLK), jnp.bfloat16),
            pltpu.VMEM((4, TILE, W), jnp.bfloat16),
            pltpu.VMEM((4 * HALO, 2 * HALO), jnp.bfloat16),
            pltpu.VMEM((2, 8 + TILE, SPAN), jnp.float32),
            pltpu.SemaphoreType.DMA((6,)),
        ],
        compiler_params=PARAMS,
        name="message",
    )(part, starts, slots, live, weights, dual, table)


def synthesized(part, received, dual, table):
    return pl.pallas_call(
        synthesis,
        out_shape=jax.ShapeDtypeStruct((FR, SPAN), jnp.float32),
        in_specs=[SMEM_SPEC] + [VMEM_SPEC] * 3,
        out_specs=VMEM_SPEC,
        scratch_shapes=[pltpu.VMEM((2, FR + 16, SPAN), jnp.float32)],
        compiler_params=pltpu.CompilerParams(vmem_limit_bytes=16 * 1024 * 1024),
        name="synthesized",
    )(part, received, dual, table)


def own_spectra(starts, slots, live, weights, payload, table, pixels):
    return pl.pallas_call(
        own_pass,
        out_shape=(SPECTRA, SPECTRA),
        in_specs=[HBM_SPEC] * 7,
        out_specs=(VMEM_SPEC,) * 2,
        scratch_shapes=[
            pltpu.SMEM((1, BLK), jnp.int32),
            pltpu.SMEM((1, BLK), jnp.int32),
            pltpu.SMEM((1, 1), jnp.int32),
            pltpu.SMEM((BLK + UNROLL,), jnp.int32),
            pltpu.VMEM((TILE, BLK), jnp.bfloat16),
            pltpu.VMEM((BLK, TILE, 128), jnp.bfloat16),
            TABLE,
            pltpu.VMEM((FR, W), jnp.float32),
            pltpu.VMEM((PART, PART), jnp.bfloat16),
            pltpu.VMEM((Q, FR, R), jnp.float32),
            pltpu.VMEM((Q, FR, R), jnp.float32),
            pltpu.VMEM((CHUNKS + 1, FR, 128), jnp.float32),
            pltpu.SemaphoreType.DMA((7,)),
        ],
        compiler_params=PARAMS,
        cost_estimate=COST,
        name="own_spectra",
    )(starts, slots, live, weights, payload, table, pixels)


def gradient_parts(received, payload, spectra, own, table):
    return pl.pallas_call(
        below_pass,
        out_shape=jax.ShapeDtypeStruct((DP, FR, SPAN), jnp.bfloat16),
        in_specs=[HBM_SPEC] * 5,
        out_specs=VMEM_SPEC,
        scratch_shapes=[
            pltpu.SMEM((BLK + UNROLL,), jnp.int32),
            pltpu.SMEM((8, 128), jnp.int32),
            pltpu.VMEM((8, 128), jnp.int32),
            pltpu.VMEM((TILE, 128), jnp.bfloat16),
            pltpu.VMEM((BLK, TILE, 128), jnp.bfloat16),
            pltpu.VMEM((CHUNKS + 1, FR, 128), jnp.bfloat16),
            pltpu.VMEM((CHUNKS + 1, FR, 128), jnp.bfloat16),
            pltpu.VMEM((CHUNKS + 1, FR, 128), jnp.float32),
            pltpu.VMEM((2 * Q * R, R), jnp.bfloat16),
            pltpu.VMEM((PART, PART), jnp.bfloat16),
            pltpu.VMEM((Q, FR, R), jnp.float32),
            pltpu.VMEM((Q, FR, R), jnp.float32),
            pltpu.VMEM((Q, FR, R), jnp.float32),
            pltpu.SemaphoreType.DMA((6,)),
        ],
        compiler_params=PARAMS,
        cost_estimate=COST,
        name="gradient_parts",
    )(received, payload, spectra, own, table)


def finish(parts_ref, pixels_ref, image_hbm, dual_hbm, image_ref, sems):
    copies = []
    for d in range(DP):
        tile = pl.ds(PART * d, PART)
        copies.append(
            pltpu.make_async_copy(
                parts_ref.at[d, pl.ds(0, 4)], dual_hbm.at[:, :, tile], sems.at[d]
            )
        )
        copies[-1].start()
    for d in range(DP):
        tile = pl.ds(PART * d, PART)
        descent = parts_ref[d, 4].astype(jnp.float32)
        image_ref[:, tile] = jnp.maximum(pixels_ref[:, tile] - TAU_STEP * descent, 0.0)
    copies.append(pltpu.make_async_copy(image_ref, image_hbm, sems.at[DP]))
    copies[-1].start()
    for copy in copies:
        copy.wait()


def finished(parts, pixels):
    return pl.pallas_call(
        finish,
        out_shape=(
            jax.ShapeDtypeStruct((FR, W), jnp.float32),
            jax.ShapeDtypeStruct((4, FR, W), jnp.bfloat16),
        ),
        in_specs=[VMEM_SPEC] * 2,
        out_specs=(HBM_SPEC,) * 2,
        scratch_shapes=[pltpu.VMEM((FR, W), jnp.float32), pltpu.SemaphoreType.DMA((DP + 1,))],
        compiler_params=pltpu.CompilerParams(vmem_limit_bytes=16 * 1024 * 1024),
        name="finished",
    )(parts, pixels)


def hop(block, distance):
    devices = range(lax.axis_size("facet"))
    route = [(i - distance, i) for i in devices if i - distance in devices]
    return lax.ppermute(block, "facet", route)


def gathered_sum(parts):
    mixed = lax.all_to_all(parts, "dp", 0, 0)
    return jnp.sum(mixed.astype(jnp.float32), 0)


def analyze(extra, first, count):
    subbands = []
    for row_taps in (LOWPASS, HIGHPASS):
        filtered = sum(row_taps[k] * extra[first - k : first - k + count] for k in range(8))
        for col_taps in (LOWPASS, HIGHPASS):
            subbands.append(
                sum(col_taps[k] * filtered[:, HALO - k : HALO - k + PART] for k in range(8))
            )
    return jnp.stack(subbands)


def on_device(image, dual, payload, vis_weight, freq_start, tile_slot, live):
    table, flipped = jnp.asarray(constants()), jnp.asarray(flipped_table())
    position = lax.axis_index("dp")
    own_rows = image[0]
    part = position[None]
    weights = vis_weight[0].T
    payload_below = hop(payload[0], -1)
    received = hop(
        message(part, freq_start, tile_slot, live, weights, dual[:, 0], table), -1
    )

    left = position * PART
    own_dual = lax.dynamic_slice_in_dim(dual[:, 0], left, PART, 2).astype(jnp.float32)
    old = lax.dynamic_slice_in_dim(
        jnp.pad(own_rows, ((0, 0), (HALO, 0))), left, SPAN, 1
    )

    spectra, own = own_spectra(
        freq_start, tile_slot, live, weights, payload[0], table, own_rows
    )
    terms = gradient_parts(received, payload_below, spectra, own, flipped)
    terms, received = lax.optimization_barrier((terms, received))
    synth = synthesized(part, received, dual[:, 0], table)
    total = gathered_sum(terms) + synth
    new = jnp.maximum(old - TAU_STEP * total, 0.0)
    column = lax.broadcasted_iota(jnp.int32, old.shape, 1) + left
    extra = jnp.where(column >= HALO, 2.0 * new - old, 0.0)
    extra_above = hop(extra[FR - 8 :].astype(jnp.bfloat16), 1).astype(jnp.float32)
    lower = own_dual[:, 8:] + SIGMA_STEP * analyze(extra, 8, FR - 8)
    lower, extra_above = lax.optimization_barrier((lower, extra_above))
    top = jnp.concatenate([extra_above, extra[:8]], 0)
    upper = own_dual[:, :8] + SIGMA_STEP * analyze(top, 8, 8)
    shifted = jnp.concatenate([upper, lower], 1)
    squares = lax.all_gather((shifted * shifted).astype(jnp.bfloat16), "cube")
    norms = jnp.sqrt(jnp.sum(squares.astype(jnp.float32), 0))
    dual_part = (shifted * (RADIUS / jnp.maximum(norms, RADIUS))).astype(jnp.bfloat16)
    own_part = jnp.concatenate([dual_part, total[None, :, HALO:].astype(jnp.bfloat16)], 0)
    parts = lax.all_to_all(jnp.broadcast_to(own_part, (DP,) + own_part.shape), "dp", 0, 0)
    updated, dual_next = finished(parts, own_rows)
    return (updated[None], dual_next[:, None])


def solution(mesh):
    return jax.shard_map(
        on_device,
        mesh=mesh,
        in_specs=(
            P("cube", "facet", None),
            P(None, "cube", "facet", None),
            P("cube", ("facet", "dp"), None, None),
            P("cube", ("facet", "dp"), None),
            P("cube", ("facet", "dp")),
            P("cube", ("facet", "dp")),
            P("cube", ("facet", "dp")),
        ),
        out_specs=(P("cube", "facet", None), P(None, "cube", "facet", None)),
        check_vma=False,
    )
```

```python
import functools
import math

import jax
import jax.numpy as jnp
import numpy as np
from jax import lax
from jax.experimental import pallas as pl
from jax.experimental.pallas import tpu as pltpu
from jax.sharding import PartitionSpec as P

LOWPASS = (
    0.2303778133088964,
    0.7148465705529155,
    0.6308807679298587,
    -0.027983769416859854,
    -0.18703481171909309,
    0.030841381835560764,
    0.0328830116668852,
    -0.010597401785069032,
)
HIGHPASS = (
    -0.010597401785069032,
    -0.0328830116668852,
    0.030841381835560764,
    0.18703481171909309,
    -0.027983769416859854,
    -0.6308807679298587,
    0.7148465705529155,
    -0.2303778133088964,
)
TAU_STEP = 0.5
SIGMA_STEP = 0.5
RADIUS = 3.0

W = 2560
TILE = 16
FR = 48
BLK = 64
PER = FR // TILE
Q = 20
R = 128
DP = 4
PART = W // DP
HALO = 128
SPAN = PART + HALO
CHUNKS = W // 64
UNROLL = 16
VMEM_LIMIT = 60 * 1024 * 1024
NORM = 1.0 / math.sqrt(W)
C1, C2 = math.cos(2 * math.pi / 5), math.cos(4 * math.pi / 5)
S1, S2 = math.sin(2 * math.pi / 5), math.sin(4 * math.pi / 5)


def tables():
    x = np.arange(W).reshape(R, Q).T
    angles = (x[:, :, None] * np.arange(R)[None, None, :] % W) * (2.0 * math.pi / W)
    table = np.concatenate([np.cos(angles), -np.sin(angles)], -1).astype(jnp.bfloat16)
    return table


def constants():
    table = tables()
    return np.concatenate([table.reshape(Q * R, 2 * R), column_filters().reshape(-1, 2 * HALO)])


def flipped_table():
    return tables().transpose(0, 2, 1).reshape(2 * Q * R, R)


def column_filters():
    band = np.zeros((2 * HALO, 2 * HALO), np.float32)
    for b, taps in enumerate((LOWPASS, HIGHPASS)):
        for k in range(8):
            j = np.arange(HALO)
            band[HALO + j - k, HALO * b + j] = taps[k]
    leading = band.astype(jnp.bfloat16)
    rest = (band - leading.astype(np.float32)).astype(jnp.bfloat16)
    return np.stack([leading, rest])


def times_i(value, sign):
    re, im = value
    return (-im, re) if sign > 0 else (im, -re)


def plus(u, v):
    return (u[0] + v[0], u[1] + v[1])


def minus(u, v):
    return (u[0] - v[0], u[1] - v[1])


def dft4(x, sign):
    a, b = plus(x[0], x[2]), minus(x[0], x[2])
    c, d = plus(x[1], x[3]), times_i(minus(x[1], x[3]), sign)
    return [plus(a, c), plus(b, d), minus(a, c), minus(b, d)]


def dft5(x, sign):
    t1, t2 = plus(x[1], x[4]), plus(x[2], x[3])
    t3, t4 = minus(x[1], x[4]), minus(x[2], x[3])
    m1 = tuple(z + C1 * u + C2 * v for z, u, v in zip(x[0], t1, t2))
    m2 = tuple(z + C2 * u + C1 * v for z, u, v in zip(x[0], t1, t2))
    n1 = times_i(tuple(S1 * u + S2 * v for u, v in zip(t3, t4)), sign)
    n2 = times_i(tuple(S2 * u - S1 * v for u, v in zip(t3, t4)), sign)
    return [plus(x[0], plus(t1, t2)), plus(m1, n1), plus(m2, n2), minus(m2, n2), minus(m1, n1)]


def dft20(x, sign):
    columns = [dft4([x[(5 * a + 4 * b) % 20] for a in range(4)], sign) for b in range(5)]
    out = [None] * 20
    for c in range(4):
        line = dft5([columns[b][c] for b in range(5)], sign)
        for e in range(5):
            out[(5 * c + 16 * e) % 20] = line[e]
    return out


def residue_order():
    y = lax.broadcasted_iota(jnp.int32, (PART, 128), 0)
    group = ((y.astype(jnp.float32) + 0.5) * (1.0 / Q)).astype(jnp.int32)
    target = (y - Q * group) * 32 + group
    lane = lax.broadcasted_iota(jnp.int32, (PART, 128), 1)
    tiles = [jnp.where(target == lane + 128 * j, 1.0, 0.0) for j in range(PART // 128)]
    return jnp.concatenate(tiles, 1).astype(jnp.bfloat16)


def natural_order():
    row = lax.broadcasted_iota(jnp.int32, (PART, 128), 0)
    tiles = []
    for j in range(PART // 128):
        y = lax.broadcasted_iota(jnp.int32, (1, 128), 1) + 128 * j
        group = ((y.astype(jnp.float32) + 0.5) * (1.0 / Q)).astype(jnp.int32)
        tiles.append(jnp.where(row == (y - Q * group) * 32 + group, 1.0, 0.0))
    return jnp.concatenate(tiles, 1).astype(jnp.bfloat16)


def add_blocks(base, start, slot, live, weights, payload_ref, spec_ref, grad_ref, list_ref):
    lane = lax.broadcasted_iota(jnp.int32, (1, 128), 1)
    half = lane & 63

    def collect(b, count):
        place = slot(b) - base
        list_ref[count] = b
        return count + jnp.where((place >= 0) & (place < PER), 1, 0)

    count = lax.fori_loop(0, live, collect, 0)
    for u in range(UNROLL):
        list_ref[count + u] = list_ref[0]
    slot_lane = lax.broadcasted_iota(jnp.int32, (1, 128), 1)
    ones = jnp.ones((128, 128), jnp.bfloat16)

    def blocks(step, carry):
        places = [step * UNROLL + u for u in range(UNROLL)]
        numbers = [list_ref[place] for place in places]
        picked = [
            jnp.where(slot_lane == jnp.where(place < count, b, -1), weights, 0.0)
            for place, b in zip(places, numbers)
        ]
        factors = jnp.dot(
            jnp.concatenate(picked, 0).astype(jnp.bfloat16), ones, preferred_element_type=jnp.float32
        )
        found = []
        for u, b in enumerate(numbers):
            chunk, offset = start(b)
            tile = jnp.clip(slot(b) - base, 0, PER - 1)
            rows = pl.ds(pl.multiple_of(tile * TILE, TILE), TILE)
            first = pltpu.roll(spec_ref[chunk, rows, :].astype(jnp.float32), (128 - offset) & 127, 1)
            second = pltpu.roll(spec_ref[chunk + 1, rows, :].astype(jnp.float32), 64 - offset, 1)
            model = jnp.where(half < 64 - offset, first, second)
            misfit = factors[TILE * u : TILE * (u + 1)] * (
                model - payload_ref[b].astype(jnp.float32)
            )
            lower = jnp.where(half >= offset, pltpu.roll(misfit, offset, 1), 0.0)
            upper = jnp.where(half < offset, pltpu.roll(misfit, 64 + offset, 1), 0.0)
            found.append((chunk, rows, lower, upper))
        for chunk, rows, lower, upper in found:
            grad_ref[chunk, rows, :] += lower
            grad_ref[chunk + 1, rows, :] += upper
        return carry

    lax.fori_loop(0, (count + UNROLL - 1) // UNROLL, blocks, 0)


def columns_back(part, rows, dual_ref, filters, rows_ref):
    tiles = SPAN // HALO + 1
    blocks = []
    for j in range(tiles):
        place = (PART // HALO) * part - 1 + j
        inside = (place >= 0) & (place < W // HALO)
        columns = pl.ds(pl.multiple_of(jnp.clip(place, 0, W // HALO - 1) * HALO, HALO), HALO)
        for a in range(2):
            pair = jnp.concatenate([dual_ref[2 * a + b, :rows, columns] for b in range(2)], 1)
            blocks.append(jnp.where(inside, pair, jnp.zeros_like(pair)))
    stacked = jnp.concatenate(blocks, 0)
    across = sum(
        lax.dot_general(
            stacked, filters(i), (((1,), (1,)), ((), ())), preferred_element_type=jnp.float32
        )
        for i in range(2)
    )
    for j in range(tiles - 1):
        for a in range(2):
            here, right = [across[rows * (2 * i + a) : rows * (2 * i + a + 1)] for i in (j, j + 1)]
            rows_ref[a, 8 : 8 + rows, HALO * j : HALO * (j + 1)] = (
                here[:, HALO:] + right[:, :HALO]
            )


def rows_back(first, count, tile, rows_ref):
    value = 0.0
    for a, taps in enumerate((LOWPASS, HIGHPASS)):
        for k in range(8):
            value = value + taps[k] * rows_ref[a, 8 + first + k : 8 + first + k + count, tile]
    return value


def fill_message(part, starts, slots, live, weights, dual_ref, filters_ref, rows_ref, out_ref):
    rows_ref[:, :8, :] = jnp.zeros((2, 8, SPAN), jnp.float32)
    columns_back(
        part,
        TILE,
        dual_ref,
        lambda i: filters_ref[2 * HALO * i : 2 * HALO * (i + 1)],
        rows_ref,
    )
    for i in range(SPAN // HALO // 2):
        pair = [rows_back(-8, 8, pl.ds(HALO * (2 * i + j), HALO), rows_ref) for j in range(2)]
        out_ref[1 + i] = jnp.concatenate(pair, 0).astype(jnp.bfloat16)
    row = lax.broadcasted_iota(jnp.int32, (TILE, BLK), 0)
    numbers = jnp.where(row == 0, starts >> 6, starts & 63)
    numbers = jnp.where(row == 2, slots, numbers)
    numbers = jnp.where(row == 3, live, numbers)
    out_ref[0] = jnp.concatenate([weights, numbers.astype(jnp.float32)], 1).astype(jnp.bfloat16)


def synthesis(part_ref, message_ref, dual_ref, constants_ref, synth_ref, rows_ref):
    columns_back(
        part_ref[0],
        FR,
        dual_ref,
        lambda i: constants_ref[Q * R + 2 * HALO * i : Q * R + 2 * HALO * (i + 1)],
        rows_ref,
    )
    rows_ref[:, 8 + FR :, :] = jnp.zeros((2, 8, SPAN), jnp.float32)
    for j in range(SPAN // HALO):
        tile = pl.ds(HALO * j, HALO)
        synth_ref[:, tile] = rows_back(0, FR, tile, rows_ref)
        below = message_ref[1 + j // 2].astype(jnp.float32)
        synth_ref[FR - 8 :, tile] += below[8 * (j % 2) : 8 * (j % 2) + 8]


def own_pass(
    part_ref,
    starts_hbm,
    slots_hbm,
    live_hbm,
    weight_hbm,
    payload_hbm,
    table_hbm,
    pixels_hbm,
    dual_hbm,
    spec_ref,
    own_ref,
    message_ref,
    starts_ref,
    slots_ref,
    live_ref,
    list_ref,
    starts_vec,
    slots_vec,
    dual_ref,
    filters_ref,
    rows_ref,
    weight_ref,
    payload_ref,
    table_ref,
    pixels_ref,
    order_ref,
    re_ref,
    im_ref,
    grad_ref,
    sems,
):
    pairs = [
        (pixels_hbm, pixels_ref),
        (table_hbm.at[pl.ds(0, Q * R), :], table_ref),
        (weight_hbm, weight_ref),
        (payload_hbm, payload_ref),
        (starts_hbm, starts_ref),
        (slots_hbm, slots_ref),
        (live_hbm, live_ref),
        (starts_hbm, starts_vec),
        (slots_hbm, slots_vec),
        (dual_hbm.at[:, :TILE, :], dual_ref),
        (table_hbm.at[pl.ds(Q * R, 4 * HALO), :], filters_ref),
    ]
    copies = [pltpu.make_async_copy(s, d, sems.at[i]) for i, (s, d) in enumerate(pairs)]
    for copy in copies:
        copy.start()
    lane = lax.broadcasted_iota(jnp.int32, (1, 128), 1)
    low = lane < 64
    quarter = lane >> 5

    order_ref[...] = residue_order()
    copies[0].wait()
    stacked = jnp.concatenate(
        [pixels_ref[:, PART * g : PART * (g + 1)].astype(jnp.bfloat16) for g in range(4)], 0
    )
    sorted_rows = jnp.dot(stacked, order_ref[...], preferred_element_type=jnp.float32)
    copies[1].wait()
    for j in range(5):
        tiles = [sorted_rows[FR * g : FR * (g + 1), 128 * j : 128 * (j + 1)] for g in range(4)]
        for p in range(4):
            turned = [
                tiles[g] if g == p else pltpu.roll(tiles[g], (32 * (g - p)) % 128, 1)
                for g in range(4)
            ]
            rows = turned[3]
            for g in range(3):
                rows = jnp.where(quarter == g, turned[g], rows)
            q = 4 * j + p
            partial = jnp.dot(
                rows.astype(jnp.bfloat16),
                table_ref[R * q : R * (q + 1)],
                preferred_element_type=jnp.float32,
            )
            re_ref[q] = partial[:, :R]
            im_ref[q] = partial[:, R:]

    def forward(i, carry):
        for j in range(2):
            rows = pl.ds(pl.multiple_of(i * TILE + 8 * j, 8), 8)
            spectrum = dft20([(re_ref[q, rows, :], im_ref[q, rows, :]) for q in range(Q)], -1)
            for k, (re, im) in enumerate(spectrum):
                re, im = re * NORM, im * NORM
                grad_ref[2 * k, rows, :] = jnp.where(low, re, pltpu.roll(im, 64, 1))
                grad_ref[2 * k + 1, rows, :] = jnp.where(low, pltpu.roll(re, 64, 1), im)
        return carry

    lax.fori_loop(0, FR // TILE, forward, 0)
    spec_ref[:CHUNKS] = grad_ref[:CHUNKS].astype(jnp.bfloat16)
    spec_ref[CHUNKS] = spec_ref[0]
    grad_ref[...] = jnp.zeros_like(grad_ref)
    for copy in copies[2:]:
        copy.wait()
    blank = jnp.zeros((TILE, 128 - BLK), jnp.float32)
    weights = weight_ref[...].astype(jnp.float32)
    fill_message(
        part_ref[0],
        starts_vec[...],
        slots_vec[...],
        live_ref[0, 0],
        weights,
        dual_ref,
        filters_ref,
        rows_ref,
        message_ref,
    )
    weights = jnp.concatenate([weights, blank], 1)
    add_blocks(
        PER,
        lambda b: (starts_ref[0, b] >> 6, starts_ref[0, b] & 63),
        lambda b: slots_ref[0, b],
        live_ref[0, 0],
        weights,
        payload_ref,
        spec_ref,
        grad_ref,
        list_ref,
    )
    own_ref[...] = grad_ref[...].astype(jnp.bfloat16)


def below_pass(
    message_hbm,
    payload_hbm,
    spec_hbm,
    own_hbm,
    table_hbm,
    out_ref,
    list_ref,
    numbers_ref,
    vector_ref,
    message_ref,
    payload_ref,
    spec_ref,
    own_ref,
    grad_ref,
    table_ref,
    order_ref,
    re_ref,
    im_ref,
    tile_ref,
    sems,
):
    pairs = [
        (message_hbm.at[0], message_ref),
        (spec_hbm, spec_ref),
        (own_hbm, own_ref),
        (payload_hbm, payload_ref),
        (table_hbm, table_ref),
    ]
    copies = [pltpu.make_async_copy(s, d, sems.at[i]) for i, (s, d) in enumerate(pairs)]
    for copy in copies:
        copy.start()
    lane = lax.broadcasted_iota(jnp.int32, (1, 128), 1)
    low = lane < 64
    quarter = lane >> 5
    copies[0].wait()
    meta = message_ref[...].astype(jnp.float32)
    vector_ref[...] = meta[:8].astype(jnp.int32)
    read = pltpu.make_async_copy(vector_ref, numbers_ref, sems.at[5])
    read.start()
    order_ref[...] = natural_order()
    read.wait()
    for copy in copies[1:4]:
        copy.wait()
    grad_ref[...] = own_ref[...].astype(jnp.float32)
    add_blocks(
        0,
        lambda b: (numbers_ref[0, BLK + b], numbers_ref[1, BLK + b]),
        lambda b: numbers_ref[2, BLK + b],
        numbers_ref[3, BLK],
        jnp.where(low, meta, 0.0),
        payload_ref,
        spec_ref,
        grad_ref,
        list_ref,
    )
    grad_ref[0] += grad_ref[CHUNKS]

    def backward(i, carry):
        rows = pl.ds(pl.multiple_of(i * 8, 8), 8)
        spectrum = []
        for k in range(Q):
            even, odd = grad_ref[2 * k, rows, :], grad_ref[2 * k + 1, rows, :]
            spectrum.append(
                (
                    jnp.where(low, even, pltpu.roll(odd, 64, 1)),
                    jnp.where(low, pltpu.roll(even, 64, 1), odd),
                )
            )
        for q, (re, im) in enumerate(dft20(spectrum, 1)):
            re_ref[q, rows, :] = re * NORM
            im_ref[q, rows, :] = im * NORM
        return carry

    lax.fori_loop(0, FR // 8, backward, 0)
    copies[4].wait()
    for j in range(5):
        places = [[] for _ in range(4)]
        for p in range(4):
            q = 4 * j + p
            pair = jnp.concatenate([re_ref[q], im_ref[q]], 1).astype(jnp.bfloat16)
            rows = jnp.dot(
                pair, table_ref[2 * R * q : 2 * R * (q + 1)], preferred_element_type=jnp.float32
            )
            for g in range(4):
                places[g].append(rows if g == p else pltpu.roll(rows, (32 * (p - g)) % 128, 1))
        for g in range(4):
            tile = places[g][3]
            for p in range(3):
                tile = jnp.where(quarter == p, places[g][p], tile)
            tile_ref[5 * g + j] = tile
    mixed = jnp.concatenate(
        [jnp.concatenate([tile_ref[5 * g + j] for j in range(5)], 1) for g in range(4)], 0
    ).astype(jnp.bfloat16)
    natural = jnp.dot(
        mixed, order_ref[...], preferred_element_type=jnp.float32
    ).astype(jnp.bfloat16)
    out_ref[0, :, :HALO] = jnp.zeros((FR, HALO), jnp.bfloat16)
    for g in range(4):
        rows = natural[FR * g : FR * (g + 1)]
        out_ref[g, :, HALO:] = rows
        if g < 3:
            out_ref[g + 1, :, :HALO] = rows[:, PART - HALO :]


HBM_SPEC = pl.BlockSpec(memory_space=pltpu.HBM)
SMEM_SPEC = pl.BlockSpec(memory_space=pltpu.SMEM)
VMEM_SPEC = pl.BlockSpec(memory_space=pltpu.VMEM)
SPECTRA = jax.ShapeDtypeStruct((CHUNKS + 1, FR, 128), jnp.bfloat16)


TABLE = pltpu.VMEM((Q * R, 2 * R), jnp.bfloat16)
PARAMS = pltpu.CompilerParams(vmem_limit_bytes=VMEM_LIMIT)
COST = pl.CostEstimate(flops=2 * 10**9, bytes_accessed=4 * 10**6, transcendentals=0)


def synthesized(part, received, dual, table):
    return pl.pallas_call(
        synthesis,
        out_shape=jax.ShapeDtypeStruct((FR, SPAN), jnp.float32),
        in_specs=[SMEM_SPEC] + [VMEM_SPEC] * 3,
        out_specs=VMEM_SPEC,
        scratch_shapes=[pltpu.VMEM((2, FR + 16, SPAN), jnp.float32)],
        compiler_params=pltpu.CompilerParams(vmem_limit_bytes=16 * 1024 * 1024),
        name="synthesized",
    )(part, received, dual, table)


def own_spectra(part, starts, slots, live, weights, payload, table, pixels, dual):
    return pl.pallas_call(
        own_pass,
        out_shape=(
            SPECTRA,
            SPECTRA,
            jax.ShapeDtypeStruct((1 + SPAN // HALO // 2, TILE, 128), jnp.bfloat16),
        ),
        in_specs=[SMEM_SPEC] + [HBM_SPEC] * 8,
        out_specs=(VMEM_SPEC,) * 3,
        scratch_shapes=[
            pltpu.SMEM((1, BLK), jnp.int32),
            pltpu.SMEM((1, BLK), jnp.int32),
            pltpu.SMEM((1, 1), jnp.int32),
            pltpu.SMEM((BLK + UNROLL,), jnp.int32),
            pltpu.VMEM((1, BLK), jnp.int32),
            pltpu.VMEM((1, BLK), jnp.int32),
            pltpu.VMEM((4, TILE, W), jnp.bfloat16),
            pltpu.VMEM((4 * HALO, 2 * HALO), jnp.bfloat16),
            pltpu.VMEM((2, 8 + TILE, SPAN), jnp.float32),
            pltpu.VMEM((TILE, BLK), jnp.bfloat16),
            pltpu.VMEM((BLK, TILE, 128), jnp.bfloat16),
            TABLE,
            pltpu.VMEM((FR, W), jnp.float32),
            pltpu.VMEM((PART, PART), jnp.bfloat16),
            pltpu.VMEM((Q, FR, R), jnp.float32),
            pltpu.VMEM((Q, FR, R), jnp.float32),
            pltpu.VMEM((CHUNKS + 1, FR, 128), jnp.float32),
            pltpu.SemaphoreType.DMA((11,)),
        ],
        compiler_params=PARAMS,
        cost_estimate=COST,
        name="own_spectra",
    )(part, starts, slots, live, weights, payload, table, pixels, dual)


def gradient_parts(received, payload, spectra, own, table):
    return pl.pallas_call(
        below_pass,
        out_shape=jax.ShapeDtypeStruct((DP, FR, SPAN), jnp.bfloat16),
        in_specs=[HBM_SPEC] * 5,
        out_specs=VMEM_SPEC,
        scratch_shapes=[
            pltpu.SMEM((BLK + UNROLL,), jnp.int32),
            pltpu.SMEM((8, 128), jnp.int32),
            pltpu.VMEM((8, 128), jnp.int32),
            pltpu.VMEM((TILE, 128), jnp.bfloat16),
            pltpu.VMEM((BLK, TILE, 128), jnp.bfloat16),
            pltpu.VMEM((CHUNKS + 1, FR, 128), jnp.bfloat16),
            pltpu.VMEM((CHUNKS + 1, FR, 128), jnp.bfloat16),
            pltpu.VMEM((CHUNKS + 1, FR, 128), jnp.float32),
            pltpu.VMEM((2 * Q * R, R), jnp.bfloat16),
            pltpu.VMEM((PART, PART), jnp.bfloat16),
            pltpu.VMEM((Q, FR, R), jnp.float32),
            pltpu.VMEM((Q, FR, R), jnp.float32),
            pltpu.VMEM((Q, FR, R), jnp.float32),
            pltpu.SemaphoreType.DMA((6,)),
        ],
        compiler_params=PARAMS,
        cost_estimate=COST,
        name="gradient_parts",
    )(received, payload, spectra, own, table)


def finish(parts_ref, pixels_ref, image_hbm, dual_hbm, image_ref, sems):
    copies = []
    for d in range(DP):
        tile = pl.ds(PART * d, PART)
        copies.append(
            pltpu.make_async_copy(
                parts_ref.at[d, pl.ds(0, 4)], dual_hbm.at[:, :, tile], sems.at[d]
            )
        )
        copies[-1].start()
    for d in range(DP):
        tile = pl.ds(PART * d, PART)
        descent = parts_ref[d, 4].astype(jnp.float32)
        image_ref[:, tile] = jnp.maximum(pixels_ref[:, tile] - TAU_STEP * descent, 0.0)
        copies.append(
            pltpu.make_async_copy(image_ref.at[:, tile], image_hbm.at[:, tile], sems.at[DP + d])
        )
        copies[-1].start()
    for copy in copies:
        copy.wait()


def finished(parts, pixels):
    return pl.pallas_call(
        finish,
        out_shape=(
            jax.ShapeDtypeStruct((FR, W), jnp.float32),
            jax.ShapeDtypeStruct((4, FR, W), jnp.bfloat16),
        ),
        in_specs=[VMEM_SPEC] * 2,
        out_specs=(HBM_SPEC,) * 2,
        scratch_shapes=[pltpu.VMEM((FR, W), jnp.float32), pltpu.SemaphoreType.DMA((2 * DP,))],
        compiler_params=pltpu.CompilerParams(vmem_limit_bytes=16 * 1024 * 1024),
        name="finished",
    )(parts, pixels)


def hop(block, distance):
    devices = range(lax.axis_size("facet"))
    route = [(i - distance, i) for i in devices if i - distance in devices]
    return lax.ppermute(block, "facet", route)


def gathered_sum(parts):
    mixed = lax.all_to_all(parts, "dp", 0, 0)
    return jnp.sum(mixed.astype(jnp.float32), 0)


def analyze(extra, first, count):
    subbands = []
    for row_taps in (LOWPASS, HIGHPASS):
        filtered = sum(row_taps[k] * extra[first - k : first - k + count] for k in range(8))
        for col_taps in (LOWPASS, HIGHPASS):
            subbands.append(
                sum(col_taps[k] * filtered[:, HALO - k : HALO - k + PART] for k in range(8))
            )
    return jnp.stack(subbands)


def on_device(image, dual, payload, vis_weight, freq_start, tile_slot, live):
    table, flipped = jnp.asarray(constants()), jnp.asarray(flipped_table())
    position = lax.axis_index("dp")
    own_rows = image[0]
    part = position[None]
    weights = vis_weight[0].T
    payload_below = hop(payload[0], -1)
    left = position * PART
    own_dual = lax.dynamic_slice_in_dim(dual[:, 0], left, PART, 2).astype(jnp.float32)
    old = lax.dynamic_slice_in_dim(
        jnp.pad(own_rows, ((0, 0), (HALO, 0))), left, SPAN, 1
    )

    spectra, own, sent = own_spectra(
        part, freq_start, tile_slot, live, weights, payload[0], table, own_rows, dual[:, 0]
    )
    received = hop(sent, -1)
    terms = gradient_parts(received, payload_below, spectra, own, flipped)
    terms, received = lax.optimization_barrier((terms, received))
    synth = synthesized(part, received, dual[:, 0], table)
    total = gathered_sum(terms) + synth
    new = jnp.maximum(old - TAU_STEP * total, 0.0)
    column = lax.broadcasted_iota(jnp.int32, old.shape, 1) + left
    extra = jnp.where(column >= HALO, 2.0 * new - old, 0.0)
    extra_above = hop(extra[FR - 8 :].astype(jnp.bfloat16), 1).astype(jnp.float32)
    lower = own_dual[:, 8:] + SIGMA_STEP * analyze(extra, 8, FR - 8)
    lower, extra_above = lax.optimization_barrier((lower, extra_above))
    top = jnp.concatenate([extra_above, extra[:8]], 0)
    upper = own_dual[:, :8] + SIGMA_STEP * analyze(top, 8, 8)
    shifted = jnp.concatenate([upper, lower], 1)
    squares = lax.all_gather((shifted * shifted).astype(jnp.bfloat16), "cube")
    norms = jnp.sqrt(jnp.sum(squares.astype(jnp.float32), 0))
    dual_part = (shifted * (RADIUS / jnp.maximum(norms, RADIUS))).astype(jnp.bfloat16)
    own_part = jnp.concatenate([dual_part, total[None, :, HALO:].astype(jnp.bfloat16)], 0)
    parts = lax.all_to_all(jnp.broadcast_to(own_part, (DP,) + own_part.shape), "dp", 0, 0)
    updated, dual_next = finished(parts, own_rows)
    return (updated[None], dual_next[:, None])


def solution(mesh):
    return jax.shard_map(
        on_device,
        mesh=mesh,
        in_specs=(
            P("cube", "facet", None),
            P(None, "cube", "facet", None),
            P("cube", ("facet", "dp"), None, None),
            P("cube", ("facet", "dp"), None),
            P("cube", ("facet", "dp")),
            P("cube", ("facet", "dp")),
            P("cube", ("facet", "dp")),
        ),
        out_specs=(P("cube", "facet", None), P(None, "cube", "facet", None)),
        check_vma=False,
    )
```

```python
import functools
import math

import jax
import jax.numpy as jnp
import numpy as np
from jax import lax
from jax.experimental import pallas as pl
from jax.experimental.pallas import tpu as pltpu
from jax.sharding import PartitionSpec as P

LOWPASS = (
    0.2303778133088964,
    0.7148465705529155,
    0.6308807679298587,
    -0.027983769416859854,
    -0.18703481171909309,
    0.030841381835560764,
    0.0328830116668852,
    -0.010597401785069032,
)
HIGHPASS = (
    -0.010597401785069032,
    -0.0328830116668852,
    0.030841381835560764,
    0.18703481171909309,
    -0.027983769416859854,
    -0.6308807679298587,
    0.7148465705529155,
    -0.2303778133088964,
)
TAU_STEP = 0.5
SIGMA_STEP = 0.5
RADIUS = 3.0

W = 2560
TILE = 16
FR = 48
BLK = 64
PER = FR // TILE
Q = 20
R = 128
DP = 4
PART = W // DP
HALO = 128
SPAN = PART + HALO
CHUNKS = W // 64
UNROLL = 20
VMEM_LIMIT = 60 * 1024 * 1024
NORM = 1.0 / math.sqrt(W)
C1, C2 = math.cos(2 * math.pi / 5), math.cos(4 * math.pi / 5)
S1, S2 = math.sin(2 * math.pi / 5), math.sin(4 * math.pi / 5)


def tables():
    x = np.arange(W).reshape(R, Q).T
    angles = (x[:, :, None] * np.arange(R)[None, None, :] % W) * (2.0 * math.pi / W)
    table = np.concatenate([np.cos(angles), -np.sin(angles)], -1).astype(jnp.bfloat16)
    return table


def constants():
    table = tables()
    return np.concatenate([table.reshape(Q * R, 2 * R), column_filters().reshape(-1, 2 * HALO)])


def flipped_table():
    return tables().transpose(0, 2, 1).reshape(2 * Q * R, R)


def column_filters():
    band = np.zeros((2 * HALO, 2 * HALO), np.float32)
    for b, taps in enumerate((LOWPASS, HIGHPASS)):
        for k in range(8):
            j = np.arange(HALO)
            band[HALO + j - k, HALO * b + j] = taps[k]
    leading = band.astype(jnp.bfloat16)
    rest = (band - leading.astype(np.float32)).astype(jnp.bfloat16)
    return np.stack([leading, rest])


def times_i(value, sign):
    re, im = value
    return (-im, re) if sign > 0 else (im, -re)


def plus(u, v):
    return (u[0] + v[0], u[1] + v[1])


def minus(u, v):
    return (u[0] - v[0], u[1] - v[1])


def dft4(x, sign):
    a, b = plus(x[0], x[2]), minus(x[0], x[2])
    c, d = plus(x[1], x[3]), times_i(minus(x[1], x[3]), sign)
    return [plus(a, c), plus(b, d), minus(a, c), minus(b, d)]


def dft5(x, sign):
    t1, t2 = plus(x[1], x[4]), plus(x[2], x[3])
    t3, t4 = minus(x[1], x[4]), minus(x[2], x[3])
    m1 = tuple(z + C1 * u + C2 * v for z, u, v in zip(x[0], t1, t2))
    m2 = tuple(z + C2 * u + C1 * v for z, u, v in zip(x[0], t1, t2))
    n1 = times_i(tuple(S1 * u + S2 * v for u, v in zip(t3, t4)), sign)
    n2 = times_i(tuple(S2 * u - S1 * v for u, v in zip(t3, t4)), sign)
    return [plus(x[0], plus(t1, t2)), plus(m1, n1), plus(m2, n2), minus(m2, n2), minus(m1, n1)]


def dft20(x, sign):
    columns = [dft4([x[(5 * a + 4 * b) % 20] for a in range(4)], sign) for b in range(5)]
    out = [None] * 20
    for c in range(4):
        line = dft5([columns[b][c] for b in range(5)], sign)
        for e in range(5):
            out[(5 * c + 16 * e) % 20] = line[e]
    return out


def residue_order():
    y = lax.broadcasted_iota(jnp.int32, (PART, 128), 0)
    group = ((y.astype(jnp.float32) + 0.5) * (1.0 / Q)).astype(jnp.int32)
    target = (y - Q * group) * 32 + group
    lane = lax.broadcasted_iota(jnp.int32, (PART, 128), 1)
    tiles = [jnp.where(target == lane + 128 * j, 1.0, 0.0) for j in range(PART // 128)]
    return jnp.concatenate(tiles, 1).astype(jnp.bfloat16)


def natural_order():
    row = lax.broadcasted_iota(jnp.int32, (PART, 128), 0)
    tiles = []
    for j in range(PART // 128):
        y = lax.broadcasted_iota(jnp.int32, (1, 128), 1) + 128 * j
        group = ((y.astype(jnp.float32) + 0.5) * (1.0 / Q)).astype(jnp.int32)
        tiles.append(jnp.where(row == (y - Q * group) * 32 + group, 1.0, 0.0))
    return jnp.concatenate(tiles, 1).astype(jnp.bfloat16)


def add_blocks(base, start, slot, live, weights, payload_ref, spec_ref, grad_ref, list_ref):
    lane = lax.broadcasted_iota(jnp.int32, (1, 128), 1)
    half = lane & 63

    def collect(b, count):
        place = slot(b) - base
        list_ref[count] = b
        return count + jnp.where((place >= 0) & (place < PER), 1, 0)

    count = lax.fori_loop(0, live, collect, 0)
    for u in range(UNROLL):
        list_ref[count + u] = list_ref[0]
    slot_lane = lax.broadcasted_iota(jnp.int32, (1, 128), 1)
    ones = jnp.ones((128, 128), jnp.bfloat16)

    def blocks(step, carry):
        places = [step * UNROLL + u for u in range(UNROLL)]
        numbers = [list_ref[place] for place in places]
        picked = [
            jnp.where(slot_lane == jnp.where(place < count, b, -1), weights, 0.0)
            for place, b in zip(places, numbers)
        ]
        factors = jnp.dot(
            jnp.concatenate(picked, 0).astype(jnp.bfloat16), ones, preferred_element_type=jnp.float32
        )
        found = []
        for u, b in enumerate(numbers):
            chunk, offset = start(b)
            tile = jnp.clip(slot(b) - base, 0, PER - 1)
            rows = pl.ds(pl.multiple_of(tile * TILE, TILE), TILE)
            first = pltpu.roll(spec_ref[chunk, rows, :].astype(jnp.float32), (128 - offset) & 127, 1)
            second = pltpu.roll(spec_ref[chunk + 1, rows, :].astype(jnp.float32), 64 - offset, 1)
            model = jnp.where(half < 64 - offset, first, second)
            misfit = factors[TILE * u : TILE * (u + 1)] * (
                model - payload_ref[b].astype(jnp.float32)
            )
            lower = jnp.where(half >= offset, pltpu.roll(misfit, offset, 1), 0.0)
            upper = jnp.where(half < offset, pltpu.roll(misfit, 64 + offset, 1), 0.0)
            found.append((chunk, rows, lower, upper))
        for chunk, rows, lower, upper in found:
            grad_ref[chunk, rows, :] += lower
            grad_ref[chunk + 1, rows, :] += upper
        return carry

    lax.fori_loop(0, (count + UNROLL - 1) // UNROLL, blocks, 0)


def columns_back(part, rows, dual_ref, filters, rows_ref):
    tiles = SPAN // HALO + 1
    blocks = []
    for j in range(tiles):
        place = (PART // HALO) * part - 1 + j
        inside = (place >= 0) & (place < W // HALO)
        columns = pl.ds(pl.multiple_of(jnp.clip(place, 0, W // HALO - 1) * HALO, HALO), HALO)
        for a in range(2):
            pair = jnp.concatenate([dual_ref[2 * a + b, :rows, columns] for b in range(2)], 1)
            blocks.append(jnp.where(inside, pair, jnp.zeros_like(pair)))
    stacked = jnp.concatenate(blocks, 0)
    across = sum(
        lax.dot_general(
            stacked, filters(i), (((1,), (1,)), ((), ())), preferred_element_type=jnp.float32
        )
        for i in range(2)
    )
    for j in range(tiles - 1):
        for a in range(2):
            here, right = [across[rows * (2 * i + a) : rows * (2 * i + a + 1)] for i in (j, j + 1)]
            rows_ref[a, 8 : 8 + rows, HALO * j : HALO * (j + 1)] = (
                here[:, HALO:] + right[:, :HALO]
            )


def rows_back(first, count, tile, rows_ref):
    value = 0.0
    for a, taps in enumerate((LOWPASS, HIGHPASS)):
        for k in range(8):
            value = value + taps[k] * rows_ref[a, 8 + first + k : 8 + first + k + count, tile]
    return value


def fill_message(part, starts, slots, live, weights, dual_ref, filters_ref, rows_ref, out_ref):
    rows_ref[:, :8, :] = jnp.zeros((2, 8, SPAN), jnp.float32)
    columns_back(
        part,
        TILE,
        dual_ref,
        lambda i: filters_ref[2 * HALO * i : 2 * HALO * (i + 1)],
        rows_ref,
    )
    for i in range(SPAN // HALO // 2):
        pair = [rows_back(-8, 8, pl.ds(HALO * (2 * i + j), HALO), rows_ref) for j in range(2)]
        out_ref[1 + i] = jnp.concatenate(pair, 0).astype(jnp.bfloat16)
    row = lax.broadcasted_iota(jnp.int32, (TILE, BLK), 0)
    numbers = jnp.where(row == 0, starts >> 6, starts & 63)
    numbers = jnp.where(row == 2, slots, numbers)
    numbers = jnp.where(row == 3, live, numbers)
    out_ref[0] = jnp.concatenate([weights, numbers.astype(jnp.float32)], 1).astype(jnp.bfloat16)


def synthesis(part_ref, message_ref, dual_ref, constants_ref, synth_ref, rows_ref):
    columns_back(
        part_ref[0],
        FR,
        dual_ref,
        lambda i: constants_ref[Q * R + 2 * HALO * i : Q * R + 2 * HALO * (i + 1)],
        rows_ref,
    )
    rows_ref[:, 8 + FR :, :] = jnp.zeros((2, 8, SPAN), jnp.float32)
    for j in range(SPAN // HALO):
        tile = pl.ds(HALO * j, HALO)
        synth_ref[:, tile] = rows_back(0, FR, tile, rows_ref)
        below = message_ref[1 + j // 2].astype(jnp.float32)
        synth_ref[FR - 8 :, tile] += below[8 * (j % 2) : 8 * (j % 2) + 8]


def own_pass(
    part_ref,
    starts_hbm,
    slots_hbm,
    live_hbm,
    weight_hbm,
    payload_hbm,
    table_hbm,
    pixels_hbm,
    dual_hbm,
    spec_ref,
    own_ref,
    message_ref,
    starts_ref,
    slots_ref,
    live_ref,
    list_ref,
    starts_vec,
    slots_vec,
    dual_ref,
    filters_ref,
    rows_ref,
    weight_ref,
    payload_ref,
    table_ref,
    pixels_ref,
    order_ref,
    re_ref,
    im_ref,
    grad_ref,
    sems,
):
    pairs = [
        (pixels_hbm, pixels_ref),
        (table_hbm.at[pl.ds(0, Q * R), :], table_ref),
        (weight_hbm, weight_ref),
        (payload_hbm, payload_ref),
        (starts_hbm, starts_ref),
        (slots_hbm, slots_ref),
        (live_hbm, live_ref),
        (starts_hbm, starts_vec),
        (slots_hbm, slots_vec),
        (dual_hbm.at[:, :TILE, :], dual_ref),
        (table_hbm.at[pl.ds(Q * R, 4 * HALO), :], filters_ref),
    ]
    copies = [pltpu.make_async_copy(s, d, sems.at[i]) for i, (s, d) in enumerate(pairs)]
    for copy in copies:
        copy.start()
    lane = lax.broadcasted_iota(jnp.int32, (1, 128), 1)
    low = lane < 64
    quarter = lane >> 5

    order_ref[...] = residue_order()
    copies[0].wait()
    stacked = jnp.concatenate(
        [pixels_ref[:, PART * g : PART * (g + 1)].astype(jnp.bfloat16) for g in range(4)], 0
    )
    sorted_rows = jnp.dot(stacked, order_ref[...], preferred_element_type=jnp.float32)
    copies[1].wait()
    for j in range(5):
        tiles = [sorted_rows[FR * g : FR * (g + 1), 128 * j : 128 * (j + 1)] for g in range(4)]
        for p in range(4):
            turned = [
                tiles[g] if g == p else pltpu.roll(tiles[g], (32 * (g - p)) % 128, 1)
                for g in range(4)
            ]
            rows = turned[3]
            for g in range(3):
                rows = jnp.where(quarter == g, turned[g], rows)
            q = 4 * j + p
            partial = jnp.dot(
                rows.astype(jnp.bfloat16),
                table_ref[R * q : R * (q + 1)],
                preferred_element_type=jnp.float32,
            )
            re_ref[q] = partial[:, :R]
            im_ref[q] = partial[:, R:]

    def forward(i, carry):
        for j in range(2):
            rows = pl.ds(pl.multiple_of(i * TILE + 8 * j, 8), 8)
            spectrum = dft20([(re_ref[q, rows, :], im_ref[q, rows, :]) for q in range(Q)], -1)
            for k, (re, im) in enumerate(spectrum):
                re, im = re * NORM, im * NORM
                grad_ref[2 * k, rows, :] = jnp.where(low, re, pltpu.roll(im, 64, 1))
                grad_ref[2 * k + 1, rows, :] = jnp.where(low, pltpu.roll(re, 64, 1), im)
        return carry

    lax.fori_loop(0, FR // TILE, forward, 0)
    spec_ref[:CHUNKS] = grad_ref[:CHUNKS].astype(jnp.bfloat16)
    spec_ref[CHUNKS] = spec_ref[0]
    grad_ref[...] = jnp.zeros_like(grad_ref)
    for copy in copies[2:]:
        copy.wait()
    blank = jnp.zeros((TILE, 128 - BLK), jnp.float32)
    weights = weight_ref[...].astype(jnp.float32)
    fill_message(
        part_ref[0],
        starts_vec[...],
        slots_vec[...],
        live_ref[0, 0],
        weights,
        dual_ref,
        filters_ref,
        rows_ref,
        message_ref,
    )
    weights = jnp.concatenate([weights, blank], 1)
    add_blocks(
        PER,
        lambda b: (starts_ref[0, b] >> 6, starts_ref[0, b] & 63),
        lambda b: slots_ref[0, b],
        live_ref[0, 0],
        weights,
        payload_ref,
        spec_ref,
        grad_ref,
        list_ref,
    )
    own_ref[...] = grad_ref[...].astype(jnp.bfloat16)


def below_pass(
    message_hbm,
    payload_hbm,
    spec_hbm,
    own_hbm,
    table_hbm,
    out_ref,
    list_ref,
    numbers_ref,
    vector_ref,
    message_ref,
    payload_ref,
    spec_ref,
    own_ref,
    grad_ref,
    table_ref,
    order_ref,
    re_ref,
    im_ref,
    tile_ref,
    sems,
):
    pairs = [
        (message_hbm.at[0], message_ref),
        (spec_hbm, spec_ref),
        (own_hbm, own_ref),
        (payload_hbm, payload_ref),
        (table_hbm, table_ref),
    ]
    copies = [pltpu.make_async_copy(s, d, sems.at[i]) for i, (s, d) in enumerate(pairs)]
    for copy in copies:
        copy.start()
    lane = lax.broadcasted_iota(jnp.int32, (1, 128), 1)
    low = lane < 64
    quarter = lane >> 5
    copies[0].wait()
    meta = message_ref[...].astype(jnp.float32)
    vector_ref[...] = meta[:8].astype(jnp.int32)
    read = pltpu.make_async_copy(vector_ref, numbers_ref, sems.at[5])
    read.start()
    order_ref[...] = natural_order()
    read.wait()
    for copy in copies[1:4]:
        copy.wait()
    grad_ref[...] = own_ref[...].astype(jnp.float32)
    add_blocks(
        0,
        lambda b: (numbers_ref[0, BLK + b], numbers_ref[1, BLK + b]),
        lambda b: numbers_ref[2, BLK + b],
        numbers_ref[3, BLK],
        jnp.where(low, meta, 0.0),
        payload_ref,
        spec_ref,
        grad_ref,
        list_ref,
    )
    grad_ref[0] += grad_ref[CHUNKS]

    def backward(i, carry):
        rows = pl.ds(pl.multiple_of(i * 8, 8), 8)
        spectrum = []
        for k in range(Q):
            even, odd = grad_ref[2 * k, rows, :], grad_ref[2 * k + 1, rows, :]
            spectrum.append(
                (
                    jnp.where(low, even, pltpu.roll(odd, 64, 1)),
                    jnp.where(low, pltpu.roll(even, 64, 1), odd),
                )
            )
        for q, (re, im) in enumerate(dft20(spectrum, 1)):
            re_ref[q, rows, :] = re * NORM
            im_ref[q, rows, :] = im * NORM
        return carry

    lax.fori_loop(0, FR // 8, backward, 0)
    copies[4].wait()
    for j in range(5):
        places = [[] for _ in range(4)]
        for p in range(4):
            q = 4 * j + p
            pair = jnp.concatenate([re_ref[q], im_ref[q]], 1).astype(jnp.bfloat16)
            rows = jnp.dot(
                pair, table_ref[2 * R * q : 2 * R * (q + 1)], preferred_element_type=jnp.float32
            )
            for g in range(4):
                places[g].append(rows if g == p else pltpu.roll(rows, (32 * (p - g)) % 128, 1))
        for g in range(4):
            tile = places[g][3]
            for p in range(3):
                tile = jnp.where(quarter == p, places[g][p], tile)
            tile_ref[5 * g + j] = tile
    mixed = jnp.concatenate(
        [jnp.concatenate([tile_ref[5 * g + j] for j in range(5)], 1) for g in range(4)], 0
    ).astype(jnp.bfloat16)
    natural = jnp.dot(
        mixed, order_ref[...], preferred_element_type=jnp.float32
    ).astype(jnp.bfloat16)
    out_ref[0, :, :HALO] = jnp.zeros((FR, HALO), jnp.bfloat16)
    for g in range(4):
        rows = natural[FR * g : FR * (g + 1)]
        out_ref[g, :, HALO:] = rows
        if g < 3:
            out_ref[g + 1, :, :HALO] = rows[:, PART - HALO :]


HBM_SPEC = pl.BlockSpec(memory_space=pltpu.HBM)
SMEM_SPEC = pl.BlockSpec(memory_space=pltpu.SMEM)
VMEM_SPEC = pl.BlockSpec(memory_space=pltpu.VMEM)
SPECTRA = jax.ShapeDtypeStruct((CHUNKS + 1, FR, 128), jnp.bfloat16)


TABLE = pltpu.VMEM((Q * R, 2 * R), jnp.bfloat16)
PARAMS = pltpu.CompilerParams(vmem_limit_bytes=VMEM_LIMIT)
COST = pl.CostEstimate(flops=2 * 10**9, bytes_accessed=4 * 10**6, transcendentals=0)


def synthesized(part, received, dual, table):
    return pl.pallas_call(
        synthesis,
        out_shape=jax.ShapeDtypeStruct((FR, SPAN), jnp.float32),
        in_specs=[SMEM_SPEC] + [VMEM_SPEC] * 3,
        out_specs=VMEM_SPEC,
        scratch_shapes=[pltpu.VMEM((2, FR + 16, SPAN), jnp.float32)],
        compiler_params=pltpu.CompilerParams(vmem_limit_bytes=16 * 1024 * 1024),
        name="synthesized",
    )(part, received, dual, table)


def own_spectra(part, starts, slots, live, weights, payload, table, pixels, dual):
    return pl.pallas_call(
        own_pass,
        out_shape=(
            SPECTRA,
            SPECTRA,
            jax.ShapeDtypeStruct((1 + SPAN // HALO // 2, TILE, 128), jnp.bfloat16),
        ),
        in_specs=[SMEM_SPEC] + [HBM_SPEC] * 8,
        out_specs=(VMEM_SPEC,) * 3,
        scratch_shapes=[
            pltpu.SMEM((1, BLK), jnp.int32),
            pltpu.SMEM((1, BLK), jnp.int32),
            pltpu.SMEM((1, 1), jnp.int32),
            pltpu.SMEM((BLK + UNROLL,), jnp.int32),
            pltpu.VMEM((1, BLK), jnp.int32),
            pltpu.VMEM((1, BLK), jnp.int32),
            pltpu.VMEM((4, TILE, W), jnp.bfloat16),
            pltpu.VMEM((4 * HALO, 2 * HALO), jnp.bfloat16),
            pltpu.VMEM((2, 8 + TILE, SPAN), jnp.float32),
            pltpu.VMEM((TILE, BLK), jnp.bfloat16),
            pltpu.VMEM((BLK, TILE, 128), jnp.bfloat16),
            TABLE,
            pltpu.VMEM((FR, W), jnp.float32),
            pltpu.VMEM((PART, PART), jnp.bfloat16),
            pltpu.VMEM((Q, FR, R), jnp.float32),
            pltpu.VMEM((Q, FR, R), jnp.float32),
            pltpu.VMEM((CHUNKS + 1, FR, 128), jnp.float32),
            pltpu.SemaphoreType.DMA((11,)),
        ],
        compiler_params=PARAMS,
        cost_estimate=COST,
        name="own_spectra",
    )(part, starts, slots, live, weights, payload, table, pixels, dual)


def gradient_parts(received, payload, spectra, own, table):
    return pl.pallas_call(
        below_pass,
        out_shape=jax.ShapeDtypeStruct((DP, FR, SPAN), jnp.bfloat16),
        in_specs=[HBM_SPEC] * 5,
        out_specs=VMEM_SPEC,
        scratch_shapes=[
            pltpu.SMEM((BLK + UNROLL,), jnp.int32),
            pltpu.SMEM((8, 128), jnp.int32),
            pltpu.VMEM((8, 128), jnp.int32),
            pltpu.VMEM((TILE, 128), jnp.bfloat16),
            pltpu.VMEM((BLK, TILE, 128), jnp.bfloat16),
            pltpu.VMEM((CHUNKS + 1, FR, 128), jnp.bfloat16),
            pltpu.VMEM((CHUNKS + 1, FR, 128), jnp.bfloat16),
            pltpu.VMEM((CHUNKS + 1, FR, 128), jnp.float32),
            pltpu.VMEM((2 * Q * R, R), jnp.bfloat16),
            pltpu.VMEM((PART, PART), jnp.bfloat16),
            pltpu.VMEM((Q, FR, R), jnp.float32),
            pltpu.VMEM((Q, FR, R), jnp.float32),
            pltpu.VMEM((Q, FR, R), jnp.float32),
            pltpu.SemaphoreType.DMA((6,)),
        ],
        compiler_params=PARAMS,
        cost_estimate=COST,
        name="gradient_parts",
    )(received, payload, spectra, own, table)


def finish(parts_ref, pixels_ref, image_hbm, dual_hbm, image_ref, sems):
    copies = []
    for d in range(DP):
        tile = pl.ds(PART * d, PART)
        copies.append(
            pltpu.make_async_copy(
                parts_ref.at[d, pl.ds(0, 4)], dual_hbm.at[:, :, tile], sems.at[d]
            )
        )
        copies[-1].start()
    for d in range(DP):
        tile = pl.ds(PART * d, PART)
        descent = parts_ref[d, 4].astype(jnp.float32)
        image_ref[:, tile] = jnp.maximum(pixels_ref[:, tile] - TAU_STEP * descent, 0.0)
        copies.append(
            pltpu.make_async_copy(image_ref.at[:, tile], image_hbm.at[:, tile], sems.at[DP + d])
        )
        copies[-1].start()
    for copy in copies:
        copy.wait()


def finished(parts, pixels):
    return pl.pallas_call(
        finish,
        out_shape=(
            jax.ShapeDtypeStruct((FR, W), jnp.float32),
            jax.ShapeDtypeStruct((4, FR, W), jnp.bfloat16),
        ),
        in_specs=[VMEM_SPEC] * 2,
        out_specs=(HBM_SPEC,) * 2,
        scratch_shapes=[pltpu.VMEM((FR, W), jnp.float32), pltpu.SemaphoreType.DMA((2 * DP,))],
        compiler_params=pltpu.CompilerParams(vmem_limit_bytes=16 * 1024 * 1024),
        name="finished",
    )(parts, pixels)


def hop(block, distance):
    devices = range(lax.axis_size("facet"))
    route = [(i - distance, i) for i in devices if i - distance in devices]
    return lax.ppermute(block, "facet", route)


def gathered_sum(parts):
    mixed = lax.all_to_all(parts, "dp", 0, 0)
    return jnp.sum(mixed.astype(jnp.float32), 0)


def analyze(extra, first, count):
    subbands = []
    for row_taps in (LOWPASS, HIGHPASS):
        filtered = sum(row_taps[k] * extra[first - k : first - k + count] for k in range(8))
        for col_taps in (LOWPASS, HIGHPASS):
            subbands.append(
                sum(col_taps[k] * filtered[:, HALO - k : HALO - k + PART] for k in range(8))
            )
    return jnp.stack(subbands)


def on_device(image, dual, payload, vis_weight, freq_start, tile_slot, live):
    table, flipped = jnp.asarray(constants()), jnp.asarray(flipped_table())
    position = lax.axis_index("dp")
    own_rows = image[0]
    part = position[None]
    weights = vis_weight[0].T
    payload_below = hop(payload[0], -1)
    left = position * PART
    own_dual = lax.dynamic_slice_in_dim(dual[:, 0], left, PART, 2).astype(jnp.float32)
    old = lax.dynamic_slice_in_dim(
        jnp.pad(own_rows, ((0, 0), (HALO, 0))), left, SPAN, 1
    )

    spectra, own, sent = own_spectra(
        part, freq_start, tile_slot, live, weights, payload[0], table, own_rows, dual[:, 0]
    )
    received = hop(sent, -1)
    terms = gradient_parts(received, payload_below, spectra, own, flipped)
    terms, received = lax.optimization_barrier((terms, received))
    synth = synthesized(part, received, dual[:, 0], table)
    total = gathered_sum(terms) + synth
    new = jnp.maximum(old - TAU_STEP * total, 0.0)
    column = lax.broadcasted_iota(jnp.int32, old.shape, 1) + left
    extra = jnp.where(column >= HALO, 2.0 * new - old, 0.0)
    extra_above = hop(extra[FR - 8 :].astype(jnp.bfloat16), 1).astype(jnp.float32)
    lower = own_dual[:, 8:] + SIGMA_STEP * analyze(extra, 8, FR - 8)
    lower, extra_above = lax.optimization_barrier((lower, extra_above))
    top = jnp.concatenate([extra_above, extra[:8]], 0)
    upper = own_dual[:, :8] + SIGMA_STEP * analyze(top, 8, 8)
    shifted = jnp.concatenate([upper, lower], 1)
    squares = lax.all_gather((shifted * shifted).astype(jnp.bfloat16), "cube")
    norms = jnp.sqrt(jnp.sum(squares.astype(jnp.float32), 0))
    dual_part = (shifted * (RADIUS / jnp.maximum(norms, RADIUS))).astype(jnp.bfloat16)
    own_part = jnp.concatenate([dual_part, total[None, :, HALO:].astype(jnp.bfloat16)], 0)
    parts = lax.all_to_all(jnp.broadcast_to(own_part, (DP,) + own_part.shape), "dp", 0, 0)
    updated, dual_next = finished(parts, own_rows)
    return (updated[None], dual_next[:, None])


def solution(mesh):
    return jax.shard_map(
        on_device,
        mesh=mesh,
        in_specs=(
            P("cube", "facet", None),
            P(None, "cube", "facet", None),
            P("cube", ("facet", "dp"), None, None),
            P("cube", ("facet", "dp"), None),
            P("cube", ("facet", "dp")),
            P("cube", ("facet", "dp")),
            P("cube", ("facet", "dp")),
        ),
        out_specs=(P("cube", "facet", None), P(None, "cube", "facet", None)),
        check_vma=False,
    )
```
